32 devices in a mesh: rep: 4 (over x, core), dp: 8 (over z, y).
Axes of the slice: x: 2, y: 2, z: 4, core: 2. Of those that a mesh axis runs over, the one named last changes fastest.
Arguments:
- images: bfloat16 [1024, 7, 7, 2048], P(('rep', 'dp'))
- labels: int32 [1024], P(('rep', 'dp')), may hold values from 0 to 999
- conv_weight: float32 [13, 512, 512], P(None, 'dp'), may hold values from -0.1875 to 0.1875
- conv_mask: int32 [13, 512, 512], P(None, 'dp'), may hold values 0 or 1
- conv_rank: int32 [13, 512, 512], P(None, 'dp'), may hold values from 0 to 262143, as said below
- head_weight: float32 [512, 1000], P('dp'), may hold values from -0.25 to 0.25
- norm_params: float32 [4, 512], replicated, may hold values from 0.5 to 1.5
- head_bias: float32 [1000], replicated, may hold values from -3 to 3
- conv_first: float32 [4, 13, 512, 512], P('rep', None, 'dp'), may hold values from -0.000125 to 0.000125
- conv_second: float32 [4, 13, 512, 512], P('rep', None, 'dp'), may hold values from 1.7578125e-11 to 2.8125e-10
- head_first: float32 [4, 512, 1000], P('rep', 'dp'), may hold values from -0.0004125 to 0.0004125
- head_second: float32 [4, 512, 1000], P('rep', 'dp'), may hold values from 1.953125e-10 to 3.125e-09
- norm_first: float32 [4, 4, 512], P('rep'), may hold values from -0.00020625 to 0.00020625
- norm_second: float32 [4, 4, 512], P('rep'), may hold values from 4.8828126e-11 to 7.8125e-10
- bias_first: float32 [4, 1000], P('rep'), may hold values from -0.00125 to 0.00125
- bias_second: float32 [4, 1000], P('rep'), may hold values from 1.7578125e-09 to 2.8125e-08
- conv_outer: float32 [13, 512, 512], P(None, 'dp'), may hold values from -0.12 to 0.12
- head_outer: float32 [512, 1000], P('dp'), may hold values from -0.12 to 0.12
- norm_outer: float32 [4, 512], replicated, may hold values from -0.12 to 0.12
- bias_outer: float32 [1000], replicated, may hold values from -0.12 to 0.12
Outputs:
- conv_weight_new: float32 [13, 512, 512], P(None, 'dp')
- conv_mask_new: int32 [13, 512, 512], P(None, 'dp')
- conv_first_new: float32 [4, 13, 512, 512], P('rep', None, 'dp')
- conv_second_new: float32 [4, 13, 512, 512], P('rep', None, 'dp')
- conv_outer_new: float32 [13, 512, 512], P(None, 'dp')
- head_weight_new: float32 [512, 1000], P('dp')
- head_first_new: float32 [4, 512, 1000], P('rep', 'dp')
- head_second_new: float32 [4, 512, 1000], P('rep', 'dp')
- head_outer_new: float32 [512, 1000], P('dp')
- norm_new: float32 [4, 512], replicated
- norm_first_new: float32 [4, 4, 512], P('rep')
- norm_second_new: float32 [4, 4, 512], P('rep')
- norm_outer_new: float32 [4, 512], replicated
- bias_new: float32 [1000], replicated
- bias_first_new: float32 [4, 1000], P('rep')
- bias_second_new: float32 [4, 1000], P('rep')
- bias_outer_new: float32 [1000], replicated
- loss_sums: float32 [4], P('rep')
The draws below stay inside these ranges and needn't reach their ends.
Inputs may be any that keep to these rules, and one draw needn't show every extreme that they name: `conv_rank`: each block of 512 x 512 entries holds each number of 0 to 262143 once.
All inputs are finite; a program needn't handle non-finite values. No bound on the sum of `conv_mask` on one device may be relied on, other than what follows from the above.
Results may differ from the reference program's by a relative error of at most 0.01065.
The reference program's roundings to bfloat16 on the way count: a program that leaves them out, or rounds other values in their place, can miss the bound.
Values may be sent and summed in bfloat16 or wider, within the bound.
No kernel may reach another device: no remote copies, remote signals or barrier semaphores. Data moves between devices by JAX's collectives and lax.ppermute only.
A program may use at most 256 MiB of HBM per device.

```python
import math
import jax
import jax.numpy as jnp
from jax import lax

C_IN = 2048
C_MID = 512
CLASSES = 1000
SIDE = 7
STEP = 10
PIX = 49
GROUP_IMG = 256
IMAGES = 1024
REPS = 4
BLOCKS = 13
BLOCK = 262144
DROP_CUT = 78643
GROW_CUT = 242484


def draw_images(key, part):
    key = jax.random.fold_in(key, 5)
    base_key, image_key, channel_key = jax.random.split(key, 3)
    shape = (IMAGES, SIDE, SIDE, C_IN)
    position = (jnp.arange(IMAGES) % GROUP_IMG).astype(jnp.float32) / max(GROUP_IMG - 1, 1)
    rise = 3.0
    base = jax.random.normal(base_key, shape, jnp.float32)
    image_scale = rise ** position * jnp.exp(jax.random.uniform(image_key, (IMAGES,), jnp.float32, -0.35, 0.35))
    channel_scale = jnp.exp(jax.random.uniform(channel_key, (C_IN,), jnp.float32, -1.2, 1.2))
    return (base * image_scale[:, None, None, None] * channel_scale).astype(jnp.bfloat16)


def draw_conv_rank(key, part):
    key = jax.random.fold_in(key, 7)
    block_keys = jax.random.split(key, BLOCKS)
    orders = jax.vmap(lambda k: jax.random.permutation(k, BLOCK))(block_keys)
    return orders.reshape(BLOCKS, C_MID, C_MID).astype(jnp.int32)


def plant(entries, rng, low, top_value):
    place = [jax.random.randint(jax.random.fold_in(rng, axis), (), 0, length) for axis, length in enumerate(entries.shape)]
    main_axis = entries.shape.index(max(entries.shape))
    neighbour = place[:main_axis] + [(place[main_axis] + 1) % entries.shape[main_axis]] + place[main_axis + 1:]
    return entries.at[tuple(place)].set(low).at[tuple(neighbour)].set(top_value)


def shard_levels(key, extent, cuts, smallest, largest):
    def one(dim, blocks):
        heights = jax.random.uniform(jax.random.fold_in(jax.random.fold_in(key, 6), dim), (blocks,), jnp.float32, smallest / len(cuts), largest / len(cuts))
        return jnp.repeat(jnp.exp(heights), extent[dim] // blocks).reshape((-1,) + (1,) * (len(extent) - dim - 1))

    factor_of = one(*cuts[0])
    for cut in cuts[1:]:
        factor_of = factor_of * one(*cut)
    return factor_of


def normal_values(own_key, dims, deviation, reach, cuts=(), kind=jnp.bfloat16):
    entries = jax.random.normal(own_key, dims, jnp.float32) * deviation
    if len(cuts) > 0:
        entries = shard_levels(own_key, dims, cuts, -0.22, 0.18) * entries
    return jnp.clip(entries, min=-reach, max=reach).astype(kind)


def setup_inputs(seed: int = 0) -> dict:
    keys = jax.random.split(jax.random.key(seed), 21)
    return {
        "images": draw_images(jax.random.fold_in(keys[20], 71), 0),
        "labels": plant(jax.random.randint(keys[1], (IMAGES,), 0, CLASSES), jax.random.fold_in(keys[1], 1), 0, CLASSES - 1).astype(jnp.int32),
        "conv_weight": normal_values(keys[2], (BLOCKS, C_MID, C_MID), (9 * C_MID // 5) ** -0.5, 0.1875, ((1, 8),), jnp.float32),
        "conv_mask": plant((jax.random.randint(keys[3], (BLOCKS, C_MID, C_MID), 0, 5) < 1).astype(jnp.int32), jax.random.fold_in(keys[3], 1), 0, 1),
        "conv_rank": draw_conv_rank(jax.random.fold_in(keys[20], 71), 0),
        "head_weight": normal_values(keys[5], (C_MID, CLASSES), C_MID ** -0.5, 0.25, ((0, 8),), jnp.float32),
        "norm_params": jnp.clip(jax.random.uniform(keys[6], (4, C_MID), jnp.float32, 0.5, 1.5), 0.5, 1.5),
        "head_bias": normal_values(keys[7], (CLASSES,), 0.5, 3.0, (), jnp.float32),
        "conv_first": normal_values(keys[8], (REPS, BLOCKS, C_MID, C_MID), (0.00033 / GROUP_IMG ** 0.5), 0.000125, ((0, 4), (2, 8)), jnp.float32),
        "conv_second": jnp.clip(jnp.exp(math.log(2.8124999551515373e-10) - 2.7725887 * jax.random.uniform(keys[9], (REPS, BLOCKS, C_MID, C_MID), jnp.float32) ** shard_levels(keys[9], (REPS, BLOCKS, C_MID, C_MID), ((0, 4), (2, 8)), -0.2, 0.2)), 1.7578124719697108e-11, 2.8124999551515373e-10),
        "head_first": normal_values(keys[10], (REPS, C_MID, CLASSES), (0.0011 / GROUP_IMG ** 0.5), 0.0004125, ((0, 4), (1, 8)), jnp.float32),
        "head_second": jnp.clip(jnp.exp(math.log(3.1250000365190544e-09) - 2.7725887 * jax.random.uniform(keys[11], (REPS, C_MID, CLASSES), jnp.float32) ** shard_levels(keys[11], (REPS, C_MID, CLASSES), ((0, 4), (1, 8)), -0.2, 0.2)), 1.953125022824409e-10, 3.1250000365190544e-09),
        "norm_first": normal_values(keys[12], (REPS, 4, C_MID), (0.00055 / GROUP_IMG ** 0.5), 0.00020625, ((0, 4),), jnp.float32),
        "norm_second": jnp.clip(jnp.exp(math.log(7.812500091297636e-10) - 2.7725887 * jax.random.uniform(keys[13], (REPS, 4, C_MID), jnp.float32) ** shard_levels(keys[13], (REPS, 4, C_MID), ((0, 4),), -0.2, 0.2)), 4.8828125570610226e-11, 7.812500091297636e-10),
        "bias_first": normal_values(keys[14], (REPS, CLASSES), (0.0033 / GROUP_IMG ** 0.5), 0.00125, ((0, 4),), jnp.float32),
        "bias_second": jnp.clip(jnp.exp(math.log(2.8124999218448465e-08) - 2.7725887 * jax.random.uniform(keys[15], (REPS, CLASSES), jnp.float32) ** shard_levels(keys[15], (REPS, CLASSES), ((0, 4),), -0.2, 0.2)), 1.757812451153029e-09, 2.8124999218448465e-08),
        "conv_outer": normal_values(keys[16], (BLOCKS, C_MID, C_MID), 0.02, 0.12, ((1, 8),), jnp.float32),
        "head_outer": normal_values(keys[17], (C_MID, CLASSES), 0.02, 0.12, ((0, 8),), jnp.float32),
        "norm_outer": normal_values(keys[18], (4, C_MID), 0.02, 0.12, (), jnp.float32),
        "bias_outer": normal_values(keys[19], (CLASSES,), 0.02, 0.12, (), jnp.float32),
    }


@jax.custom_vjp
def low(v):
    return lax.optimization_barrier(v.astype(jnp.bfloat16)).astype(jnp.float32)

@jax.custom_vjp
def low_back(v):
    return v

def low_keep(v):
    return (low(v), None)

def low_pass(kept, grad):
    return (grad,)

def back_keep(v):
    return (v, None)

def back_low(kept, grad):
    return (low(grad),)
low.defvjp(low_keep, low_pass)
low_back.defvjp(back_keep, back_low)

def matmul(left, right):
    return jnp.dot(left, right, precision=lax.Precision.HIGHEST, preferred_element_type=jnp.float32)

def unfold(maps):
    padded = jnp.pad(maps, ((0, 0), (1, 1), (1, 1), (0, 0)))
    pieces = [padded[:, a:a + SIDE, b:b + SIDE, :] for a in range(3) for b in range(3)]
    return jnp.concatenate(pieces, axis=-1).reshape(maps.shape[0] * PIX, 9 * maps.shape[3])

def norm_act(pre, gain, shift):
    mean = lax.optimization_barrier(jnp.mean(pre, axis=0))
    var = lax.optimization_barrier(jnp.mean(pre * pre, axis=0)) - mean * mean
    normed = (pre - mean) * lax.rsqrt(var + 1e-05)
    return jax.nn.silu(gain * normed + shift)

def forward(effective, head_w, norm_p, head_b, pictures, classes):
    count = pictures.shape[0]
    blocks = C_IN // C_MID
    weights = low(effective)
    first_conv = weights[:blocks].reshape(C_IN, C_MID)
    taps = weights[blocks:].reshape(9 * C_MID, C_MID)
    inputs = pictures.reshape(count * PIX, C_IN)
    y_one = low_back(matmul(inputs, first_conv))
    h_one = low(norm_act(y_one, norm_p[0], norm_p[1]))
    y_two = low_back(matmul(unfold(h_one.reshape(count, SIDE, SIDE, C_MID)), taps))
    h_two = norm_act(y_two, norm_p[2], norm_p[3])
    pooled = low(lax.optimization_barrier(jnp.mean(h_two.reshape(count, PIX, C_MID), axis=1)))
    logits = low_back(matmul(pooled, low(head_w)) + head_b)
    picked = lax.optimization_barrier(jnp.sum(logits * jax.nn.one_hot(classes, CLASSES, dtype=jnp.float32), axis=1))
    cross = jax.nn.logsumexp(logits, axis=1) - picked
    loss = jnp.sum(cross) / count + 0.5 * 5e-05 * jnp.sum(effective * effective)
    return (loss, jnp.sum(cross))

def adamw(weight, grad, first, second, rate):
    first = 0.9 * first + 0.1 * grad
    second = 0.999 * second + 0.001 * grad * grad
    normal_step = first / (1.0 - 0.9 ** STEP) / (jnp.sqrt(second / (1.0 - 0.999 ** STEP)) + 1e-08)
    return (weight - rate * (normal_step + 0.01 * weight), first, second)

def outer_step(start, group_sum, momentum):
    delta = start - group_sum / REPS
    momentum = 0.9 * momentum + delta
    return (start - 0.7 * (delta + 0.9 * momentum), momentum)

def reference(images, labels, conv_weight, conv_mask, conv_rank, head_weight, norm_params, head_bias, conv_first, conv_second, head_first, head_second, norm_first, norm_second, bias_first, bias_second, conv_outer, head_outer, norm_outer, bias_outer):
    mask_old = conv_mask.astype(jnp.float32)
    dropped = (conv_mask == 1) & (conv_rank < DROP_CUT)
    grown = (conv_mask == 0) & (conv_rank >= GROW_CUT)
    mask_int = jnp.where(dropped, 0, jnp.where(grown, 1, conv_mask)).astype(jnp.int32)
    mask_new = mask_int.astype(jnp.float32)
    kept = mask_old * mask_new
    effective = conv_weight * mask_old
    start = conv_weight * kept
    pictures_all = images.astype(jnp.float32)
    results = []
    for group in range(REPS):
        pictures = pictures_all[group * GROUP_IMG:(group + 1) * GROUP_IMG]
        classes = labels[group * GROUP_IMG:(group + 1) * GROUP_IMG]
        loss, backward, cross_sum = jax.vjp(lambda a, b, c, d: forward(a, b, c, d, pictures, classes), effective, head_weight, norm_params, head_bias, has_aux=True)
        dense, head_grad, norm_grad, bias_grad = backward(jnp.float32(1.0))
        conv_g, conv_m, conv_v = adamw(start, mask_new * dense, conv_first[group] * kept, conv_second[group] * kept, 0.03)
        head_g, head_m, head_v = adamw(head_weight, head_grad, head_first[group], head_second[group], 0.03)
        norm_g, norm_m, norm_v = adamw(norm_params, norm_grad, norm_first[group], norm_second[group], 0.3)
        bias_g, bias_m, bias_v = adamw(head_bias, bias_grad, bias_first[group], bias_second[group], 0.3)
        results.append((conv_g * mask_new, conv_m * mask_new, conv_v * mask_new, head_g, head_m, head_v, norm_g, norm_m, norm_v, bias_g, bias_m, bias_v, cross_sum))
    stacked = [jnp.stack([item[k] for item in results]) for k in range(13)]
    conv_new, conv_mom = outer_step(start, lax.optimization_barrier(jnp.sum(stacked[0], axis=0)), conv_outer)
    head_new, head_mom = outer_step(head_weight, lax.optimization_barrier(jnp.sum(stacked[3], axis=0)), head_outer)
    norm_new, norm_mom = outer_step(norm_params, lax.optimization_barrier(jnp.sum(stacked[6], axis=0)), norm_outer)
    bias_new, bias_mom = outer_step(head_bias, lax.optimization_barrier(jnp.sum(stacked[9], axis=0)), bias_outer)
    return (conv_new * mask_new, mask_int, stacked[1], stacked[2], conv_mom * mask_new, head_new, stacked[4], stacked[5], head_mom, norm_new, stacked[7], stacked[8], norm_mom, bias_new, stacked[10], stacked[11], bias_mom, stacked[12])
```

```python
import functools

import jax
import jax.numpy as jnp
from jax import lax
from jax.experimental import pallas as pl
from jax.experimental.pallas import tpu as pltpu
from jax.sharding import PartitionSpec as P

C_IN = 2048
C_MID = 512
CLASSES = 1000
WIDE = 1024
SIDE = 7
STEP = 10
PIX = 49
DROP_CUT = 78643
GROW_CUT = 242484
BF = jnp.bfloat16
F32 = jnp.float32
I32 = jnp.int32
I16 = jnp.int16
EXTRA = 16
LEVELS = 32000.0
VMEM_BYTES = 44 * 1024 * 1024


def swap(x, axis, bit):
    n = lax.axis_size(axis)
    return lax.ppermute(x, axis, [(i, i ^ bit) for i in range(n)])


def bits_of(axis):
    n = lax.axis_size(axis)
    return [1 << k for k in range(n.bit_length() - 1)]


def sum_all(x, axis):
    for bit in bits_of(axis):
        x = x + swap(x, axis, bit)
    return x


def pick(x, axis, index):
    return lax.dynamic_index_in_dim(x, index, axis, keepdims=False)


def gather_pieces(own):
    bits = bits_of("dp")
    buf, rel = own[None], [0]
    for bit in reversed(bits[2:]):
        buf = jnp.concatenate([buf, swap(buf, "dp", bit)], axis=0)
        rel = rel + [r ^ bit for r in rel]
    near = swap(buf, "dp", bits[1])
    side = swap(buf, "dp", bits[0])
    far = swap(near, "dp", bits[0])
    pieces = [buf, near, side, far]
    shifts = [0, bits[1], bits[0], bits[1] | bits[0]]
    codes = [[(0, r ^ s) for r in rel] for s in shifts]
    pieces += [swap(p, "rep", 1) for p in pieces]
    codes += [[(1, r) for _, r in c] for c in codes]
    if own.shape[1] % 16:
        return place(pieces, codes), None
    return pieces, codes


def place(pieces, codes):
    n = lax.axis_size("dp")
    flat = [c * n + r for code in codes for c, r in code]
    inverse = jnp.array([flat.index(k) for k in range(2 * n)], I32)
    me = (lax.axis_index("rep") % 2) * n + lax.axis_index("dp")
    full = jnp.take(jnp.concatenate(pieces, axis=0), inverse[jnp.arange(2 * n, dtype=I32) ^ me], axis=0)
    _, blocks, r, w = full.shape
    full = full.reshape(2, n, blocks, r, w).transpose(2, 1, 0, 3, 4)
    return [full.reshape(1, blocks, n * 2 * r, w)]


def assemble(refs, codes, me, out, blocks):
    for p, ref in enumerate(refs):
        r = ref.shape[2]
        for i in range(ref.shape[0]):
            if codes is None:
                row = 0
            else:
                c, s = codes[p][i]
                row = pl.multiple_of(((me[0] ^ s) * 2 + (me[1] ^ c)) * r, 16)
            for at, b in enumerate(blocks):
                out[at, pl.ds(row, r), :] = ref[i, b]


def code_scale(k):
    return jnp.exp2(k * (1.0 / 16.0))


def code_step(top):
    return jnp.minimum(jnp.ceil(jnp.log2(jnp.maximum(top, 1e-30)) * 16.0), 2032.0)


def code_of(x, k):
    return jnp.floor(x * (LEVELS / code_scale(k)) + 0.5).astype(I32).astype(I16)


def value_of(q, k):
    return q.astype(I32).astype(F32) * (code_scale(k.astype(I32).astype(F32)) * (1.0 / LEVELS))


def encode(x):
    top = jnp.max(jnp.abs(x), axis=1, keepdims=True)
    k = code_step(top)
    row = jnp.broadcast_to(k, (x.shape[0], EXTRA, x.shape[2])).astype(I32).astype(I16)
    return jnp.concatenate([code_of(x, k), row], axis=1)


def decode(payload):
    rows = payload.shape[1] - EXTRA
    return value_of(payload[:, :rows], payload[:, rows : rows + 1])


def split_plain(full, bit):
    b, n, r, w = full.shape
    view = full.reshape(b, n // 2, 2, r, w)
    return encode(pick(view, 2, 1 - bit).reshape(b, n // 2 * r, w)), pick(view, 2, bit)


def put_split(block, bit, send_ref, keep_ref, at):
    n, r, w = block.shape
    top = jnp.zeros((1, w), F32)
    for j in range(n // 2):
        keep_ref[at, j] = block[2 * j + bit]
        top = jnp.maximum(top, jnp.max(jnp.abs(block[2 * j + 1 - bit]), axis=0, keepdims=True))
    k = code_step(top)
    for j in range(n // 2):
        send_ref[at, j * r : (j + 1) * r, :] = code_of(block[2 * j + 1 - bit], k)
    send_ref[at, n // 2 * r :, :] = jnp.broadcast_to(k, (EXTRA, w)).astype(I32).astype(I16)


def emit(block, bit_ref, outs):
    if len(outs) == 1:
        outs[0][0] = block[...]
    else:
        put_split(block, bit_ref[0], *outs, 0)


def part_shape(n, r):
    return (n, r) if r % 16 == 0 else (1, n * r)


def split_of(outs, n, r, bit):
    if len(outs) == 2:
        return outs
    full = outs[0]
    return split_plain(full.reshape(full.shape[0], n, r, full.shape[-1]), bit)


def split_shapes(blocks, n, r, w):
    if r % 16:
        return [jax.ShapeDtypeStruct((blocks, 1, n * r, w), F32)]
    return [
        jax.ShapeDtypeStruct((blocks, n // 2 * r + EXTRA, w), I16),
        jax.ShapeDtypeStruct((blocks, n // 2, r, w), F32),
    ]


def add_split_kernel(bit_ref, keep_in, got, send_ref, keep_ref, total):
    n, r = keep_in.shape[1:3]
    k = got[0, n * r : n * r + 16, :][0:1]
    for j in range(n):
        total[j] = keep_in[0, j] + value_of(got[0, j * r : (j + 1) * r, :], k)
    put_split(total, bit_ref[0], send_ref, keep_ref, 0)


def add_split(keep, got, bit):
    b, n, r, w = keep.shape
    if r % 16:
        return split_plain(keep + decode(got).reshape(keep.shape), bit)
    one = lambda shape: pl.BlockSpec((1,) + shape, lambda i: (i,) + (0,) * len(shape))
    return pl.pallas_call(
        add_split_kernel,
        grid=(b,),
        in_specs=[
            pl.BlockSpec(memory_space=pltpu.SMEM), one((n, r, w)), one((n * r + EXTRA, w)),
        ],
        out_specs=[one((n // 2 * r + EXTRA, w)), one((n // 2, r, w))],
        out_shape=split_shapes(b, n, r, w),
        scratch_shapes=[pltpu.VMEM((n, r, w), F32)],
        name="add_split",
    )(bit.reshape(1), keep, got)


def scatter(send, keep, bits):
    me = lax.axis_index("dp")
    for at, bit in enumerate(bits):
        got = swap(send, "dp", bit)
        if at == len(bits) - 1:
            return keep[:, 0] + decode(got)
        send, keep = add_split(keep, got, (me // bits[at + 1]) % 2)


def norm_of(y, sums, gain, shift, total):
    mean = sums[0:1] * (1.0 / total)
    var = sums[1:2] * (1.0 / total) - mean * mean
    rstd = lax.rsqrt(var + 1e-05)
    n = (y - mean) * rstd
    return n, gain * n + shift, rstd


def sigmoid(z):
    return 1.0 / (1.0 + jnp.exp(-z))


def silu_grad(z):
    sig = sigmoid(z)
    return sig * (1.0 + z * (1.0 - sig))


def flat(x):
    return x.reshape(-1, x.shape[-1])


SMEM = pl.BlockSpec(memory_space=pltpu.SMEM)
PARAMS = pltpu.CompilerParams(vmem_limit_bytes=VMEM_BYTES)


def whole(shape):
    return pl.BlockSpec(tuple(shape), lambda *_: (0,) * len(shape))


def cost(flops, byte_count):
    return pl.CostEstimate(flops=int(flops), bytes_accessed=int(byte_count), transcendentals=0)


def first_kernel(codes, count, me, x, *refs):
    pieces, (y, sums, weights) = refs[:count], refs[count:]
    step = pl.program_id(0)

    @pl.when(step == 0)
    def _():
        assemble(pieces, codes, me, weights, range(weights.shape[0]))
        sums[...] = jnp.zeros_like(sums)

    out = jnp.dot(x[0], weights[...].reshape(-1, C_MID), preferred_element_type=F32)
    y[0] = out
    sums[0:1] += jnp.sum(out, axis=0, keepdims=True)
    sums[1:2] += jnp.sum(out * out, axis=0, keepdims=True)


def first_forward(me, x, pieces, codes):
    rows = x.shape[1]
    blocks = C_IN // C_MID
    return pl.pallas_call(
        functools.partial(first_kernel, codes, len(pieces)),
        grid=(SIDE,),
        in_specs=[SMEM, pl.BlockSpec((1, rows, C_IN), lambda i: (i, 0, 0))]
        + [whole(p.shape) for p in pieces],
        out_specs=[pl.BlockSpec((1, rows, C_MID), lambda i: (i, 0, 0)), whole((2, C_MID))],
        out_shape=[
            jax.ShapeDtypeStruct((SIDE, rows, C_MID), F32),
            jax.ShapeDtypeStruct((2, C_MID), F32),
        ],
        scratch_shapes=[pltpu.VMEM((blocks, C_MID, C_MID), BF)],
        compiler_params=PARAMS,
        cost_estimate=cost(2 * SIDE * rows * C_IN * C_MID, 12e6),
        name="first_forward",
    )(me, x, *pieces)


def second_kernel(codes, count, total, me, y1, sums1, params, *refs):
    pieces, (h1, y2, sums2, pad, taps) = refs[:count], refs[count:]
    step = pl.program_id(0)
    batch = pad.shape[2]

    @pl.when(step == 0)
    def _():
        pad[...] = jnp.zeros_like(pad)
        assemble(pieces, codes, me, taps, range(9))
        sums2[...] = jnp.zeros_like(sums2)

    @pl.when(step < SIDE)
    def _():
        _, z, _ = norm_of(y1[0], sums1[...], params[0:1], params[1:2], total)
        h = (z * sigmoid(z)).astype(BF)
        h1[0] = h
        pad[step + 1, 1 : SIDE + 1] = h.reshape(SIDE, batch, C_MID)

    @pl.when(step > 0)
    def _():
        out = None
        for a in range(3):
            patch = jnp.concatenate(
                [flat(pad[step - 1 + a, b : b + SIDE]) for b in range(3)], axis=1
            )
            part = jnp.dot(
                patch, taps[3 * a : 3 * a + 3].reshape(3 * C_MID, C_MID), preferred_element_type=F32
            )
            out = part if out is None else out + part
        y2[0] = out
        sums2[0:1] += jnp.sum(out, axis=0, keepdims=True)
        sums2[1:2] += jnp.sum(out * out, axis=0, keepdims=True)


def second_forward(me, y1, sums1, params, pieces, codes, total):
    rows = y1.shape[1]
    batch = rows // SIDE
    row = lambda f: pl.BlockSpec((1, rows, C_MID), lambda i: (f(i), 0, 0))
    here = row(lambda i: jnp.minimum(i, SIDE - 1))
    return pl.pallas_call(
        functools.partial(second_kernel, codes, len(pieces), total),
        grid=(SIDE + 1,),
        in_specs=[SMEM, here, whole(sums1.shape), whole(params.shape)] + [whole(p.shape) for p in pieces],
        out_specs=[here, row(lambda i: jnp.maximum(i - 1, 0)), whole((2, C_MID))],
        out_shape=[
            jax.ShapeDtypeStruct((SIDE, rows, C_MID), BF),
            jax.ShapeDtypeStruct((SIDE, rows, C_MID), F32),
            jax.ShapeDtypeStruct((2, C_MID), F32),
        ],
        scratch_shapes=[
            pltpu.VMEM((SIDE + 2, SIDE + 2, batch, C_MID), BF),
            pltpu.VMEM((9, C_MID, C_MID), BF),
        ],
        compiler_params=PARAMS,
        cost_estimate=cost(2 * SIDE * rows * 9 * C_MID * C_MID, 14e6),
        name="second_forward",
    )(me, y1, sums1, params, *pieces)


def head_kernel(codes, count, total, group_images, me, y2, sums2, params, bias, labels, *refs):
    pieces, (grad, packed, dpool_out, head, sum_h, sum_a, sum_b) = refs[:count], refs[count:]
    step = pl.program_id(0)
    batch = sum_h.shape[0]

    @pl.when(step == 0)
    def _():
        assemble(pieces, codes, me, head, (9, 10))
        for ref in (sum_h, sum_a, sum_b):
            ref[...] = jnp.zeros_like(ref)

    n, z, _ = norm_of(y2[0], sums2[...], params[2:3], params[3:4], total)
    sig = sigmoid(z)
    slope = sig * (1.0 + z * (1.0 - sig))
    fold = lambda v: jnp.sum(v.reshape(SIDE, batch, C_MID), axis=0)
    sum_h[...] += fold(z * sig)
    sum_a[...] += fold(slope)
    sum_b[...] += fold(slope * n)

    @pl.when(step == SIDE - 1)
    def _():
        pooled = (sum_h[...] * (1.0 / PIX)).astype(BF)
        logits = jnp.concatenate(
            [jnp.dot(pooled, head[k], preferred_element_type=F32) for k in range(2)], axis=1
        )
        logits = logits + bias[...]
        column = lax.broadcasted_iota(I32, (batch, WIDE), 1)
        logits = jnp.where(column < CLASSES, logits, -1e30)
        onehot = (labels[...] == column).astype(F32)
        top = jnp.max(logits, axis=1, keepdims=True)
        expo = jnp.exp(logits - top)
        expsum = jnp.sum(expo, axis=1, keepdims=True)
        lse = top + jnp.log(expsum)
        loss = jnp.sum(lse - jnp.sum(logits * onehot, axis=1, keepdims=True), axis=0, keepdims=True)
        dlogits = ((jnp.exp(logits - lse) - onehot) * (1.0 / group_images)).astype(BF)
        bias_sum = jnp.sum(dlogits.astype(F32), axis=0, keepdims=True)
        last = lax.broadcasted_iota(I32, (1, WIDE), 1) == WIDE - 1
        bias_sum = jnp.where(last, loss, bias_sum)
        dpool = jnp.zeros((batch, C_MID), F32)
        for k in range(2):
            part = dlogits[:, k * C_MID : (k + 1) * C_MID]
            grad[k] = lax.dot_general(
                pooled, part, (((0,), (0,)), ((), ())), preferred_element_type=F32
            )
            dpool = dpool + lax.dot_general(
                part, head[k], (((1,), (1,)), ((), ())), preferred_element_type=F32
            )
        dpool = dpool * (1.0 / PIX)
        dpool_out[...] = dpool
        packed[0:1] = jnp.sum(dpool * sum_b[...], axis=0, keepdims=True)
        packed[1:2] = jnp.sum(dpool * sum_a[...], axis=0, keepdims=True)
        packed[2:3] = bias_sum[:, :C_MID]
        packed[3:4] = bias_sum[:, C_MID:]


def head_step(me, y2, sums2, params, bias, labels, pieces, codes, total, group_images):
    rows = y2.shape[1]
    batch = rows // SIDE
    return pl.pallas_call(
        functools.partial(head_kernel, codes, len(pieces), total, group_images),
        grid=(SIDE,),
        in_specs=[
            SMEM, pl.BlockSpec((1, rows, C_MID), lambda i: (i, 0, 0)), whole(sums2.shape),
            whole(params.shape), whole(bias.shape), whole(labels.shape),
        ] + [whole(p.shape) for p in pieces],
        out_specs=[whole((2, C_MID, C_MID)), whole((4, C_MID)), whole((batch, C_MID))],
        out_shape=[
            jax.ShapeDtypeStruct((2, C_MID, C_MID), F32),
            jax.ShapeDtypeStruct((4, C_MID), F32),
            jax.ShapeDtypeStruct((batch, C_MID), F32),
        ],
        scratch_shapes=[pltpu.VMEM((2, C_MID, C_MID), BF)] + [pltpu.VMEM((batch, C_MID), F32)] * 3,
        compiler_params=PARAMS,
        cost_estimate=cost(40e6, 10e6),
        name="head_step",
    )(me, y2, sums2, params, bias, labels, *pieces)


def taps_kernel(total, first_tap, count, bit_ref, y2, sums2, back, params, dpool, h1, dy_out, turned, *refs):
    outs, (pad, block) = refs[:-2], refs[-2:]
    step = pl.program_id(0)
    batch = pad.shape[2]

    @pl.when(step == 0)
    def _():
        pad[...] = jnp.zeros_like(pad)
        turned[...] = h1[...].T

    @pl.when(step < SIDE)
    def _():
        n, z, rstd = norm_of(y2[0], sums2[...], params[2:3], params[3:4], total)
        dz = silu_grad(z).reshape(SIDE, batch, C_MID) * dpool[...][None]
        dz = flat(dz)
        dy = params[2:3] * rstd * (dz - back[1:2] * (1.0 / total) - n * (back[0:1] * (1.0 / total)))
        pad[step + 1, 1 : SIDE + 1] = dy.astype(BF).reshape(SIDE, batch, C_MID)

    @pl.when(step == SIDE - 1)
    def _():
        dy_out[...] = pad[...]

    @pl.when(step >= SIDE)
    def _():
        tap = step - SIDE + first_tap
        one_tap(tap, pad, turned, bit_ref, block, outs)


def one_tap(tap, pad, turned, bit_ref, block, outs):
    a, b = tap // 3, tap % 3
    moved = flat(pad[pl.ds(2 - a, SIDE), pl.ds(2 - b, SIDE)].reshape(-1, C_MID))
    block[...] = jnp.dot(turned[...], moved, preferred_element_type=F32).reshape(block.shape)
    emit(block, bit_ref, outs)


def taps_more_kernel(first_tap, bit_ref, pad, turned, *refs):
    one_tap(pl.program_id(0) + first_tap, pad, turned, bit_ref, refs[-1], refs[:-1])


def split_specs(n, r, f):
    if r % 16:
        return [pl.BlockSpec((1, 1, n * r, C_MID), lambda i: (f(i), 0, 0, 0))]
    return [
        pl.BlockSpec((1, n // 2 * r + EXTRA, C_MID), lambda i: (f(i), 0, 0)),
        pl.BlockSpec((1, n // 2, r, C_MID), lambda i: (f(i), 0, 0, 0)),
    ]


def taps_grad_first(bit, y2, sums2, back, params, dpool, h1, total, n, r, first_tap, count):
    rows = y2.shape[1]
    batch = rows // SIDE
    padded = (SIDE + 2, SIDE + 2, batch, C_MID)
    return pl.pallas_call(
        functools.partial(taps_kernel, total, first_tap, count),
        grid=(SIDE + count,),
        in_specs=[
            SMEM, pl.BlockSpec((1, rows, C_MID), lambda i: (jnp.minimum(i, SIDE - 1), 0, 0)),
            whole(sums2.shape), whole(back.shape), whole(params.shape), whole(dpool.shape),
            whole(h1.shape),
        ],
        out_specs=[whole(padded), whole((C_MID, h1.shape[0]))]
        + split_specs(n, r, lambda i: jnp.maximum(i - SIDE, 0)),
        out_shape=[
            jax.ShapeDtypeStruct(padded, BF), jax.ShapeDtypeStruct((C_MID, h1.shape[0]), BF),
        ] + split_shapes(count, n, r, C_MID),
        scratch_shapes=[pltpu.VMEM(padded, BF), pltpu.VMEM(part_shape(n, r) + (C_MID,), F32)],
        compiler_params=PARAMS,
        cost_estimate=cost(2 * SIDE * rows * count * C_MID * C_MID, 14e6),
        name="taps_grad_first",
    )(bit.reshape(1), y2, sums2, back, params, dpool, h1)


def taps_grad_more(bit, pad, turned, n, r, first_tap, count):
    return pl.pallas_call(
        functools.partial(taps_more_kernel, first_tap),
        grid=(count,),
        in_specs=[SMEM, whole(pad.shape), whole(turned.shape)],
        out_specs=split_specs(n, r, lambda i: i),
        out_shape=split_shapes(count, n, r, C_MID),
        scratch_shapes=[pltpu.VMEM(part_shape(n, r) + (C_MID,), F32)],
        compiler_params=PARAMS,
        cost_estimate=cost(2 * turned.shape[1] * count * C_MID * C_MID, 10e6),
        name="taps_grad_more",
    )(bit.reshape(1), pad, turned)


def input_grad_kernel(codes, count, total, me, pad, y1, sums1, params, *refs):
    pieces, (dz1, sums, taps) = refs[:count], refs[count:]
    step = pl.program_id(0)

    @pl.when(step == 0)
    def _():
        assemble(pieces, codes, me, taps, range(9))
        sums[...] = jnp.zeros_like(sums)

    dh = None
    for a in range(3):
        for b in range(3):
            part = lax.dot_general(
                flat(pad[step + 2 - a, 2 - b : 2 - b + SIDE]), taps[3 * a + b],
                (((1,), (1,)), ((), ())), preferred_element_type=F32,
            )
            dh = part if dh is None else dh + part
    n, z, _ = norm_of(y1[0], sums1[...], params[0:1], params[1:2], total)
    dz = dh * silu_grad(z)
    dz1[0] = dz
    sums[0:1] += jnp.sum(dz * n, axis=0, keepdims=True)
    sums[1:2] += jnp.sum(dz, axis=0, keepdims=True)


def input_grad(me, pad, y1, sums1, params, pieces, codes, total):
    rows = y1.shape[1]
    row = pl.BlockSpec((1, rows, C_MID), lambda i: (i, 0, 0))
    return pl.pallas_call(
        functools.partial(input_grad_kernel, codes, len(pieces), total),
        grid=(SIDE,),
        in_specs=[SMEM, whole(pad.shape), row, whole(sums1.shape), whole(params.shape)]
        + [whole(p.shape) for p in pieces],
        out_specs=[row, whole((2, C_MID))],
        out_shape=[
            jax.ShapeDtypeStruct(y1.shape, F32), jax.ShapeDtypeStruct((2, C_MID), F32),
        ],
        scratch_shapes=[pltpu.VMEM((9, C_MID, C_MID), BF)],
        compiler_params=PARAMS,
        cost_estimate=cost(2 * SIDE * rows * 9 * C_MID * C_MID, 16e6),
        name="input_grad",
    )(me, pad, y1, sums1, params, *pieces)


def first_grad_kernel(total, bit_ref, dz1, y1, sums1, back, params, x, dy_out, *refs):
    step = pl.program_id(0)

    @pl.when(step < SIDE)
    def _():
        n, _, rstd = norm_of(y1[0], sums1[...], params[0:1], params[1:2], total)
        dy = params[0:1] * rstd * (
            dz1[0] - back[1:2] * (1.0 / total) - n * (back[0:1] * (1.0 / total))
        )
        dy_out[step] = dy.astype(BF)

    @pl.when(step >= SIDE)
    def _():
        one_first(x, dy_out, bit_ref, refs[-1], refs[:-1])


def one_first(x, dy, bit_ref, block, outs):
    block[...] = lax.dot_general(
        flat(x[...]), flat(dy[...]), (((0,), (0,)), ((), ())), preferred_element_type=F32
    ).reshape(block.shape)
    emit(block, bit_ref, outs)


def first_more_kernel(bit_ref, x, dy, *refs):
    one_first(x, dy, bit_ref, refs[-1], refs[:-1])


def first_grad_first(bit, dz1, y1, sums1, back, params, x, total, n, r, count):
    rows = y1.shape[1]
    row = pl.BlockSpec((1, rows, C_MID), lambda i: (jnp.minimum(i, SIDE - 1), 0, 0))
    here = lambda i: jnp.maximum(i - SIDE, 0)
    return pl.pallas_call(
        functools.partial(first_grad_kernel, total),
        grid=(SIDE + count,),
        in_specs=[
            SMEM, row, row, whole(sums1.shape), whole(back.shape), whole(params.shape),
            pl.BlockSpec((SIDE, rows, C_MID), lambda i: (0, 0, here(i))),
        ],
        out_specs=[whole((SIDE, rows, C_MID))] + split_specs(n, r, here),
        out_shape=[jax.ShapeDtypeStruct((SIDE, rows, C_MID), BF)] + split_shapes(count, n, r, C_MID),
        scratch_shapes=[pltpu.VMEM(part_shape(n, r) + (C_MID,), F32)],
        compiler_params=PARAMS,
        cost_estimate=cost(2 * SIDE * rows * count * C_MID * C_MID, 14e6),
        name="first_grad_first",
    )(bit.reshape(1), dz1, y1, sums1, back, params, x)


def first_grad_more(bit, x, dy, n, r, first_block, count):
    rows = dy.shape[1]
    return pl.pallas_call(
        first_more_kernel,
        grid=(count,),
        in_specs=[
            SMEM, pl.BlockSpec((SIDE, rows, C_MID), lambda i: (0, 0, i + first_block)), whole(dy.shape),
        ],
        out_specs=split_specs(n, r, lambda i: i),
        out_shape=split_shapes(count, n, r, C_MID),
        scratch_shapes=[pltpu.VMEM(part_shape(n, r) + (C_MID,), F32)],
        compiler_params=PARAMS,
        cost_estimate=cost(2 * SIDE * rows * count * C_MID * C_MID, 8e6),
        name="first_grad_more",
    )(bit.reshape(1), x, dy)


def adamw(weight, grad, first, second, rate):
    first = 0.9 * first + 0.1 * grad
    second = 0.999 * second + 0.001 * grad * grad
    normal_step = first / (1.0 - 0.9**STEP) / (jnp.sqrt(second / (1.0 - 0.999**STEP)) + 1e-08)
    return (-rate * (normal_step + 0.01 * weight), first, second)


def outer_step(start, step_sum, momentum, groups):
    delta = -(step_sum / groups)
    momentum = 0.9 * momentum + delta
    return (start - 0.7 * (delta + 0.9 * momentum), momentum)


def rep_sum(x):
    for bit in bits_of("rep"):
        low = x.astype(BF)
        x = low.astype(F32) + swap(low, "rep", bit).astype(F32)
    return x


def per_device(
    images, labels, conv_weight, conv_mask, conv_rank, head_weight, norm_params, head_bias,
    conv_first, conv_second, head_first, head_second, norm_first, norm_second, bias_first,
    bias_second, conv_outer, head_outer, norm_outer, bias_outer,
):
    devices = lax.axis_size("dp")
    groups = lax.axis_size("rep")
    width = C_MID
    blocks = C_IN // C_MID
    core = lax.axis_index("rep") % 2
    dp = lax.axis_index("dp")
    me = jnp.stack([dp, core]).astype(I32)
    bits = bits_of("dp")
    bit = dp % 2
    shard = conv_weight.shape[1]
    batch = images.shape[0]
    rows = batch * PIX
    total = float(rows * devices)
    group_images = batch * devices
    half = shard // 2

    def mine(x):
        return pick(x.reshape(-1, 2, half, width), 1, core)

    def active(sl):
        return jnp.where(mine(conv_mask[sl]) == 1, mine(conv_weight[sl]), 0.0).astype(BF)

    head_wide = jnp.pad(head_weight.astype(BF), ((0, 0), (0, WIDE - CLASSES)))
    head_low = mine(head_wide.reshape(shard, 2, width).transpose(1, 0, 2))
    first_pieces, first_codes = gather_pieces(active(slice(0, blocks)))
    rest = jnp.concatenate([active(slice(blocks, None)), head_low], axis=0)
    taps_pieces, taps_codes = gather_pieces(rest)
    x = images.transpose(1, 2, 0, 3).reshape(SIDE, SIDE * batch, C_IN)
    y_one, sums_one = first_forward(me, x, first_pieces, first_codes)
    sums_one = sum_all(sums_one, "dp")
    h_one, y_two, sums_two = second_forward(
        me, y_one, sums_one, norm_params, taps_pieces, taps_codes, total
    )
    sums_two = sum_all(sums_two, "dp")
    bias_wide = jnp.pad(head_bias, (0, WIDE - CLASSES)).reshape(1, WIDE)
    head_local, packed, dpool = head_step(
        me, y_two, sums_two, norm_params, bias_wide, labels[:, None], taps_pieces, taps_codes, total,
        group_images,
    )
    packed = sum_all(packed, "dp")
    bias_grad = packed[2:].reshape(-1)[:CLASSES]
    loss_sum = packed[3, C_MID - 1 :]
    head_send, head_keep = split_plain(head_local.reshape(2, devices, shard, width), bit)
    cut = 4
    n, r = devices, shard
    grads = {}
    pad, turned, *outs = taps_grad_first(
        bit, y_two, sums_two, packed, norm_params, dpool, flat(h_one), total, n, r, 0, cut
    )
    grads["taps_a"] = (*split_of(outs, n, r, bit), blocks)
    outs = taps_grad_more(bit, pad, turned, n, r, cut, 9 - cut)
    grads["taps_b"] = (*split_of(outs, n, r, bit), blocks + cut)
    dz_one, back_one = input_grad(
        me, pad, y_one, sums_one, norm_params, taps_pieces, taps_codes, total
    )
    back_one = sum_all(back_one, "dp")
    dy_one, *outs = first_grad_first(
        bit, dz_one, y_one, sums_one, back_one, norm_params, x, total, n, r, 2
    )
    grads["first_a"] = (*split_of(outs, n, r, bit), 0)
    outs = first_grad_more(bit, x, dy_one, n, r, 2, 2)
    grads["first_b"] = (*split_of(outs, n, r, bit), 2)

    mask_old = conv_mask.astype(F32)
    dropped = (conv_mask == 1) & (conv_rank < DROP_CUT)
    grown = (conv_mask == 0) & (conv_rank >= GROW_CUT)
    mask_int = jnp.where(dropped, 0, jnp.where(grown, 1, conv_mask))
    mask_new = mask_int.astype(F32)
    kept = mask_old * mask_new
    effective = conv_weight * mask_old
    start = conv_weight * kept
    head_grad = scatter(head_send, head_keep, bits)
    head_grad = head_grad.transpose(1, 0, 2).reshape(shard, WIDE)[:, :CLASSES]
    done = {}
    for send, keep, at in grads.values():
        count = keep.shape[0]
        sl = slice(at, at + count)
        owned = scatter(send, keep, bits)
        dense = owned + 5e-05 * effective[sl]
        step, m, v = adamw(
            start[sl], mask_new[sl] * dense, conv_first[0, sl] * kept[sl],
            conv_second[0, sl] * kept[sl], 0.03
        )
        new, mom = outer_step(start[sl], rep_sum(step * mask_new[sl]), conv_outer[sl], groups)
        done[at] = (new * mask_new[sl], m * mask_new[sl], v * mask_new[sl], mom * mask_new[sl])
    conv_new, conv_m, conv_v, conv_mom = (
        jnp.concatenate([done[at][k] for at in sorted(done)], axis=0) for k in range(4)
    )
    norm_grad = jnp.concatenate([back_one, packed[:2]], axis=0)
    head_s, head_m, head_v = adamw(head_weight, head_grad, head_first[0], head_second[0], 0.03)
    head_new, head_mom = outer_step(head_weight, rep_sum(head_s), head_outer, groups)
    norm_s, norm_m, norm_v = adamw(norm_params, norm_grad, norm_first[0], norm_second[0], 0.3)
    bias_s, bias_m, bias_v = adamw(head_bias, bias_grad, bias_first[0], bias_second[0], 0.3)
    small = jnp.concatenate([norm_s.reshape(-1), bias_s, jnp.zeros((24,), F32)]).reshape(-1, 128)
    small = sum_all(small, "rep").reshape(-1)
    norm_new, norm_mom = outer_step(norm_params, small[: 4 * width].reshape(4, width), norm_outer, groups)
    bias_new, bias_mom = outer_step(head_bias, small[4 * width : 4 * width + CLASSES], bias_outer, groups)
    return (
        conv_new, mask_int, conv_m[None], conv_v[None], conv_mom,
        head_new, head_m[None], head_v[None], head_mom,
        norm_new, norm_m[None], norm_v[None], norm_mom,
        bias_new, bias_m[None], bias_v[None], bias_mom, loss_sum,
    )
def solution(mesh):
    conv = P(None, "dp", None)
    conv_rep = P("rep", None, "dp", None)
    head = P("dp", None)
    head_rep = P("rep", "dp", None)
    in_specs = (
        P(("rep", "dp"), None, None, None), P(("rep", "dp")), conv, conv, conv, head, P(), P(),
        conv_rep, conv_rep, head_rep, head_rep, P("rep", None, None), P("rep", None, None),
        P("rep", None), P("rep", None), conv, head, P(), P(),
    )
    out_specs = (
        conv, conv, conv_rep, conv_rep, conv, head, head_rep, head_rep, head,
        P(), P("rep", None, None), P("rep", None, None), P(),
        P(), P("rep", None), P("rep", None), P(), P("rep"),
    )
    return jax.shard_map(
        per_device, mesh=mesh, in_specs=in_specs, out_specs=out_specs, check_vma=False
    )
```

```python
import functools

import jax
import jax.numpy as jnp
from jax import lax
from jax.experimental import pallas as pl
from jax.experimental.pallas import tpu as pltpu
from jax.sharding import PartitionSpec as P

C_IN = 2048
C_MID = 512
CLASSES = 1000
WIDE = 1024
SIDE = 7
STEP = 10
PIX = 49
DROP_CUT = 78643
GROW_CUT = 242484
BF = jnp.bfloat16
F32 = jnp.float32
I32 = jnp.int32
I16 = jnp.int16
EXTRA = 16
LEVELS = 32000.0
LOG2E = 1.4426950408889634


def swap(x, axis, bit):
    n = lax.axis_size(axis)
    return lax.ppermute(x, axis, [(i, i ^ bit) for i in range(n)])


def bits_of(axis):
    n = lax.axis_size(axis)
    return [1 << k for k in range(n.bit_length() - 1)]


def sum_all(x, axis, *deps):
    bits = bits_of(axis)
    bits = bits[1:] + bits[:1]
    for bit in bits:
        if deps and bit == bits[-1]:
            x = after(x, *deps)
        x = x + swap(x, axis, bit)
    return x


def room(mib):
    return pltpu.CompilerParams(vmem_limit_bytes=mib * 1024 * 1024)


def pick(x, axis, index):
    return lax.dynamic_index_in_dim(x, index, axis, keepdims=False)


def gather_more(buf, rel, bit, *deps):
    buf = after(buf, *deps) if deps else buf
    return jnp.concatenate([buf, swap(buf, "dp", bit)], axis=0), rel + [r ^ bit for r in rel]


class Gather:
    def __init__(self, own):
        bits = bits_of("dp")
        self.own, self.rel = own[None], [0]
        for bit in reversed(bits[2:]):
            self.own = jnp.concatenate([self.own, swap(self.own, "dp", bit)], axis=0)
            self.rel = self.rel + [r ^ bit for r in self.rel]

    def spread(self, *deps):
        own = after(self.own, *deps) if deps else self.own
        bits = bits_of("dp")
        self.near, self.side = swap(own, "dp", bits[1]), swap(own, "dp", bits[0])

    def reach(self, *deps):
        near = after(self.near, *deps) if deps else self.near
        self.far = swap(near, "dp", bits_of("dp")[0])

    def finish(self, *deps):
        bits = bits_of("dp")
        far = after(self.far, *deps) if deps else self.far
        pieces = [self.own, self.near, self.side, far]
        shifts = [0, bits[1], bits[0], bits[1] | bits[0]]
        codes = [[(0, r ^ s) for r in self.rel] for s in shifts]
        pieces += [swap(p, "rep", 1) for p in pieces]
        codes += [[(1, r) for _, r in c] for c in codes]
        if self.own.shape[2] % 16:
            return place(pieces, codes), None
        return pieces, codes


def place(pieces, codes):
    n = lax.axis_size("dp")
    flat = [c * n + r for code in codes for c, r in code]
    cores = len(flat) // n
    inverse = jnp.array([flat.index(k) for k in range(len(flat))], I32)
    me = (lax.axis_index("rep") % cores) * n + lax.axis_index("dp")
    where = inverse[jnp.arange(len(flat), dtype=I32) ^ me]
    full = jnp.take(jnp.concatenate(pieces, axis=0), where, axis=0)
    _, blocks, r, w = full.shape
    full = full.reshape(cores, n, blocks, r, w).transpose(2, 1, 0, 3, 4)
    return [full.reshape(1, blocks, n * cores * r, w)]


def fetch(src, dst, sem):
    copy = pltpu.make_async_copy(src, dst, sem)
    copy.start()
    return copy


def wait_all(copies):
    for copy in copies:
        copy.wait()


def entries(pieces):
    return sum(p.shape[0] for p in pieces)


def fetch_pieces(refs, codes, me, out, sems):
    copies = []
    for p, ref in enumerate(refs):
        r = ref.shape[2]
        for i in range(ref.shape[0]):
            if codes is None:
                row = 0
            else:
                c, s = codes[p][i]
                row = me[0] ^ s
                if any(c for code in codes for c, _ in code):
                    row = row * 2 + (me[1] ^ c)
                row = pl.multiple_of(row * r, 16)
            copies.append(fetch(ref.at[i], out.at[:, pl.ds(row, r), :], sems.at[len(copies)]))
    return copies


def by_blocks(count, outs, body):
    done = []
    for i in range(count):
        body(i)
        done += [fetch(buf.at[i], at(i), sems.at[i]) for at, buf, sems in outs]
    wait_all(done)


def dma(n):
    return pltpu.SemaphoreType.DMA((n,))


ANY = pl.BlockSpec(memory_space=pl.ANY)
IN_VMEM = pl.BlockSpec(memory_space=pltpu.VMEM)


SMEM = pl.BlockSpec(memory_space=pltpu.SMEM)

def cost(flops, byte_count):
    return pl.CostEstimate(flops=1, bytes_accessed=1, transcendentals=0)


def code_scale(k):
    return jnp.exp2(k * (1.0 / 16.0))


def code_step(top):
    return jnp.minimum(jnp.ceil(jnp.log2(jnp.maximum(top, 1e-30)) * 16.0), 2032.0)


def code_of(x, k):
    return jnp.floor(x * (LEVELS / code_scale(k)) + 0.5).astype(I32).astype(I16)


def value_of(q, k):
    return q.astype(I32).astype(F32) * (code_scale(k.astype(I32).astype(F32)) * (1.0 / LEVELS))


def encode(x):
    top = jnp.max(jnp.abs(x), axis=1, keepdims=True)
    k = code_step(top)
    row = jnp.broadcast_to(k, (x.shape[0], EXTRA, x.shape[2])).astype(I32).astype(I16)
    return jnp.concatenate([code_of(x, k), row], axis=1)


def decode(payload):
    rows = payload.shape[1] - EXTRA
    return value_of(payload[:, :rows], payload[:, rows : rows + 1])


def split_plain(full, bit, stride=1):
    b, n, r, w = full.shape
    view = full.reshape(b, n // (2 * stride), 2, stride, r, w)
    keep = pick(view, 2, bit).reshape(b, n // 2, r, w)
    return encode(pick(view, 2, 1 - bit).reshape(b, n // 2 * r, w)), keep


def side_of(me, bit):
    return (me[0] // bit) % 2


def put_split(block, bit, stride, send_ref, keep_ref, at):
    n, r, w = block.shape
    top = jnp.zeros((1, w), F32)
    base = [j // stride * 2 * stride + j % stride for j in range(n // 2)]
    for j in range(n // 2):
        keep_ref[at, j] = block[base[j] + stride * bit]
        top = jnp.maximum(
            top, jnp.max(jnp.abs(block[base[j] + stride * (1 - bit)]), axis=0, keepdims=True)
        )
    k = code_step(top)
    for j in range(n // 2):
        send_ref[at, j * r : (j + 1) * r, :] = code_of(block[base[j] + stride * (1 - bit)], k)
    send_ref[at, n // 2 * r :, :] = jnp.broadcast_to(k, (EXTRA, w)).astype(I32).astype(I16)


def part_shape(n, r):
    return (n, r) if r % 16 == 0 else (1, n * r)


def split_of(me, outs, n, r, bit, stride):
    if len(outs) == 2:
        return outs
    full = outs[0]
    return split_plain(full.reshape(full.shape[0], n, r, full.shape[-1]), side_of(me, bit), stride)


def split_shapes(blocks, n, r, w):
    if r % 16:
        return [jax.ShapeDtypeStruct((blocks, 1, n * r, w), F32)]
    return [
        jax.ShapeDtypeStruct((blocks, n // 2 * r + EXTRA, w), I16),
        jax.ShapeDtypeStruct((blocks, n // 2, r, w), F32),
    ]


def add_split_kernel(bit, stride, me, keep_in, got, send, keep, total):
    n, r = keep_in.shape[1:3]
    for i in range(keep_in.shape[0]):
        k = got[i, n * r : n * r + EXTRA, :][0:1]
        for j in range(n):
            total[j] = keep_in[i, j] + value_of(got[i, j * r : (j + 1) * r, :], k)
        put_split(total, side_of(me, bit), stride, send, keep, i)


def add_split(me, keep, got, bit, stride):
    b, n, r, w = keep.shape
    if r % 16:
        return split_plain(keep + decode(got).reshape(keep.shape), side_of(me, bit), stride)
    return pl.pallas_call(
        functools.partial(add_split_kernel, bit, stride),
        in_specs=[SMEM, IN_VMEM, IN_VMEM],
        out_specs=[IN_VMEM, IN_VMEM],
        out_shape=split_shapes(b, n, r, w),
        scratch_shapes=[pltpu.VMEM((n, r, w), F32)],
        compiler_params=room(8),
        cost_estimate=cost(1, 1),
        name="add_split",
    )(me, keep, got)


def after(x, *deps):
    return lax.optimization_barrier((x, deps))[0]


class Sum:
    def __init__(self, me, send, keep, bits):
        self.me = me
        self.send, self.keep, self.bits, self.done = send, keep, list(bits), []
        self.got = swap(send, "dp", self.bits[0])

    def turn(self, *deps):
        self.done.append(self.bits.pop(0))
        nxt = self.bits[0]
        stride = nxt
        for used in self.done:
            stride = stride // 2 if used < nxt else stride
        got = after(self.got, *deps) if deps else self.got
        self.send, self.keep = add_split(self.me, self.keep, got, nxt, stride)
        self.got = swap(self.send, "dp", nxt)
        return self.keep

    def turns(self, *deps):
        while len(self.bits) > 1:
            deps = (self.turn(*deps),)
        return deps


def norm_rows(sums, gain, shift, total):
    mean = sums[0:1] * (1.0 / total)
    var = sums[1:2] * (1.0 / total) - mean * mean
    rstd = lax.rsqrt(var + 1e-05)
    factor = gain * rstd
    return mean, rstd, factor, shift - mean * factor


def inverse(d):
    r = pl.reciprocal(d, approx=True)
    return r * (2.0 - d * r)


def gate(y, factor, offset):
    z = y * factor + offset
    power = jnp.minimum(y * (factor * -LOG2E) + offset * -LOG2E, 100.0)
    return z, inverse(1.0 + jnp.exp2(power))


def slope_of(z, sig):
    return sig * (1.0 + (z - z * sig))


def back_rows(back, rstd, mean, factor, total):
    d = -(factor * rstd) * (back[0:1] * (1.0 / total))
    return d, -factor * (back[1:2] * (1.0 / total)) - mean * d


def flat(x):
    return x.reshape(-1, x.shape[-1])


def add_sums(sums, one, two):
    sums[0:1] += jnp.sum(one, axis=0, keepdims=True)
    sums[1:2] += jnp.sum(two, axis=0, keepdims=True)


def first_kernel(codes, count, me, x, *refs):
    pieces, (y, sums, weights, p_sem) = refs[:count], refs[count:]
    copies = fetch_pieces(pieces, codes, me, weights, p_sem)
    sums[...] = jnp.zeros_like(sums)
    wait_all(copies)
    for k in range(SIDE):
        out = jnp.dot(x[k], weights[...].reshape(-1, C_MID), preferred_element_type=F32)
        y[k] = out
        add_sums(sums, out, out * out)


def first_forward(me, x, pieces, codes):
    rows = x.shape[1]
    return pl.pallas_call(
        functools.partial(first_kernel, codes, len(pieces)),
        in_specs=[SMEM, IN_VMEM] + [ANY] * len(pieces),
        out_specs=[IN_VMEM, IN_VMEM],
        out_shape=[
            jax.ShapeDtypeStruct((SIDE, rows, C_MID), F32), jax.ShapeDtypeStruct((2, C_MID), F32),
        ],
        scratch_shapes=[
            pltpu.VMEM((C_IN // C_MID, C_MID, C_MID), BF), dma(entries(pieces)),
        ],
        compiler_params=room(8),
        cost_estimate=cost(1, 1),
        name="first_forward",
    )(me, x, *pieces)


def clear_border(pad):
    zero = jnp.zeros(pad.shape[1:], pad.dtype)
    pad[0] = zero
    pad[SIDE + 1] = zero
    for k in range(1, SIDE + 1):
        pad[k, 0] = zero[0]
        pad[k, SIDE + 1] = zero[0]


def second_kernel(codes, count, total, me, y1, sums1, params, *refs):
    pieces, (h1, y2, sums2, taps, pad, p_sem) = refs[:count], refs[count:]
    batch = pad.shape[2]
    copies = fetch_pieces(pieces, codes, me, taps, p_sem)
    clear_border(pad)
    sums2[...] = jnp.zeros_like(sums2)
    _, _, factor, offset = norm_rows(sums1[...], params[0:1], params[1:2], total)

    def act(k):
        z, sig = gate(y1[k], factor, offset)
        h = (z * sig).astype(BF).reshape(SIDE, batch, C_MID)
        pad[k + 1, 1 : SIDE + 1] = h
        h1[k] = h

    act(0)
    act(1)
    wait_all(copies)
    for k in range(SIDE):
        out = None
        for a in range(3):
            if 0 <= k + a - 1 < SIDE:
                patch = jnp.concatenate([flat(pad[k + a, b : b + SIDE]) for b in range(3)], axis=1)
                part = jnp.dot(
                    patch, taps[3 * a : 3 * a + 3].reshape(3 * C_MID, C_MID),
                    preferred_element_type=F32,
                )
                out = part if out is None else out + part
        if k + 2 < SIDE:
            act(k + 2)
        y2[k] = out
        add_sums(sums2, out, out * out)


def second_forward(me, y1, sums1, params, pieces, codes, total):
    rows = y1.shape[1]
    batch = rows // SIDE
    return pl.pallas_call(
        functools.partial(second_kernel, codes, len(pieces), total),
        in_specs=[SMEM, IN_VMEM, IN_VMEM, IN_VMEM] + [ANY] * len(pieces),
        out_specs=[IN_VMEM] * 4,
        out_shape=[
            jax.ShapeDtypeStruct((SIDE, SIDE, batch, C_MID), BF),
            jax.ShapeDtypeStruct(y1.shape, F32),
            jax.ShapeDtypeStruct((2, C_MID), F32),
            jax.ShapeDtypeStruct((9, C_MID, C_MID), BF),
        ],
        scratch_shapes=[
            pltpu.VMEM((SIDE + 2, SIDE + 2, batch, C_MID), BF), dma(entries(pieces)),
        ],
        compiler_params=room(12),
        cost_estimate=cost(1, 1),
        name="second_forward",
    )(me, y1, sums1, params, *pieces)


def head_kernel(codes, count, outs_n, total, group_images, me, y2, sums2, params, bias, labels, *refs):
    pieces, refs = refs[:count], refs[count:]
    outs, (packed, dpool_out, head, block, p_sem) = refs[:outs_n], refs[outs_n:]
    batch = dpool_out.shape[0]
    copies = fetch_pieces(pieces, codes, me, head, p_sem)
    mean, rstd, factor, offset = norm_rows(sums2[...], params[2:3], params[3:4], total)
    sum_h = sum_a = sum_b = jnp.zeros((batch, C_MID), F32)
    fold = lambda v: jnp.sum(v.reshape(SIDE, batch, C_MID), axis=0)
    for k in range(SIDE):
        z, sig = gate(y2[k], factor, offset)
        slope = slope_of(z, sig)
        sum_h = sum_h + fold(z * sig)
        sum_a = sum_a + fold(slope)
        sum_b = sum_b + fold(slope * ((y2[k] - mean) * rstd))
    wait_all(copies)
    pooled = (sum_h * (1.0 / PIX)).astype(BF)
    logits = jnp.concatenate(
        [jnp.dot(pooled, head[k], preferred_element_type=F32) for k in range(2)], axis=1
    )
    logits = logits + bias[...]
    column = lax.broadcasted_iota(I32, (batch, WIDE), 1)
    logits = jnp.where(column < CLASSES, logits, -1e30)
    across = lax.broadcasted_iota(I32, (batch, batch), 0) == lax.broadcasted_iota(I32, (batch, batch), 1)
    label = jnp.sum(jnp.where(across, labels[...], 0), axis=1, keepdims=True)
    onehot = (label == column).astype(F32)
    top = jnp.max(logits, axis=1, keepdims=True)
    expo = jnp.exp(logits - top)
    expsum = jnp.sum(expo, axis=1, keepdims=True)
    lse = top + jnp.log(expsum)
    loss = jnp.sum(lse - jnp.sum(logits * onehot, axis=1, keepdims=True), axis=0, keepdims=True)
    dlogits = ((jnp.exp(logits - lse) - onehot) * (1.0 / group_images)).astype(BF)
    bias_sum = jnp.sum(dlogits.astype(F32), axis=0, keepdims=True)
    last = lax.broadcasted_iota(I32, (1, WIDE), 1) == WIDE - 1
    bias_sum = jnp.where(last, loss, bias_sum)
    dpool = jnp.zeros((batch, C_MID), F32)
    for k in range(2):
        part = dlogits[:, k * C_MID : (k + 1) * C_MID]
        block[...] = lax.dot_general(
            pooled, part, (((0,), (0,)), ((), ())), preferred_element_type=F32
        ).reshape(block.shape)
        emit(block, me, 1, outs, k)
        dpool = dpool + lax.dot_general(
            part, head[k], (((1,), (1,)), ((), ())), preferred_element_type=F32
        )
    dpool = dpool * (1.0 / PIX)
    dpool_out[...] = dpool
    packed[0:1] = jnp.sum(dpool * sum_b, axis=0, keepdims=True)
    packed[1:2] = jnp.sum(dpool * sum_a, axis=0, keepdims=True)
    packed[2:3] = bias_sum[:, :C_MID]
    packed[3:4] = bias_sum[:, C_MID:]


def head_step(me, y2, sums2, params, bias, labels, pieces, codes, total, group_images, n, r):
    rows = y2.shape[1]
    batch = rows // SIDE
    shapes = split_shapes(2, n, r, C_MID)
    return pl.pallas_call(
        functools.partial(head_kernel, codes, len(pieces), len(shapes), total, group_images),
        in_specs=[SMEM] + [IN_VMEM] * 5 + [ANY] * len(pieces),
        out_specs=[IN_VMEM] * (2 + len(shapes)),
        out_shape=shapes + [
            jax.ShapeDtypeStruct((4, C_MID), F32), jax.ShapeDtypeStruct((batch, C_MID), F32),
        ],
        scratch_shapes=[
            pltpu.VMEM((2, C_MID, C_MID), BF), pltpu.VMEM(part_shape(n, r) + (C_MID,), F32),
            dma(entries(pieces)),
        ],
        compiler_params=room(8),
        cost_estimate=cost(1, 1),
        name="head_step",
    )(me, y2, sums2, params, bias, labels, *pieces)


def emit(block, me, bit, outs, i):
    if len(outs) == 1:
        outs[0][i] = block[...]
    else:
        put_split(block, side_of(me, bit), bit, *outs, i)


def one_tap(tap, pad, turned, block):
    a, b = tap // 3, tap % 3
    moved = pad[2 - a : 2 - a + SIDE, 2 - b : 2 - b + SIDE].reshape(-1, C_MID)
    block[...] = jnp.dot(turned[...], moved, preferred_element_type=F32).reshape(block.shape)


def taps_kernel(total, me, y2, sums2, back, params, dpool, h1, pad, turned, *refs):
    outs, block = refs[:-1], refs[-1]
    batch = pad.shape[2]
    clear_border(pad)
    mean, rstd, factor, offset = norm_rows(sums2[...], params[2:3], params[3:4], total)
    d, e = back_rows(back, rstd, mean, factor, total)
    scaled = (dpool[...] * factor)[None]
    turned[...] = h1[...].reshape(-1, C_MID).T
    for k in range(SIDE):
        z, sig = gate(y2[k], factor, offset)
        dz = flat(slope_of(z, sig).reshape(SIDE, batch, C_MID) * scaled)
        dy = dz + (y2[k] * d + e)
        pad[k + 1, 1 : SIDE + 1] = dy.astype(BF).reshape(SIDE, batch, C_MID)
    for i in range(outs[0].shape[0]):
        one_tap(i, pad, turned, block)
        emit(block, me, 1, outs, i)


def taps_more_kernel(first_tap, me, pad, turned, *refs):
    outs, block = refs[:-1], refs[-1]
    for i in range(outs[0].shape[0]):
        one_tap(i + first_tap, pad, turned, block)
        emit(block, me, 1, outs, i)


def taps_grad_first(me, y2, sums2, back, params, dpool, h1, total, n, r, count):
    batch = h1.shape[2]
    shapes = split_shapes(count, n, r, C_MID)
    return pl.pallas_call(
        functools.partial(taps_kernel, total),
        in_specs=[SMEM] + [IN_VMEM] * 6,
        out_specs=[IN_VMEM] * (2 + len(shapes)),
        out_shape=[
            jax.ShapeDtypeStruct((SIDE + 2, SIDE + 2, batch, C_MID), BF),
            jax.ShapeDtypeStruct((C_MID, SIDE * SIDE * batch), BF),
        ] + shapes,
        scratch_shapes=[pltpu.VMEM(part_shape(n, r) + (C_MID,), F32)],
        compiler_params=room(8),
        cost_estimate=cost(1, 1),
        name="taps_grad_first",
    )(me, y2, sums2, back, params, dpool, h1)


def taps_grad_more(me, pad, turned, n, r, first_tap, count):
    shapes = split_shapes(count, n, r, C_MID)
    return pl.pallas_call(
        functools.partial(taps_more_kernel, first_tap),
        in_specs=[SMEM, IN_VMEM, IN_VMEM],
        out_specs=[IN_VMEM] * len(shapes),
        out_shape=shapes,
        scratch_shapes=[pltpu.VMEM(part_shape(n, r) + (C_MID,), F32)],
        compiler_params=room(8),
        cost_estimate=cost(1, 1),
        name="taps_grad_more",
    )(me, pad, turned)


def input_grad_kernel(total, pad, y1, sums1, params, taps, dz1, sums):
    sums[...] = jnp.zeros_like(sums)
    mean, rstd, factor, offset = norm_rows(sums1[...], params[0:1], params[1:2], total)
    for k in range(SIDE):
        dh = None
        for a in range(3):
            for b in range(3):
                if 0 <= k + 1 - a < SIDE:
                    part = lax.dot_general(
                        flat(pad[k + 2 - a, 2 - b : 2 - b + SIDE]), taps[3 * a + b],
                        (((1,), (1,)), ((), ())), preferred_element_type=F32,
                    )
                    dh = part if dh is None else dh + part
        dz = dh * slope_of(*gate(y1[k], factor, offset))
        dz1[k] = dz
        add_sums(sums, dz * ((y1[k] - mean) * rstd), dz)


def input_grad(pad, y1, sums1, params, taps, total):
    return pl.pallas_call(
        functools.partial(input_grad_kernel, total),
        in_specs=[IN_VMEM] * 5,
        out_specs=[IN_VMEM] * 2,
        out_shape=[jax.ShapeDtypeStruct(y1.shape, F32), jax.ShapeDtypeStruct((2, C_MID), F32)],
        compiler_params=room(8),
        cost_estimate=cost(1, 1),
        name="input_grad",
    )(pad, y1, sums1, params, taps)


def one_first(x, dy, at, block):
    block[...] = lax.dot_general(
        flat(x[:, :, at * C_MID : (at + 1) * C_MID]), flat(dy[...]), (((0,), (0,)), ((), ())),
        preferred_element_type=F32,
    ).reshape(block.shape)


def first_grad_kernel(total, me, dz1, y1, sums1, back, params, x, dy, *refs):
    outs, block = refs[:-1], refs[-1]
    mean, rstd, factor, _ = norm_rows(sums1[...], params[0:1], params[1:2], total)
    d, e = back_rows(back, rstd, mean, factor, total)
    for k in range(SIDE):
        dy[k] = (dz1[k] * factor + (y1[k] * d + e)).astype(BF)
    for i in range(outs[0].shape[0]):
        one_first(x, dy, i, block)
        emit(block, me, 1, outs, i)


def first_more_kernel(bit, first, me, x, dy, *refs):
    outs, block = refs[:-1], refs[-1]
    for i in range(outs[0].shape[0]):
        one_first(x, dy, first + i, block)
        emit(block, me, bit, outs, i)


def first_grad_first(me, dz1, y1, sums1, back, params, x, total, n, r, count):
    shapes = split_shapes(count, n, r, C_MID)
    return pl.pallas_call(
        functools.partial(first_grad_kernel, total),
        in_specs=[SMEM] + [IN_VMEM] * 6,
        out_specs=[IN_VMEM] * (1 + len(shapes)),
        out_shape=[jax.ShapeDtypeStruct(y1.shape, BF)] + shapes,
        scratch_shapes=[pltpu.VMEM(part_shape(n, r) + (C_MID,), F32)],
        compiler_params=room(8),
        cost_estimate=cost(1, 1),
        name="first_grad_first",
    )(me, dz1, y1, sums1, back, params, x)


def first_grad_more(me, bit, x, dy, n, r, first_block, count):
    shapes = split_shapes(count, n, r, C_MID)
    return pl.pallas_call(
        functools.partial(first_more_kernel, bit, first_block),
        in_specs=[SMEM, IN_VMEM, IN_VMEM],
        out_specs=[IN_VMEM] * len(shapes),
        out_shape=shapes,
        scratch_shapes=[pltpu.VMEM(part_shape(n, r) + (C_MID,), F32)],
        compiler_params=room(8),
        cost_estimate=cost(1, 1),
        name="first_grad_more",
    )(me, x, dy)


def adamw(weight, grad, first, second, rate):
    first = 0.9 * first + 0.1 * grad
    second = 0.999 * second + 0.001 * grad * grad
    normal_step = first / (1.0 - 0.9**STEP) / (jnp.sqrt(second / (1.0 - 0.999**STEP)) + 1e-08)
    return (-rate * (normal_step + 0.01 * weight), first, second)


def outer_step(start, step_sum, momentum, groups):
    delta = -(step_sum / groups)
    momentum = 0.9 * momentum + delta
    return (start - 0.7 * (delta + 0.9 * momentum), momentum)


def rep_sum(x):
    for bit in bits_of("rep"):
        low = x.astype(BF)
        x = low.astype(F32) + swap(low, "rep", bit).astype(F32)
    return x


def finish_kernel(n_parts, at, before, *refs):
    parts, state, refs = refs[:n_parts], refs[n_parts : n_parts + 5], refs[n_parts + 5 + before :]
    outs, (low, *refs) = refs[:3], refs[3:]
    bufs, sems = refs[:3], refs[3:]

    def body(i):
        if n_parts == 2:
            keep, got = parts
            r = keep.shape[2]
            owned = keep[i, 0] + value_of(got[i, :r, :], got[i, r : r + EXTRA, :][0:1])
        else:
            owned = parts[0][i]
        weight, mask, rank = (ref[at + i] for ref in state[:3])
        first, second = (ref[0, at + i] for ref in state[3:])
        bufs[2][i] = mask_of(mask, rank)
        old, new = masks(mask, rank)
        effective = weight * old
        kept = old * new
        dense = owned + 5e-05 * effective
        step, m, v = adamw(weight * kept, new * dense, first * kept, second * kept, 0.03)
        bufs[0][i] = m * new
        bufs[1][i] = v * new
        low[i] = (step * new).astype(BF)

    here = lambda ref: lambda i: ref.at[at + i]
    here_rep = lambda ref: lambda i: ref.at[0, at + i]
    wheres = (here_rep, here_rep, here)
    by_blocks(low.shape[0], [(f(ref), *two) for f, ref, *two in zip(wheres, outs, bufs, sems)], body)


def mask_of(old, rank):
    return jnp.where(rank < DROP_CUT, 0, jnp.where(rank >= GROW_CUT, 1, old))


def masks(old, rank):
    return old.astype(F32), mask_of(old, rank).astype(F32)


def finish(parts, state, before, at, count):
    shard, w = state[0].shape[1:]
    own = lambda t: pltpu.VMEM((count, shard, w), t)
    n_in = len(parts) + 5
    return pl.pallas_call(
        functools.partial(finish_kernel, len(parts), at, len(before)),
        in_specs=[IN_VMEM] * n_in + [ANY] * len(before),
        out_specs=[ANY, ANY, ANY, IN_VMEM],
        out_shape=[
            jax.ShapeDtypeStruct(state[3].shape, F32), jax.ShapeDtypeStruct(state[4].shape, F32),
            jax.ShapeDtypeStruct(state[1].shape, I32),
            jax.ShapeDtypeStruct((count, shard, w), BF),
        ],
        input_output_aliases={n_in + k: k for k in range(len(before))},
        scratch_shapes=[own(F32), own(F32), own(I32)] + [dma(count)] * 3,
        compiler_params=room(12),
        cost_estimate=cost(1, 1),
        name="finish",
    )(*parts, *state, *before)


def outer_kernel(groups, at, before, low, got, *refs):
    state, refs = refs[:4], refs[4 + before :]
    outs, bufs, sems = refs[:2], refs[2:4], refs[4:]

    def body(i):
        weight, mask, rank, momentum = (ref[at + i] for ref in state)
        old, new = masks(mask, rank)
        total = low[i].astype(F32) + got[i].astype(F32)
        value, mom = outer_step(weight * (old * new), total, momentum, groups)
        bufs[0][i] = value * new
        bufs[1][i] = mom * new

    here = lambda ref: lambda i: ref.at[at + i]
    by_blocks(low.shape[0], [(here(ref), *two) for ref, *two in zip(outs, bufs, sems)], body)


def outer(low, got, state, before, at, groups):
    return pl.pallas_call(
        functools.partial(outer_kernel, groups, at, len(before)),
        in_specs=[IN_VMEM] * 6 + [ANY] * len(before),
        out_specs=[ANY, ANY],
        out_shape=[jax.ShapeDtypeStruct(state[0].shape, F32)] * 2,
        input_output_aliases={6 + k: k for k in range(len(before))},
        scratch_shapes=[pltpu.VMEM(low.shape, F32)] * 2 + [dma(low.shape[0])] * 2,
        compiler_params=room(12),
        cost_estimate=cost(1, 1),
        name="outer",
    )(low, got, *state, *before)


def per_device(
    images, labels, conv_weight, conv_mask, conv_rank, head_weight, norm_params, head_bias,
    conv_first, conv_second, head_first, head_second, norm_first, norm_second, bias_first,
    bias_second, conv_outer, head_outer, norm_outer, bias_outer,
):
    devices = lax.axis_size("dp")
    groups = lax.axis_size("rep")
    width = C_MID
    blocks = C_IN // C_MID
    core = lax.axis_index("rep") % 2
    dp = lax.axis_index("dp")
    me = jnp.stack([dp, core]).astype(I32)
    bits = bits_of("dp")
    shard = conv_weight.shape[1]
    batch = images.shape[0]
    rows = batch * PIX
    total = float(rows * devices)
    group_images = batch * devices
    half = shard // 2

    def mine(x):
        return pick(x.reshape(-1, 2, half, width), 1, core)

    def active(sl):
        return jnp.where(mine(conv_mask[sl]) == 1, mine(conv_weight[sl]), 0.0).astype(BF)

    head_wide = jnp.pad(head_weight.astype(BF), ((0, 0), (0, WIDE - CLASSES)))
    head_low = head_wide.reshape(shard, 2, width).transpose(1, 0, 2)
    get_first = Gather(active(slice(0, blocks)))
    taps_low = active(slice(blocks, None))
    get_first.spread(taps_low)
    get_first.reach()
    get_taps = Gather(after(taps_low, get_first.own))
    first_pieces, first_codes = get_first.finish()
    fine = first_codes is not None
    classes = labels.reshape(1, batch)
    x = images.transpose(1, 2, 0, 3).reshape(SIDE, SIDE * batch, C_IN)
    head_got = gather_more(head_low[None], [0], bits[0])
    first_pieces[0] = after(first_pieces[0], head_got[0])
    y_one, sums_one = first_forward(me, x, first_pieces, first_codes)
    for bit in reversed(bits[2:]):
        head_got = gather_more(*head_got, bit)
    get_taps.spread(y_one, head_got[0])
    get_taps.reach()
    for bit in bits[1:]:
        sums_one = sums_one + swap(sums_one, "dp", bit)
    head_got = gather_more(*head_got, bits[1], sums_one)
    taps_pieces, taps_codes = get_taps.finish(sums_one)
    sums_one = sums_one + swap(sums_one, "dp", bits[0])
    h_one, y_two, sums_two, taps = second_forward(
        me, y_one, sums_one, norm_params, taps_pieces, taps_codes, total
    )
    head_pieces, head_codes = [head_got[0]], [[(0, r) for r in head_got[1]]]
    if not fine:
        head_pieces, head_codes = place(head_pieces, head_codes), None
    for bit in bits:
        sums_two = sums_two + swap(sums_two, "dp", bit)
    bias_wide = jnp.pad(head_bias, (0, WIDE - CLASSES)).reshape(1, WIDE)
    *outs, packed, dpool = head_step(
        me, y_two, sums_two, norm_params, bias_wide, classes, head_pieces, head_codes, total,
        group_images, devices, shard,
    )
    packed = sum_all(packed, "dp")
    cut = 5
    n, r = devices, shard
    cross = bits[1:2] + bits[:1] + bits[2:]
    send, keep = split_of(me, outs, n, r, 1, 1)
    sum_head = Sum(me, after(send, packed), keep, bits)
    pad, turned, *outs = taps_grad_first(
        me, y_two, sums_two, packed, norm_params, dpool, h_one, total, n, r, cut
    )
    sum_a = Sum(me, *split_of(me, outs, n, r, 1, 1), bits)
    pad = after(pad, outs[0])
    dz_one, back_one = input_grad(pad, y_one, sums_one, norm_params, taps, total)
    turned = after(turned, dz_one)
    outs = taps_grad_more(me, pad, turned, n, r, cut, 9 - cut)
    back_one = sum_all(back_one, "dp", outs[0])
    send, keep = split_of(me, outs, n, r, 1, 1)
    sum_b = Sum(me, after(send, back_one), keep, bits)
    last = sum_a.turn(back_one)
    dy_one, *outs = first_grad_first(
        me, dz_one, y_one, sums_one, after(back_one, last), norm_params, x, total, n, r, 2
    )
    sum_c = Sum(me, *split_of(me, outs, n, r, 1, 1), bits)
    outs = first_grad_more(me, cross[0], x, after(dy_one, outs[0]), n, r, 2, 2)
    sum_d = Sum(me, *split_of(me, outs, n, r, cross[0], cross[0]), cross)
    state = (conv_weight, conv_mask, conv_rank, conv_first, conv_second)
    rep_bits = bits_of("rep")
    results, new = (), ()

    def close(one, at, *deps):
        one.turns()
        keep = after(one.keep, *deps)
        parts = (keep, one.got) if fine else (keep[:, 0] + decode(one.got),)
        *both, low = finish(parts, state, results, at, keep.shape[0])
        return both, low

    def to_groups(low):
        for b in rep_bits[:-1]:
            low = (low.astype(F32) + swap(low, "rep", b).astype(F32)).astype(BF)
        return low, swap(low, "rep", rep_bits[-1])

    last = sum_head.turn(outs[0])
    last = sum_a.turn(last)
    last = sum_b.turn(last)
    results, low_a = close(sum_a, blocks, last)
    last = sum_c.turn(low_a)
    low_a, got_a = to_groups(low_a)
    last = sum_d.turn(last)
    last = sum_b.turn(last, low_a)
    last = sum_d.turn(last)
    last = sum_c.turn(last)
    results, low_d = close(sum_d, 2, last, got_a)
    results, low_c = close(sum_c, 0, low_d)
    results, low_b = close(sum_b, blocks + cut, low_c)
    low_c, got_c = to_groups(jnp.concatenate([low_c, low_d], axis=0))
    low_b, got_b = to_groups(low_b)
    back_one, packed = after((back_one, packed), last)
    bias_grad = packed[2:].reshape(-1)[:CLASSES]
    loss_sum = packed[3, C_MID - 1 :]
    sum_head.turns(last)
    head_grad = sum_head.keep[:, 0] + decode(sum_head.got)
    head_grad = head_grad.transpose(1, 0, 2).reshape(shard, WIDE)[:, :CLASSES]
    for low, got, at in ((low_a, got_a, blocks), (low_c, got_c, 0), (low_b, got_b, blocks + cut)):
        new = outer(low, got, state[:3] + (conv_outer,), new, at, groups)
    (conv_m, conv_v, mask_int), (conv_new, conv_mom) = results, new
    norm_grad = jnp.concatenate([back_one, packed[:2]], axis=0)
    head_s, head_m, head_v = adamw(head_weight, head_grad, head_first[0], head_second[0], 0.03)
    head_new, head_mom = outer_step(head_weight, rep_sum(head_s), head_outer, groups)
    norm_s, norm_m, norm_v = adamw(norm_params, norm_grad, norm_first[0], norm_second[0], 0.3)
    bias_s, bias_m, bias_v = adamw(head_bias, bias_grad, bias_first[0], bias_second[0], 0.3)
    wide = jnp.pad(bias_s, (0, WIDE - CLASSES)).reshape(2, width)
    small = jnp.pad(norm_s, ((0, 2), (0, 0))) + jnp.pad(wide, ((4, 0), (0, 0)))
    small = sum_all(small, "rep")
    norm_new, norm_mom = outer_step(norm_params, small[:4], norm_outer, groups)
    bias_new, bias_mom = outer_step(head_bias, small[4:].reshape(-1)[:CLASSES], bias_outer, groups)
    return (
        conv_new, mask_int, conv_m, conv_v, conv_mom,
        head_new, head_m[None], head_v[None], head_mom,
        norm_new, norm_m[None], norm_v[None], norm_mom,
        bias_new, bias_m[None], bias_v[None], bias_mom, loss_sum,
    )
def solution(mesh):
    conv = P(None, "dp", None)
    conv_rep = P("rep", None, "dp", None)
    head = P("dp", None)
    head_rep = P("rep", "dp", None)
    in_specs = (
        P(("rep", "dp"), None, None, None), P(("rep", "dp")), conv, conv, conv, head, P(), P(),
        conv_rep, conv_rep, head_rep, head_rep, P("rep", None, None), P("rep", None, None),
        P("rep", None), P("rep", None), conv, head, P(), P(),
    )
    out_specs = (
        conv, conv, conv_rep, conv_rep, conv, head, head_rep, head_rep, head,
        P(), P("rep", None, None), P("rep", None, None), P(),
        P(), P("rep", None), P("rep", None), P(), P("rep"),
    )
    return jax.shard_map(
        per_device, mesh=mesh, in_specs=in_specs, out_specs=out_specs, check_vma=False
    )
```

```python
import functools

import jax
import jax.numpy as jnp
from jax import lax
from jax.experimental import pallas as pl
from jax.experimental.pallas import tpu as pltpu
from jax.sharding import PartitionSpec as P

C_IN = 2048
C_MID = 512
CLASSES = 1000
WIDE = 1024
SIDE = 7
STEP = 10
PIX = 49
DROP_CUT = 78643
GROW_CUT = 242484
BF = jnp.bfloat16
F32 = jnp.float32
I32 = jnp.int32
I16 = jnp.int16
EXTRA = 16
LEVELS = 32000.0
LOG2E = 1.4426950408889634


def swap(x, axis, bit):
    n = lax.axis_size(axis)
    return lax.ppermute(x, axis, [(i, i ^ bit) for i in range(n)])


def bits_of(axis):
    n = lax.axis_size(axis)
    return [1 << k for k in range(n.bit_length() - 1)]


def sum_all(x, axis, *deps):
    bits = bits_of(axis)
    bits = bits[1:] + bits[:1]
    for bit in bits:
        if deps and bit == bits[-1]:
            x = after(x, *deps)
        x = x + swap(x, axis, bit)
    return x


def room(mib):
    return pltpu.CompilerParams(vmem_limit_bytes=mib * 1024 * 1024)


def pick(x, axis, index):
    return lax.dynamic_index_in_dim(x, index, axis, keepdims=False)


def gather_more(buf, rel, bit, *deps):
    buf = after(buf, *deps) if deps else buf
    return jnp.concatenate([buf, swap(buf, "dp", bit)], axis=0), rel + [r ^ bit for r in rel]


class Gather:
    def __init__(self, own):
        self.own, self.rel = own[None], [0]
        self.got = None

    def start(self):
        for bit in reversed(bits_of("dp")[2:]):
            self.join()
            self.got = swap(self.own, "dp", bit)
            self.rel = self.rel + [r ^ bit for r in self.rel]
        return self

    def join(self, *deps):
        if self.got is not None:
            got = after(self.got, *deps) if deps else self.got
            self.own, self.got = jnp.concatenate([self.own, got], axis=0), None

    def turn_near(self, *deps):
        self.join()
        own = after(self.own, *deps) if deps else self.own
        self.near = swap(own, "dp", bits_of("dp")[1])

    def turn_side(self, *deps):
        own = after(self.own, *deps) if deps else self.own
        self.side = swap(own, "dp", bits_of("dp")[0])

    def turn_far(self, *deps):
        near = after(self.near, *deps) if deps else self.near
        self.far = swap(near, "dp", bits_of("dp")[0])

    def finish(self, *deps):
        bits = bits_of("dp")
        far = after(self.far, *deps) if deps else self.far
        pieces = [self.own, self.near, self.side, far]
        shifts = [0, bits[1], bits[0], bits[1] | bits[0]]
        codes = [[(0, r ^ s) for r in self.rel] for s in shifts]
        pieces += [swap(p, "rep", 1) for p in pieces]
        codes += [[(1, r) for _, r in c] for c in codes]
        if self.own.shape[2] % 16:
            return place(pieces, codes), None
        return pieces, codes


def place(pieces, codes):
    n = lax.axis_size("dp")
    flat = [c * n + r for code in codes for c, r in code]
    cores = len(flat) // n
    inverse = jnp.array([flat.index(k) for k in range(len(flat))], I32)
    me = (lax.axis_index("rep") % cores) * n + lax.axis_index("dp")
    where = inverse[jnp.arange(len(flat), dtype=I32) ^ me]
    full = jnp.take(jnp.concatenate(pieces, axis=0), where, axis=0)
    _, blocks, r, w = full.shape
    full = full.reshape(cores, n, blocks, r, w).transpose(2, 1, 0, 3, 4)
    return [full.reshape(1, blocks, n * cores * r, w)]


def fetch(src, dst, sem):
    copy = pltpu.make_async_copy(src, dst, sem)
    copy.start()
    return copy


def wait_all(copies):
    for copy in copies:
        copy.wait()


def entries(pieces):
    return sum(p.shape[0] for p in pieces)


def fetch_pieces(refs, codes, me, out, sems):
    copies = []
    for p, ref in enumerate(refs):
        r = ref.shape[2]
        for i in range(ref.shape[0]):
            if codes is None:
                row = 0
            else:
                c, s = codes[p][i]
                row = me[0] ^ s
                if any(c for code in codes for c, _ in code):
                    row = row * 2 + (me[1] ^ c)
                row = pl.multiple_of(row * r, 16)
            copies.append(fetch(ref.at[i], out.at[:, pl.ds(row, r), :], sems.at[len(copies)]))
    return copies


def by_blocks(count, outs, body):
    done = []
    for i in range(count):
        body(i)
        done += [fetch(buf.at[i], at(i), sems.at[i]) for at, buf, sems in outs]
    wait_all(done)


def dma(n):
    return pltpu.SemaphoreType.DMA((n,))


ANY = pl.BlockSpec(memory_space=pl.ANY)
IN_VMEM = pl.BlockSpec(memory_space=pltpu.VMEM)


SMEM = pl.BlockSpec(memory_space=pltpu.SMEM)

def cost(flops, byte_count):
    return pl.CostEstimate(flops=1, bytes_accessed=1, transcendentals=0)


def code_scale(k):
    return jnp.exp2(k * (1.0 / 16.0))


def code_step(top):
    return jnp.minimum(jnp.ceil(jnp.log2(jnp.maximum(top, 1e-30)) * 16.0), 2032.0)


def code_of(x, k):
    return jnp.floor(x * (LEVELS / code_scale(k)) + 0.5).astype(I32).astype(I16)


def value_of(q, k):
    return q.astype(I32).astype(F32) * (code_scale(k) * (1.0 / LEVELS))


def encode(x):
    k = code_step(jnp.max(jnp.abs(x), axis=1, keepdims=True))
    tail = jnp.pad(k[:, 0], ((0, EXTRA - x.shape[0]), (0, 0))).astype(I32).astype(I16)
    return jnp.concatenate([code_of(x, k).reshape(-1, x.shape[2]), tail], axis=0)


def decode(payload, blocks):
    q = payload[:-EXTRA].reshape(blocks, -1, payload.shape[1])
    return value_of(q, payload[-EXTRA:][:blocks, None, :].astype(F32))


def split_plain(full, bit, stride=1):
    b, n, r, w = full.shape
    view = full.reshape(b, n // (2 * stride), 2, stride, r, w)
    keep = pick(view, 2, bit).reshape(b, n // 2, r, w)
    return encode(pick(view, 2, 1 - bit).reshape(b, n // 2 * r, w)), keep


def side_of(me, bit):
    return (me[0] // bit) % 2


def put_split(block, bit, stride, send_ref, keep_ref, at):
    n, r, w = block.shape
    top = jnp.zeros((1, w), F32)
    base = [j // stride * 2 * stride + j % stride for j in range(n // 2)]
    for j in range(n // 2):
        keep_ref[at, j] = block[base[j] + stride * bit]
        top = jnp.maximum(
            top, jnp.max(jnp.abs(block[base[j] + stride * (1 - bit)]), axis=0, keepdims=True)
        )
    k = code_step(top)
    for j in range(n // 2):
        row = (at * (n // 2) + j) * r
        send_ref[row : row + r, :] = code_of(block[base[j] + stride * (1 - bit)], k)
    return k


def put_scales(send_ref, scales):
    w = send_ref.shape[1]
    row = lax.broadcasted_iota(I32, (EXTRA, w), 0)
    tail = jnp.zeros((EXTRA, w), F32)
    for i, k in enumerate(scales):
        tail = jnp.where(row == i, k, tail)
    send_ref[send_ref.shape[0] - EXTRA :, :] = tail.astype(I32).astype(I16)


def scales_of(got):
    return got[got.shape[0] - EXTRA :, :].astype(I32).astype(F32)


def part_shape(n, r):
    return (n, r) if r % 16 == 0 else (1, n * r)


def split_of(me, outs, n, r, bit, stride):
    if len(outs) == 2:
        return outs
    full = outs[0]
    return split_plain(full.reshape(full.shape[0], n, r, full.shape[-1]), side_of(me, bit), stride)


def split_shapes(blocks, n, r, w):
    if r % 16:
        return [jax.ShapeDtypeStruct((blocks, 1, n * r, w), F32)]
    return [
        jax.ShapeDtypeStruct((blocks * (n // 2) * r + EXTRA, w), I16),
        jax.ShapeDtypeStruct((blocks, n // 2, r, w), F32),
    ]


def add_split_kernel(bit, stride, me, keep_in, got, send, keep, total):
    n, r = keep_in.shape[1:3]
    given, scales = scales_of(got), []
    for i in range(keep_in.shape[0]):
        for j in range(n):
            row = (i * n + j) * r
            total[j] = keep_in[i, j] + value_of(got[row : row + r, :], given[i : i + 1])
        scales.append(put_split(total, side_of(me, bit), stride, send, keep, i))
    put_scales(send, scales)


def add_split(me, keep, got, bit, stride):
    b, n, r, w = keep.shape
    if r % 16:
        return split_plain(keep + decode(got, b).reshape(keep.shape), side_of(me, bit), stride)
    return pl.pallas_call(
        functools.partial(add_split_kernel, bit, stride),
        in_specs=[SMEM, IN_VMEM, IN_VMEM],
        out_specs=[IN_VMEM, IN_VMEM],
        out_shape=split_shapes(b, n, r, w),
        scratch_shapes=[pltpu.VMEM((n, r, w), F32)],
        compiler_params=room(8),
        cost_estimate=cost(1, 1),
        name="add_split",
    )(me, keep, got)


def after(x, *deps):
    return lax.optimization_barrier((x, deps))[0]


class Sum:
    def __init__(self, me, send, keep, bits):
        self.me = me
        self.send, self.keep, self.bits, self.done = send, keep, list(bits), []
        self.got = swap(send, "dp", self.bits[0])

    def turn(self, *deps):
        self.done.append(self.bits.pop(0))
        nxt = self.bits[0]
        stride = nxt
        for used in self.done:
            stride = stride // 2 if used < nxt else stride
        got = after(self.got, *deps) if deps else self.got
        self.send, self.keep = add_split(self.me, self.keep, got, nxt, stride)
        self.got = swap(self.send, "dp", nxt)
        return self.keep

    def turns(self, *deps):
        while len(self.bits) > 1:
            deps = (self.turn(*deps),)
        return deps


def norm_rows(sums, gain, shift, total):
    mean = sums[0:1] * (1.0 / total)
    var = sums[1:2] * (1.0 / total) - mean * mean
    rstd = lax.rsqrt(var + 1e-05)
    factor = gain * rstd
    return mean, rstd, factor, shift - mean * factor


def inverse(d):
    r = pl.reciprocal(d, approx=True)
    return r * (2.0 - d * r)


def gate(y, factor, offset):
    z = y * factor + offset
    power = jnp.minimum(y * (factor * -LOG2E) + offset * -LOG2E, 100.0)
    return z, inverse(1.0 + jnp.exp2(power))


def slope_of(z, sig):
    return sig * (1.0 + (z - z * sig))


def back_rows(back, rstd, mean, factor, total):
    d = -(factor * rstd) * (back[0:1] * (1.0 / total))
    return d, -factor * (back[1:2] * (1.0 / total)) - mean * d


def flat(x):
    return x.reshape(-1, x.shape[-1])


def add_sums(sums, one, two):
    sums[0:1] += jnp.sum(one, axis=0, keepdims=True)
    sums[1:2] += jnp.sum(two, axis=0, keepdims=True)


def first_kernel(codes, count, me, x, *refs):
    pieces, (y, sums, weights, p_sem) = refs[:count], refs[count:]
    copies = fetch_pieces(pieces, codes, me, weights, p_sem)
    sums[...] = jnp.zeros_like(sums)
    wait_all(copies)
    for k in range(SIDE):
        out = jnp.dot(x[k], weights[...].reshape(-1, C_MID), preferred_element_type=F32)
        y[k] = out
        add_sums(sums, out, out * out)


def first_forward(me, x, pieces, codes):
    rows = x.shape[1]
    return pl.pallas_call(
        functools.partial(first_kernel, codes, len(pieces)),
        in_specs=[SMEM, IN_VMEM] + [ANY] * len(pieces),
        out_specs=[IN_VMEM, IN_VMEM],
        out_shape=[
            jax.ShapeDtypeStruct((SIDE, rows, C_MID), F32), jax.ShapeDtypeStruct((2, C_MID), F32),
        ],
        scratch_shapes=[
            pltpu.VMEM((C_IN // C_MID, C_MID, C_MID), BF), dma(entries(pieces)),
        ],
        compiler_params=room(8),
        cost_estimate=cost(1, 1),
        name="first_forward",
    )(me, x, *pieces)


def clear_border(pad):
    zero = jnp.zeros(pad.shape[1:], pad.dtype)
    pad[0] = zero
    pad[SIDE + 1] = zero
    for k in range(1, SIDE + 1):
        pad[k, 0] = zero[0]
        pad[k, SIDE + 1] = zero[0]


def second_kernel(codes, count, total, me, y1, sums1, params, *refs):
    pieces, (h1, y2, sums2, taps, pad, p_sem) = refs[:count], refs[count:]
    batch = pad.shape[2]
    copies = fetch_pieces(pieces, codes, me, taps, p_sem)
    clear_border(pad)
    sums2[...] = jnp.zeros_like(sums2)
    _, _, factor, offset = norm_rows(sums1[...], params[0:1], params[1:2], total)

    def act(k):
        z, sig = gate(y1[k], factor, offset)
        h = (z * sig).astype(BF).reshape(SIDE, batch, C_MID)
        pad[k + 1, 1 : SIDE + 1] = h
        h1[k] = h

    act(0)
    act(1)
    wait_all(copies)
    for k in range(SIDE):
        out = None
        for a in range(3):
            if 0 <= k + a - 1 < SIDE:
                patch = jnp.concatenate([flat(pad[k + a, b : b + SIDE]) for b in range(3)], axis=1)
                part = jnp.dot(
                    patch, taps[3 * a : 3 * a + 3].reshape(3 * C_MID, C_MID),
                    preferred_element_type=F32,
                )
                out = part if out is None else out + part
        if k + 2 < SIDE:
            act(k + 2)
        y2[k] = out
        add_sums(sums2, out, out * out)


def second_forward(me, y1, sums1, params, pieces, codes, total):
    rows = y1.shape[1]
    batch = rows // SIDE
    return pl.pallas_call(
        functools.partial(second_kernel, codes, len(pieces), total),
        in_specs=[SMEM, IN_VMEM, IN_VMEM, IN_VMEM] + [ANY] * len(pieces),
        out_specs=[IN_VMEM] * 4,
        out_shape=[
            jax.ShapeDtypeStruct((SIDE, SIDE, batch, C_MID), BF),
            jax.ShapeDtypeStruct(y1.shape, F32),
            jax.ShapeDtypeStruct((2, C_MID), F32),
            jax.ShapeDtypeStruct((9, C_MID, C_MID), BF),
        ],
        scratch_shapes=[
            pltpu.VMEM((SIDE + 2, SIDE + 2, batch, C_MID), BF), dma(entries(pieces)),
        ],
        compiler_params=room(12),
        cost_estimate=cost(1, 1),
        name="second_forward",
    )(me, y1, sums1, params, *pieces)


def head_kernel(codes, count, outs_n, total, group_images, me, y2, sums2, params, bias, labels, *refs):
    pieces, refs = refs[:count], refs[count:]
    outs, (packed, dpool_out, head, block, p_sem) = refs[:outs_n], refs[outs_n:]
    batch = dpool_out.shape[0]
    copies = fetch_pieces(pieces, codes, me, head, p_sem)
    mean, rstd, factor, offset = norm_rows(sums2[...], params[2:3], params[3:4], total)
    sum_h = sum_a = sum_b = jnp.zeros((batch, C_MID), F32)
    fold = lambda v: jnp.sum(v.reshape(SIDE, batch, C_MID), axis=0)
    for k in range(SIDE):
        z, sig = gate(y2[k], factor, offset)
        slope = slope_of(z, sig)
        sum_h = sum_h + fold(z * sig)
        sum_a = sum_a + fold(slope)
        sum_b = sum_b + fold(slope * ((y2[k] - mean) * rstd))
    wait_all(copies)
    pooled = (sum_h * (1.0 / PIX)).astype(BF)
    logits = jnp.concatenate(
        [jnp.dot(pooled, head[k], preferred_element_type=F32) for k in range(2)], axis=1
    )
    logits = logits + bias[...]
    column = lax.broadcasted_iota(I32, (batch, WIDE), 1)
    logits = jnp.where(column < CLASSES, logits, -1e30)
    across = lax.broadcasted_iota(I32, (batch, batch), 0) == lax.broadcasted_iota(I32, (batch, batch), 1)
    label = jnp.sum(jnp.where(across, labels[...], 0), axis=1, keepdims=True)
    onehot = (label == column).astype(F32)
    top = jnp.max(logits, axis=1, keepdims=True)
    expo = jnp.exp(logits - top)
    expsum = jnp.sum(expo, axis=1, keepdims=True)
    lse = top + jnp.log(expsum)
    loss = jnp.sum(lse - jnp.sum(logits * onehot, axis=1, keepdims=True), axis=0, keepdims=True)
    dlogits = ((jnp.exp(logits - lse) - onehot) * (1.0 / group_images)).astype(BF)
    bias_sum = jnp.sum(dlogits.astype(F32), axis=0, keepdims=True)
    last = lax.broadcasted_iota(I32, (1, WIDE), 1) == WIDE - 1
    bias_sum = jnp.where(last, loss, bias_sum)
    dpool = jnp.zeros((batch, C_MID), F32)
    for k in range(2):
        part = dlogits[:, k * C_MID : (k + 1) * C_MID]
        dpool = dpool + lax.dot_general(
            part, head[k], (((1,), (1,)), ((), ())), preferred_element_type=F32
        )

    def make(k):
        block[...] = lax.dot_general(
            pooled, dlogits[:, k * C_MID : (k + 1) * C_MID], (((0,), (0,)), ((), ())),
            preferred_element_type=F32,
        ).reshape(block.shape)

    emit_all(2, make, block, me, 1, outs)
    dpool = dpool * (1.0 / PIX)
    dpool_out[...] = dpool
    packed[0:1] = jnp.sum(dpool * sum_b, axis=0, keepdims=True)
    packed[1:2] = jnp.sum(dpool * sum_a, axis=0, keepdims=True)
    packed[2:3] = bias_sum[:, :C_MID]
    packed[3:4] = bias_sum[:, C_MID:]


def head_step(me, y2, sums2, params, bias, labels, pieces, codes, total, group_images, n, r):
    rows = y2.shape[1]
    batch = rows // SIDE
    shapes = split_shapes(2, n, r, C_MID)
    return pl.pallas_call(
        functools.partial(head_kernel, codes, len(pieces), len(shapes), total, group_images),
        in_specs=[SMEM] + [IN_VMEM] * 5 + [ANY] * len(pieces),
        out_specs=[IN_VMEM] * (2 + len(shapes)),
        out_shape=shapes + [
            jax.ShapeDtypeStruct((4, C_MID), F32), jax.ShapeDtypeStruct((batch, C_MID), F32),
        ],
        scratch_shapes=[
            pltpu.VMEM((2, C_MID, C_MID), BF), pltpu.VMEM(part_shape(n, r) + (C_MID,), F32),
            dma(entries(pieces)),
        ],
        compiler_params=room(8),
        cost_estimate=cost(1, 1),
        name="head_step",
    )(me, y2, sums2, params, bias, labels, *pieces)


def emit_all(count, make, block, me, bit, outs):
    scales = []
    for i in range(count):
        make(i)
        if len(outs) == 1:
            outs[0][i] = block[...]
        else:
            scales.append(put_split(block, side_of(me, bit), bit, *outs, i))
    if scales:
        put_scales(outs[0], scales)


def one_tap(tap, pad, turned, block):
    a, b = tap // 3, tap % 3
    moved = pad[2 - a : 2 - a + SIDE, 2 - b : 2 - b + SIDE].reshape(-1, C_MID)
    block[...] = jnp.dot(turned[...], moved, preferred_element_type=F32).reshape(block.shape)


def taps_kernel(total, me, y2, sums2, back, params, dpool, h1, pad, turned, *refs):
    outs, block = refs[:-1], refs[-1]
    batch = pad.shape[2]
    clear_border(pad)
    mean, rstd, factor, offset = norm_rows(sums2[...], params[2:3], params[3:4], total)
    d, e = back_rows(back, rstd, mean, factor, total)
    scaled = (dpool[...] * factor)[None]
    turned[...] = h1[...].reshape(-1, C_MID).T
    for k in range(SIDE):
        z, sig = gate(y2[k], factor, offset)
        dz = flat(slope_of(z, sig).reshape(SIDE, batch, C_MID) * scaled)
        dy = dz + (y2[k] * d + e)
        pad[k + 1, 1 : SIDE + 1] = dy.astype(BF).reshape(SIDE, batch, C_MID)
    emit_all(outs[-1].shape[0], lambda i: one_tap(i, pad, turned, block), block, me, 1, outs)


def taps_more_kernel(first_tap, me, pad, turned, *refs):
    outs, block = refs[:-1], refs[-1]
    make = lambda i: one_tap(i + first_tap, pad, turned, block)
    emit_all(outs[-1].shape[0], make, block, me, 1, outs)


def taps_grad_first(me, y2, sums2, back, params, dpool, h1, total, n, r, count):
    batch = h1.shape[2]
    shapes = split_shapes(count, n, r, C_MID)
    return pl.pallas_call(
        functools.partial(taps_kernel, total),
        in_specs=[SMEM] + [IN_VMEM] * 6,
        out_specs=[IN_VMEM] * (2 + len(shapes)),
        out_shape=[
            jax.ShapeDtypeStruct((SIDE + 2, SIDE + 2, batch, C_MID), BF),
            jax.ShapeDtypeStruct((C_MID, SIDE * SIDE * batch), BF),
        ] + shapes,
        scratch_shapes=[pltpu.VMEM(part_shape(n, r) + (C_MID,), F32)],
        compiler_params=room(8),
        cost_estimate=cost(1, 1),
        name="taps_grad_first",
    )(me, y2, sums2, back, params, dpool, h1)


def taps_grad_more(me, pad, turned, n, r, first_tap, count):
    shapes = split_shapes(count, n, r, C_MID)
    return pl.pallas_call(
        functools.partial(taps_more_kernel, first_tap),
        in_specs=[SMEM, IN_VMEM, IN_VMEM],
        out_specs=[IN_VMEM] * len(shapes),
        out_shape=shapes,
        scratch_shapes=[pltpu.VMEM(part_shape(n, r) + (C_MID,), F32)],
        compiler_params=room(8),
        cost_estimate=cost(1, 1),
        name="taps_grad_more",
    )(me, pad, turned)


def input_grad_kernel(total, pad, y1, sums1, params, taps, dz1, sums):
    sums[...] = jnp.zeros_like(sums)
    mean, rstd, factor, offset = norm_rows(sums1[...], params[0:1], params[1:2], total)
    for k in range(SIDE):
        dh = None
        for a in range(3):
            for b in range(3):
                if 0 <= k + 1 - a < SIDE:
                    part = lax.dot_general(
                        flat(pad[k + 2 - a, 2 - b : 2 - b + SIDE]), taps[3 * a + b],
                        (((1,), (1,)), ((), ())), preferred_element_type=F32,
                    )
                    dh = part if dh is None else dh + part
        dz = dh * slope_of(*gate(y1[k], factor, offset))
        dz1[k] = dz
        add_sums(sums, dz * ((y1[k] - mean) * rstd), dz)


def input_grad(pad, y1, sums1, params, taps, total):
    return pl.pallas_call(
        functools.partial(input_grad_kernel, total),
        in_specs=[IN_VMEM] * 5,
        out_specs=[IN_VMEM] * 2,
        out_shape=[jax.ShapeDtypeStruct(y1.shape, F32), jax.ShapeDtypeStruct((2, C_MID), F32)],
        compiler_params=room(8),
        cost_estimate=cost(1, 1),
        name="input_grad",
    )(pad, y1, sums1, params, taps)


def one_first(x, dy, at, block):
    block[...] = lax.dot_general(
        flat(x[:, :, at * C_MID : (at + 1) * C_MID]), flat(dy[...]), (((0,), (0,)), ((), ())),
        preferred_element_type=F32,
    ).reshape(block.shape)


def first_grad_kernel(total, me, dz1, y1, sums1, back, params, x, dy, *refs):
    outs, block = refs[:-1], refs[-1]
    mean, rstd, factor, _ = norm_rows(sums1[...], params[0:1], params[1:2], total)
    d, e = back_rows(back, rstd, mean, factor, total)
    for k in range(SIDE):
        dy[k] = (dz1[k] * factor + (y1[k] * d + e)).astype(BF)
    emit_all(outs[-1].shape[0], lambda i: one_first(x, dy, i, block), block, me, 1, outs)


def first_more_kernel(bit, first, me, x, dy, *refs):
    outs, block = refs[:-1], refs[-1]
    make = lambda i: one_first(x, dy, first + i, block)
    emit_all(outs[-1].shape[0], make, block, me, bit, outs)


def first_grad_first(me, dz1, y1, sums1, back, params, x, total, n, r, count):
    shapes = split_shapes(count, n, r, C_MID)
    return pl.pallas_call(
        functools.partial(first_grad_kernel, total),
        in_specs=[SMEM] + [IN_VMEM] * 6,
        out_specs=[IN_VMEM] * (1 + len(shapes)),
        out_shape=[jax.ShapeDtypeStruct(y1.shape, BF)] + shapes,
        scratch_shapes=[pltpu.VMEM(part_shape(n, r) + (C_MID,), F32)],
        compiler_params=room(8),
        cost_estimate=cost(1, 1),
        name="first_grad_first",
    )(me, dz1, y1, sums1, back, params, x)


def first_grad_more(me, bit, x, dy, n, r, first_block, count):
    shapes = split_shapes(count, n, r, C_MID)
    return pl.pallas_call(
        functools.partial(first_more_kernel, bit, first_block),
        in_specs=[SMEM, IN_VMEM, IN_VMEM],
        out_specs=[IN_VMEM] * len(shapes),
        out_shape=shapes,
        scratch_shapes=[pltpu.VMEM(part_shape(n, r) + (C_MID,), F32)],
        compiler_params=room(8),
        cost_estimate=cost(1, 1),
        name="first_grad_more",
    )(me, x, dy)


def adamw(weight, grad, first, second, rate):
    first = 0.9 * first + 0.1 * grad
    second = 0.999 * second + 0.001 * grad * grad
    normal_step = first / (1.0 - 0.9**STEP) / (jnp.sqrt(second / (1.0 - 0.999**STEP)) + 1e-08)
    return (-rate * (normal_step + 0.01 * weight), first, second)


def outer_step(start, step_sum, momentum, groups):
    delta = -(step_sum / groups)
    momentum = 0.9 * momentum + delta
    return (start - 0.7 * (delta + 0.9 * momentum), momentum)


def rep_sum(x):
    for bit in bits_of("rep"):
        low = x.astype(BF)
        x = low.astype(F32) + swap(low, "rep", bit).astype(F32)
    return x


def finish_kernel(n_parts, at, before, *refs):
    parts, state, refs = refs[:n_parts], refs[n_parts : n_parts + 5], refs[n_parts + 5 + before :]
    outs, (low, *refs) = refs[:3], refs[3:]
    bufs, sems = refs[:3], refs[3:]
    given = scales_of(parts[1]) if n_parts == 2 else None

    def body(i):
        if n_parts == 2:
            keep, got = parts
            r = keep.shape[2]
            owned = keep[i, 0] + value_of(got[i * r : (i + 1) * r, :], given[i : i + 1])
        else:
            owned = parts[0][i]
        weight, mask, rank = (ref[at + i] for ref in state[:3])
        first, second = (ref[0, at + i] for ref in state[3:])
        bufs[2][i] = mask_of(mask, rank)
        old, new = masks(mask, rank)
        effective = weight * old
        kept = old * new
        dense = owned + 5e-05 * effective
        step, m, v = adamw(weight * kept, new * dense, first * kept, second * kept, 0.03)
        bufs[0][i] = m * new
        bufs[1][i] = v * new
        low[i] = (step * new).astype(BF)

    here = lambda ref: lambda i: ref.at[at + i]
    here_rep = lambda ref: lambda i: ref.at[0, at + i]
    wheres = (here_rep, here_rep, here)
    by_blocks(low.shape[0], [(f(ref), *two) for f, ref, *two in zip(wheres, outs, bufs, sems)], body)


def mask_of(old, rank):
    return jnp.where(rank < DROP_CUT, 0, jnp.where(rank >= GROW_CUT, 1, old))


def masks(old, rank):
    return old.astype(F32), mask_of(old, rank).astype(F32)


def finish(parts, state, before, at, count):
    shard, w = state[0].shape[1:]
    own = lambda t: pltpu.VMEM((count, shard, w), t)
    n_in = len(parts) + 5
    return pl.pallas_call(
        functools.partial(finish_kernel, len(parts), at, len(before)),
        in_specs=[IN_VMEM] * n_in + [ANY] * len(before),
        out_specs=[ANY, ANY, ANY, IN_VMEM],
        out_shape=[
            jax.ShapeDtypeStruct(state[3].shape, F32), jax.ShapeDtypeStruct(state[4].shape, F32),
            jax.ShapeDtypeStruct(state[1].shape, I32),
            jax.ShapeDtypeStruct((count, shard, w), BF),
        ],
        input_output_aliases={n_in + k: k for k in range(len(before))},
        scratch_shapes=[own(F32), own(F32), own(I32)] + [dma(count)] * 3,
        compiler_params=room(12),
        cost_estimate=cost(1, 1),
        name="finish",
    )(*parts, *state, *before)


def outer_kernel(groups, at, before, low, got, *refs):
    state, refs = refs[:4], refs[4 + before :]
    outs, bufs, sems = refs[:2], refs[2:4], refs[4:]

    def body(i):
        weight, mask, rank, momentum = (ref[at + i] for ref in state)
        old, new = masks(mask, rank)
        total = low[i].astype(F32) + got[i].astype(F32)
        value, mom = outer_step(weight * (old * new), total, momentum, groups)
        bufs[0][i] = value * new
        bufs[1][i] = mom * new

    here = lambda ref: lambda i: ref.at[at + i]
    by_blocks(low.shape[0], [(here(ref), *two) for ref, *two in zip(outs, bufs, sems)], body)


def outer(low, got, state, before, at, groups):
    return pl.pallas_call(
        functools.partial(outer_kernel, groups, at, len(before)),
        in_specs=[IN_VMEM] * 6 + [ANY] * len(before),
        out_specs=[ANY, ANY],
        out_shape=[jax.ShapeDtypeStruct(state[0].shape, F32)] * 2,
        input_output_aliases={6 + k: k for k in range(len(before))},
        scratch_shapes=[pltpu.VMEM(low.shape, F32)] * 2 + [dma(low.shape[0])] * 2,
        compiler_params=room(12),
        cost_estimate=cost(1, 1),
        name="outer",
    )(low, got, *state, *before)


def per_device(
    images, labels, conv_weight, conv_mask, conv_rank, head_weight, norm_params, head_bias,
    conv_first, conv_second, head_first, head_second, norm_first, norm_second, bias_first,
    bias_second, conv_outer, head_outer, norm_outer, bias_outer,
):
    devices = lax.axis_size("dp")
    groups = lax.axis_size("rep")
    width = C_MID
    blocks = C_IN // C_MID
    core = lax.axis_index("rep") % 2
    dp = lax.axis_index("dp")
    me = jnp.stack([dp, core]).astype(I32)
    bits = bits_of("dp")
    shard = conv_weight.shape[1]
    batch = images.shape[0]
    rows = batch * PIX
    total = float(rows * devices)
    group_images = batch * devices
    half = shard // 2

    def mine(x):
        return pick(x.reshape(-1, 2, half, width), 1, core)

    def active(sl):
        return jnp.where(mine(conv_mask[sl]) == 1, mine(conv_weight[sl]), 0.0).astype(BF)

    head_wide = jnp.pad(head_weight.astype(BF), ((0, 0), (0, WIDE - CLASSES)))
    head_low = mine(head_wide.reshape(shard, 2, width).transpose(1, 0, 2))
    taps_low = active(slice(blocks, None))
    get_first = Gather(active(slice(0, blocks))).start()
    get_first.join()
    get_taps = Gather(after(taps_low, get_first.own)).start()
    get_first.own = after(get_first.own, taps_low)
    get_first.turn_near()
    get_first.turn_side()
    get_first.turn_far()
    first_pieces, first_codes = get_first.finish()
    fine = first_codes is not None
    classes = labels.reshape(1, batch)
    x = images.transpose(1, 2, 0, 3).reshape(SIDE, SIDE * batch, C_IN)
    y_one, sums_one = first_forward(me, x, first_pieces, first_codes)
    head_got = gather_more(after(head_low, y_one)[None], [0], bits[0])
    sums_one = sums_one + swap(sums_one, "dp", bits[0])
    get_taps.join(sums_one, head_got[0])
    get_taps.turn_near()
    get_taps.turn_side()
    get_taps.turn_far(get_taps.side)
    for bit in bits[1:]:
        sums_one = sums_one + swap(sums_one, "dp", bit)
    taps_pieces, taps_codes = get_taps.finish(sums_one)
    head_got = (after(head_got[0], get_taps.near), head_got[1])
    for bit in reversed(bits[2:]):
        head_got = gather_more(*head_got, bit)
    h_one, y_two, sums_two, taps = second_forward(
        me, after(y_one, head_got[0]), sums_one, norm_params, taps_pieces, taps_codes, total
    )
    buf, rel = head_got
    got = after(swap(buf, "dp", bits[1]), sums_two)
    buf, rel = jnp.concatenate([buf, got], axis=0), rel + [code ^ bits[1] for code in rel]
    head_pieces, head_codes = [buf, swap(buf, "rep", 1)], [[(c, r) for r in rel] for c in range(2)]
    if not fine:
        head_pieces, head_codes = place(head_pieces, head_codes), None
    for bit in bits:
        sums_two = sums_two + swap(sums_two, "dp", bit)
    bias_wide = jnp.pad(head_bias, (0, WIDE - CLASSES)).reshape(1, WIDE)
    *outs, packed, dpool = head_step(
        me, y_two, sums_two, norm_params, bias_wide, classes, head_pieces, head_codes, total,
        group_images, devices, shard,
    )
    n, r = devices, shard
    sum_head = Sum(me, *split_of(me, outs, n, r, 1, 1), bits)
    packed = sum_all(packed, "dp")
    cut = 5
    cross = bits[1:2] + bits[:1] + bits[2:]
    dpool = after(dpool, sum_head.turn(packed))
    pad, turned, *outs = taps_grad_first(
        me, y_two, sums_two, packed, norm_params, dpool, h_one, total, n, r, cut
    )
    sum_a = Sum(me, *split_of(me, outs, n, r, 1, 1), bits)
    pad = after(pad, outs[0])
    dz_one, back_one = input_grad(pad, y_one, sums_one, norm_params, taps, total)
    turned = after(turned, dz_one)
    outs = taps_grad_more(me, pad, turned, n, r, cut, 9 - cut)
    back_one = sum_all(back_one, "dp", sum_head.turn(outs[0]))
    send, keep = split_of(me, outs, n, r, 1, 1)
    sum_b = Sum(me, after(send, back_one), keep, bits)
    last = sum_a.turn(back_one)
    dy_one, *outs = first_grad_first(
        me, dz_one, y_one, sums_one, after(back_one, last), norm_params, x, total, n, r, 2
    )
    sum_c = Sum(me, *split_of(me, outs, n, r, 1, 1), bits)
    outs = first_grad_more(me, cross[0], x, after(dy_one, outs[0]), n, r, 2, 2)
    sum_d = Sum(me, *split_of(me, outs, n, r, cross[0], cross[0]), cross)
    state = (conv_weight, conv_mask, conv_rank, conv_first, conv_second)
    rep_bits = bits_of("rep")
    results, new = (), ()

    def close(one, at, *deps):
        one.turns()
        keep = after(one.keep, *deps)
        parts = (keep, one.got) if fine else (keep[:, 0] + decode(one.got, keep.shape[0]),)
        *both, low = finish(parts, state, results, at, keep.shape[0])
        return both, low

    def to_groups(low):
        for b in rep_bits[:-1]:
            low = (low.astype(F32) + swap(low, "rep", b).astype(F32)).astype(BF)
        return low, swap(low, "rep", rep_bits[-1])

    last = sum_a.turn(*sum_head.turns(outs[0]))
    last = sum_b.turn(last)
    last = sum_d.turn(last)
    last = sum_c.turn(last)
    last = sum_b.turn(last)
    results, low_a = close(sum_a, blocks, last)
    last = sum_d.turn(low_a)
    low_a, got_a = to_groups(low_a)
    last = sum_c.turn(last, low_a)
    results, low_d = close(sum_d, 2, last, got_a)
    results, low_c = close(sum_c, 0, low_d)
    results, low_b = close(sum_b, blocks + cut, low_c)
    low_c, got_c = to_groups(jnp.concatenate([low_c, low_d], axis=0))
    low_b, got_b = to_groups(low_b)
    back_one, packed = after((back_one, packed), low_a)
    bias_grad = packed[2:].reshape(-1)[:CLASSES]
    loss_sum = packed[3, C_MID - 1 :]
    head_grad = after(sum_head.keep, low_a)[:, 0] + decode(sum_head.got, 2)
    head_grad = head_grad.transpose(1, 0, 2).reshape(shard, WIDE)[:, :CLASSES]
    for low, got, at in ((low_a, got_a, blocks), (low_c, got_c, 0), (low_b, got_b, blocks + cut)):
        new = outer(low, got, state[:3] + (conv_outer,), new, at, groups)
    (conv_m, conv_v, mask_int), (conv_new, conv_mom) = results, new
    norm_grad = jnp.concatenate([back_one, packed[:2]], axis=0)
    head_s, head_m, head_v = adamw(head_weight, head_grad, head_first[0], head_second[0], 0.03)
    head_new, head_mom = outer_step(head_weight, rep_sum(head_s), head_outer, groups)
    norm_s, norm_m, norm_v = adamw(norm_params, norm_grad, norm_first[0], norm_second[0], 0.3)
    bias_s, bias_m, bias_v = adamw(head_bias, bias_grad, bias_first[0], bias_second[0], 0.3)
    wide = jnp.pad(bias_s, (0, WIDE - CLASSES)).reshape(2, width)
    small = jnp.pad(norm_s, ((0, 2), (0, 0))) + jnp.pad(wide, ((4, 0), (0, 0)))
    small = sum_all(small, "rep")
    norm_new, norm_mom = outer_step(norm_params, small[:4], norm_outer, groups)
    bias_new, bias_mom = outer_step(head_bias, small[4:].reshape(-1)[:CLASSES], bias_outer, groups)
    return (
        conv_new, mask_int, conv_m, conv_v, conv_mom,
        head_new, head_m[None], head_v[None], head_mom,
        norm_new, norm_m[None], norm_v[None], norm_mom,
        bias_new, bias_m[None], bias_v[None], bias_mom, loss_sum,
    )
def solution(mesh):
    conv = P(None, "dp", None)
    conv_rep = P("rep", None, "dp", None)
    head = P("dp", None)
    head_rep = P("rep", "dp", None)
    in_specs = (
        P(("rep", "dp"), None, None, None), P(("rep", "dp")), conv, conv, conv, head, P(), P(),
        conv_rep, conv_rep, head_rep, head_rep, P("rep", None, None), P("rep", None, None),
        P("rep", None), P("rep", None), conv, head, P(), P(),
    )
    out_specs = (
        conv, conv, conv_rep, conv_rep, conv, head, head_rep, head_rep, head,
        P(), P("rep", None, None), P("rep", None, None), P(),
        P(), P("rep", None), P("rep", None), P(), P("rep"),
    )
    return jax.shard_map(
        per_device, mesh=mesh, in_specs=in_specs, out_specs=out_specs, check_vma=False
    )
```

```python
import functools

import jax
import jax.numpy as jnp
from jax import lax
from jax.experimental import pallas as pl
from jax.experimental.pallas import tpu as pltpu
from jax.sharding import PartitionSpec as P

C_IN = 2048
C_MID = 512
CLASSES = 1000
WIDE = 1024
SIDE = 7
STEP = 10
PIX = 49
DROP_CUT = 78643
GROW_CUT = 242484
BF = jnp.bfloat16
F32 = jnp.float32
I32 = jnp.int32
I16 = jnp.int16
EXTRA = 16
LEVELS = 32000.0
LOG2E = 1.4426950408889634


def swap(x, axis, bit):
    n = lax.axis_size(axis)
    return lax.ppermute(x, axis, [(i, i ^ bit) for i in range(n)])


def bits_of(axis):
    n = lax.axis_size(axis)
    return [1 << k for k in range(n.bit_length() - 1)]


def sum_all(x, axis, *deps):
    bits = bits_of(axis)
    bits = bits[1:] + bits[:1]
    for bit in bits:
        if deps and bit == bits[-1]:
            x = after(x, *deps)
        x = x + swap(x, axis, bit)
    return x


def room(mib):
    return pltpu.CompilerParams(vmem_limit_bytes=mib * 1024 * 1024)


def pick(x, axis, index):
    return lax.dynamic_index_in_dim(x, index, axis, keepdims=False)


def gather_more(buf, rel, bit, *deps):
    buf = after(buf, *deps) if deps else buf
    return jnp.concatenate([buf, swap(buf, "dp", bit)], axis=0), rel + [r ^ bit for r in rel]


class Gather:
    def __init__(self, own):
        self.own, self.rel = own[None], [0]
        self.got = None

    def start(self):
        for bit in reversed(bits_of("dp")[2:]):
            self.join()
            self.got = swap(self.own, "dp", bit)
            self.rel = self.rel + [r ^ bit for r in self.rel]
        return self

    def join(self, *deps):
        if self.got is not None:
            got = after(self.got, *deps) if deps else self.got
            self.own, self.got = jnp.concatenate([self.own, got], axis=0), None

    def turn_near(self, *deps):
        self.join()
        own = after(self.own, *deps) if deps else self.own
        self.near = swap(own, "dp", bits_of("dp")[1])

    def turn_side(self, *deps):
        own = after(self.own, *deps) if deps else self.own
        self.side = swap(own, "dp", bits_of("dp")[0])

    def turn_far(self, *deps):
        near = after(self.near, *deps) if deps else self.near
        self.far = swap(near, "dp", bits_of("dp")[0])

    def finish(self, *deps):
        bits = bits_of("dp")
        far = after(self.far, *deps) if deps else self.far
        pieces = [self.own, self.near, self.side, far]
        shifts = [0, bits[1], bits[0], bits[1] | bits[0]]
        codes = [[(0, r ^ s) for r in self.rel] for s in shifts]
        pieces += [swap(p, "rep", 1) for p in pieces]
        codes += [[(1, r) for _, r in c] for c in codes]
        if self.own.shape[2] % 16:
            return place(pieces, codes), None
        return pieces, codes


def place(pieces, codes):
    n = lax.axis_size("dp")
    flat = [c * n + r for code in codes for c, r in code]
    cores = len(flat) // n
    inverse = jnp.array([flat.index(k) for k in range(len(flat))], I32)
    me = (lax.axis_index("rep") % cores) * n + lax.axis_index("dp")
    where = inverse[jnp.arange(len(flat), dtype=I32) ^ me]
    full = jnp.take(jnp.concatenate(pieces, axis=0), where, axis=0)
    _, blocks, r, w = full.shape
    full = full.reshape(cores, n, blocks, r, w).transpose(2, 1, 0, 3, 4)
    return [full.reshape(1, blocks, n * cores * r, w)]


def fetch(src, dst, sem):
    copy = pltpu.make_async_copy(src, dst, sem)
    copy.start()
    return copy


def wait_all(copies):
    for copy in copies:
        copy.wait()


def entries(pieces):
    return sum(p.shape[0] for p in pieces)


def fetch_pieces(refs, codes, me, out, sems):
    copies = []
    for p, ref in enumerate(refs):
        r = ref.shape[2]
        for i in range(ref.shape[0]):
            if codes is None:
                row = 0
            else:
                c, s = codes[p][i]
                row = me[0] ^ s
                if any(c for code in codes for c, _ in code):
                    row = row * 2 + (me[1] ^ c)
                row = pl.multiple_of(row * r, 16)
            copies.append(fetch(ref.at[i], out.at[:, pl.ds(row, r), :], sems.at[len(copies)]))
    return copies


def by_blocks(count, outs, body):
    done = []
    for i in range(count):
        body(i)
        done += [fetch(buf.at[i], at(i), sems.at[i]) for at, buf, sems in outs]
    wait_all(done)


def dma(n):
    return pltpu.SemaphoreType.DMA((n,))


ANY = pl.BlockSpec(memory_space=pl.ANY)
IN_VMEM = pl.BlockSpec(memory_space=pltpu.VMEM)


SMEM = pl.BlockSpec(memory_space=pltpu.SMEM)

def cost(flops, byte_count):
    return pl.CostEstimate(flops=1, bytes_accessed=1, transcendentals=0)


def code_scale(k):
    return jnp.exp2(k * (1.0 / 16.0))


def code_step(top):
    return jnp.minimum(jnp.ceil(jnp.log2(jnp.maximum(top, 1e-30)) * 16.0), 2032.0)


def code_of(x, k):
    return jnp.floor(x * (LEVELS / code_scale(k)) + 0.5).astype(I32).astype(I16)


def value_of(q, k):
    return q.astype(I32).astype(F32) * (code_scale(k) * (1.0 / LEVELS))


def encode(x):
    k = code_step(jnp.max(jnp.abs(x), axis=1, keepdims=True))
    tail = jnp.pad(k[:, 0], ((0, EXTRA - x.shape[0]), (0, 0))).astype(I32).astype(I16)
    return jnp.concatenate([code_of(x, k).reshape(-1, x.shape[2]), tail], axis=0)


def decode(payload, blocks):
    q = payload[:-EXTRA].reshape(blocks, -1, payload.shape[1])
    return value_of(q, payload[-EXTRA:][:blocks, None, :].astype(F32))


def split_plain(full, bit, stride=1):
    b, n, r, w = full.shape
    view = full.reshape(b, n // (2 * stride), 2, stride, r, w)
    keep = pick(view, 2, bit).reshape(b, n // 2, r, w)
    return encode(pick(view, 2, 1 - bit).reshape(b, n // 2 * r, w)), keep


def side_of(me, bit):
    return (me[0] // bit) % 2


def put_split(block, bit, stride, send_ref, keep_ref, at):
    n, r, w = block.shape
    top = jnp.zeros((1, w), F32)
    base = [j // stride * 2 * stride + j % stride for j in range(n // 2)]
    for j in range(n // 2):
        keep_ref[at, j] = block[base[j] + stride * bit]
        top = jnp.maximum(
            top, jnp.max(jnp.abs(block[base[j] + stride * (1 - bit)]), axis=0, keepdims=True)
        )
    k = code_step(top)
    for j in range(n // 2):
        row = (at * (n // 2) + j) * r
        send_ref[row : row + r, :] = code_of(block[base[j] + stride * (1 - bit)], k)
    return k


def put_scales(send_ref, scales):
    w = send_ref.shape[1]
    row = lax.broadcasted_iota(I32, (EXTRA, w), 0)
    tail = jnp.zeros((EXTRA, w), F32)
    for i, k in enumerate(scales):
        tail = jnp.where(row == i, k, tail)
    send_ref[send_ref.shape[0] - EXTRA :, :] = tail.astype(I32).astype(I16)


def scales_of(got):
    return got[got.shape[0] - EXTRA :, :].astype(I32).astype(F32)


def part_shape(n, r):
    return (n, r) if r % 16 == 0 else (1, n * r)


def split_of(me, outs, n, r, bit, stride):
    if len(outs) == 2:
        return outs
    full = outs[0]
    return split_plain(full.reshape(full.shape[0], n, r, full.shape[-1]), side_of(me, bit), stride)


def split_shapes(blocks, n, r, w):
    if r % 16:
        return [jax.ShapeDtypeStruct((blocks, 1, n * r, w), F32)]
    return [
        jax.ShapeDtypeStruct((blocks * (n // 2) * r + EXTRA, w), I16),
        jax.ShapeDtypeStruct((blocks, n // 2, r, w), F32),
    ]


def add_split_kernel(bit, stride, me, keep_in, got, send, keep, total):
    n, r = keep_in.shape[1:3]
    given, scales = scales_of(got), []
    for i in range(keep_in.shape[0]):
        for j in range(n):
            row = (i * n + j) * r
            total[j] = keep_in[i, j] + value_of(got[row : row + r, :], given[i : i + 1])
        scales.append(put_split(total, side_of(me, bit), stride, send, keep, i))
    put_scales(send, scales)


def add_split(me, keep, got, bit, stride):
    b, n, r, w = keep.shape
    if r % 16:
        return split_plain(keep + decode(got, b).reshape(keep.shape), side_of(me, bit), stride)
    return pl.pallas_call(
        functools.partial(add_split_kernel, bit, stride),
        in_specs=[SMEM, IN_VMEM, IN_VMEM],
        out_specs=[IN_VMEM, IN_VMEM],
        out_shape=split_shapes(b, n, r, w),
        scratch_shapes=[pltpu.VMEM((n, r, w), F32)],
        compiler_params=room(8),
        cost_estimate=cost(1, 1),
        name="add_split",
    )(me, keep, got)


def after(x, *deps):
    return lax.optimization_barrier((x, deps))[0]


class Sum:
    def __init__(self, me, send, keep, bits):
        self.me = me
        self.send, self.keep, self.bits, self.done = send, keep, list(bits), []
        self.got = swap(send, "dp", self.bits[0])

    def turn(self, *deps):
        self.done.append(self.bits.pop(0))
        nxt = self.bits[0]
        stride = nxt
        for used in self.done:
            stride = stride // 2 if used < nxt else stride
        got = after(self.got, *deps) if deps else self.got
        self.send, self.keep = add_split(self.me, self.keep, got, nxt, stride)
        self.got = swap(self.send, "dp", nxt)
        return self.keep

    def turns(self, *deps):
        while len(self.bits) > 1:
            deps = (self.turn(*deps),)
        return deps


def norm_rows(sums, gain, shift, total):
    mean = sums[0:1] * (1.0 / total)
    var = sums[1:2] * (1.0 / total) - mean * mean
    rstd = lax.rsqrt(var + 1e-05)
    factor = gain * rstd
    return mean, rstd, factor, shift - mean * factor


def inverse(d):
    r = pl.reciprocal(d, approx=True)
    return r * (2.0 - d * r)


def gate(y, factor, offset):
    z = y * factor + offset
    power = jnp.minimum(y * (factor * -LOG2E) + offset * -LOG2E, 100.0)
    return z, inverse(1.0 + jnp.exp2(power))


def slope_of(z, sig):
    return sig * (1.0 + (z - z * sig))


def back_rows(back, rstd, mean, factor, total):
    d = -(factor * rstd) * (back[0:1] * (1.0 / total))
    return d, -factor * (back[1:2] * (1.0 / total)) - mean * d


def flat(x):
    return x.reshape(-1, x.shape[-1])


def add_sums(sums, one, two):
    sums[0:1] += jnp.sum(one, axis=0, keepdims=True)
    sums[1:2] += jnp.sum(two, axis=0, keepdims=True)


def first_kernel(codes, count, me, x, *refs):
    pieces, (y, sums, weights, p_sem) = refs[:count], refs[count:]
    copies = fetch_pieces(pieces, codes, me, weights, p_sem)
    sums[...] = jnp.zeros_like(sums)
    wait_all(copies)
    for k in range(SIDE):
        out = jnp.dot(x[k], weights[...].reshape(-1, C_MID), preferred_element_type=F32)
        y[k] = out
        add_sums(sums, out, out * out)


def first_forward(me, x, pieces, codes):
    rows = x.shape[1]
    return pl.pallas_call(
        functools.partial(first_kernel, codes, len(pieces)),
        in_specs=[SMEM, IN_VMEM] + [ANY] * len(pieces),
        out_specs=[IN_VMEM, IN_VMEM],
        out_shape=[
            jax.ShapeDtypeStruct((SIDE, rows, C_MID), F32), jax.ShapeDtypeStruct((2, C_MID), F32),
        ],
        scratch_shapes=[
            pltpu.VMEM((C_IN // C_MID, C_MID, C_MID), BF), dma(entries(pieces)),
        ],
        compiler_params=room(8),
        cost_estimate=cost(1, 1),
        name="first_forward",
    )(me, x, *pieces)


def clear_border(pad):
    zero = jnp.zeros(pad.shape[1:], pad.dtype)
    pad[0] = zero
    pad[SIDE + 1] = zero
    for k in range(1, SIDE + 1):
        pad[k, 0] = zero[0]
        pad[k, SIDE + 1] = zero[0]


def second_kernel(codes, count, total, me, y1, sums1, params, *refs):
    pieces, (h1, y2, sums2, taps, pad, p_sem) = refs[:count], refs[count:]
    batch = pad.shape[2]
    copies = fetch_pieces(pieces, codes, me, taps, p_sem)
    clear_border(pad)
    sums2[...] = jnp.zeros_like(sums2)
    _, _, factor, offset = norm_rows(sums1[...], params[0:1], params[1:2], total)

    def act(k):
        z, sig = gate(y1[k], factor, offset)
        h = (z * sig).astype(BF).reshape(SIDE, batch, C_MID)
        pad[k + 1, 1 : SIDE + 1] = h
        h1[k] = h

    act(0)
    act(1)
    wait_all(copies)
    for k in range(SIDE):
        out = None
        for a in range(3):
            if 0 <= k + a - 1 < SIDE:
                patch = jnp.concatenate([flat(pad[k + a, b : b + SIDE]) for b in range(3)], axis=1)
                part = jnp.dot(
                    patch, taps[3 * a : 3 * a + 3].reshape(3 * C_MID, C_MID),
                    preferred_element_type=F32,
                )
                out = part if out is None else out + part
        if k + 2 < SIDE:
            act(k + 2)
        y2[k] = out
        add_sums(sums2, out, out * out)


def second_forward(me, y1, sums1, params, pieces, codes, total):
    rows = y1.shape[1]
    batch = rows // SIDE
    return pl.pallas_call(
        functools.partial(second_kernel, codes, len(pieces), total),
        in_specs=[SMEM, IN_VMEM, IN_VMEM, IN_VMEM] + [ANY] * len(pieces),
        out_specs=[IN_VMEM] * 4,
        out_shape=[
            jax.ShapeDtypeStruct((SIDE, SIDE, batch, C_MID), BF),
            jax.ShapeDtypeStruct(y1.shape, F32),
            jax.ShapeDtypeStruct((2, C_MID), F32),
            jax.ShapeDtypeStruct((9, C_MID, C_MID), BF),
        ],
        scratch_shapes=[
            pltpu.VMEM((SIDE + 2, SIDE + 2, batch, C_MID), BF), dma(entries(pieces)),
        ],
        compiler_params=room(12),
        cost_estimate=cost(1, 1),
        name="second_forward",
    )(me, y1, sums1, params, *pieces)


def head_kernel(codes, count, outs_n, total, group_images, me, y2, sums2, params, bias, labels, *refs):
    pieces, refs = refs[:count], refs[count:]
    outs, (packed, dpool_out, head, block, p_sem) = refs[:outs_n], refs[outs_n:]
    batch = dpool_out.shape[0]
    copies = fetch_pieces(pieces, codes, me, head, p_sem)
    mean, rstd, factor, offset = norm_rows(sums2[...], params[2:3], params[3:4], total)
    sum_h = sum_a = sum_b = jnp.zeros((batch, C_MID), F32)
    fold = lambda v: jnp.sum(v.reshape(SIDE, batch, C_MID), axis=0)
    for k in range(SIDE):
        z, sig = gate(y2[k], factor, offset)
        slope = slope_of(z, sig)
        sum_h = sum_h + fold(z * sig)
        sum_a = sum_a + fold(slope)
        sum_b = sum_b + fold(slope * ((y2[k] - mean) * rstd))
    wait_all(copies)
    pooled = (sum_h * (1.0 / PIX)).astype(BF)
    logits = jnp.concatenate(
        [jnp.dot(pooled, head[k], preferred_element_type=F32) for k in range(2)], axis=1
    )
    logits = logits + bias[...]
    column = lax.broadcasted_iota(I32, (batch, WIDE), 1)
    logits = jnp.where(column < CLASSES, logits, -1e30)
    across = lax.broadcasted_iota(I32, (batch, batch), 0) == lax.broadcasted_iota(I32, (batch, batch), 1)
    label = jnp.sum(jnp.where(across, labels[...], 0), axis=1, keepdims=True)
    onehot = (label == column).astype(F32)
    top = jnp.max(logits, axis=1, keepdims=True)
    expo = jnp.exp(logits - top)
    expsum = jnp.sum(expo, axis=1, keepdims=True)
    lse = top + jnp.log(expsum)
    loss = jnp.sum(lse - jnp.sum(logits * onehot, axis=1, keepdims=True), axis=0, keepdims=True)
    dlogits = ((jnp.exp(logits - lse) - onehot) * (1.0 / group_images)).astype(BF)
    bias_sum = jnp.sum(dlogits.astype(F32), axis=0, keepdims=True)
    last = lax.broadcasted_iota(I32, (1, WIDE), 1) == WIDE - 1
    bias_sum = jnp.where(last, loss, bias_sum)
    dpool = jnp.zeros((batch, C_MID), F32)
    for k in range(2):
        part = dlogits[:, k * C_MID : (k + 1) * C_MID]
        dpool = dpool + lax.dot_general(
            part, head[k], (((1,), (1,)), ((), ())), preferred_element_type=F32
        )

    def make(k):
        block[...] = lax.dot_general(
            pooled, dlogits[:, k * C_MID : (k + 1) * C_MID], (((0,), (0,)), ((), ())),
            preferred_element_type=F32,
        ).reshape(block.shape)

    emit_all(2, make, block, me, 1, outs)
    dpool = dpool * (1.0 / PIX)
    dpool_out[...] = dpool
    packed[0:1] = jnp.sum(dpool * sum_b, axis=0, keepdims=True)
    packed[1:2] = jnp.sum(dpool * sum_a, axis=0, keepdims=True)
    packed[2:3] = bias_sum[:, :C_MID]
    packed[3:4] = bias_sum[:, C_MID:]


def head_step(me, y2, sums2, params, bias, labels, pieces, codes, total, group_images, n, r):
    rows = y2.shape[1]
    batch = rows // SIDE
    shapes = split_shapes(2, n, r, C_MID)
    return pl.pallas_call(
        functools.partial(head_kernel, codes, len(pieces), len(shapes), total, group_images),
        in_specs=[SMEM] + [IN_VMEM] * 5 + [ANY] * len(pieces),
        out_specs=[IN_VMEM] * (2 + len(shapes)),
        out_shape=shapes + [
            jax.ShapeDtypeStruct((4, C_MID), F32), jax.ShapeDtypeStruct((batch, C_MID), F32),
        ],
        scratch_shapes=[
            pltpu.VMEM((2, C_MID, C_MID), BF), pltpu.VMEM(part_shape(n, r) + (C_MID,), F32),
            dma(entries(pieces)),
        ],
        compiler_params=room(8),
        cost_estimate=cost(1, 1),
        name="head_step",
    )(me, y2, sums2, params, bias, labels, *pieces)


def emit_all(count, make, block, me, bit, outs):
    scales = []
    for i in range(count):
        make(i)
        if len(outs) == 1:
            outs[0][i] = block[...]
        else:
            scales.append(put_split(block, side_of(me, bit), bit, *outs, i))
    if scales:
        put_scales(outs[0], scales)


def one_tap(tap, pad, turned, block):
    a, b = tap // 3, tap % 3
    moved = pad[2 - a : 2 - a + SIDE, 2 - b : 2 - b + SIDE].reshape(-1, C_MID)
    block[...] = jnp.dot(turned[...], moved, preferred_element_type=F32).reshape(block.shape)


def taps_kernel(total, bits, me, y2, sums2, back, params, dpool, h1, pad, turned, *refs):
    outs, block = refs[:-1], refs[-1]
    batch = pad.shape[2]
    clear_border(pad)
    mean, rstd, factor, offset = norm_rows(sums2[...], params[2:3], params[3:4], total)
    d, e = back_rows(back, rstd, mean, factor, total)
    scaled = (dpool[...] * factor)[None]
    turned[...] = h1[...].reshape(-1, C_MID).T
    for k in range(SIDE):
        z, sig = gate(y2[k], factor, offset)
        dz = flat(slope_of(z, sig).reshape(SIDE, batch, C_MID) * scaled)
        dy = dz + (y2[k] * d + e)
        pad[k + 1, 1 : SIDE + 1] = dy.astype(BF).reshape(SIDE, batch, C_MID)
    each, first = len(outs) // len(bits), 0
    for k, bit in enumerate(bits):
        some = outs[k * each : (k + 1) * each]
        make = lambda i, first=first: one_tap(first + i, pad, turned, block)
        emit_all(some[-1].shape[0], make, block, me, bit, some)
        first += some[-1].shape[0]


def taps_more_kernel(first_tap, me, pad, turned, *refs):
    outs, block = refs[:-1], refs[-1]
    make = lambda i: one_tap(i + first_tap, pad, turned, block)
    emit_all(outs[-1].shape[0], make, block, me, 1, outs)


def taps_grad_first(me, y2, sums2, back, params, dpool, h1, total, n, r, counts, bits):
    batch = h1.shape[2]
    shapes = [v for count in counts for v in split_shapes(count, n, r, C_MID)]
    return pl.pallas_call(
        functools.partial(taps_kernel, total, bits),
        in_specs=[SMEM] + [IN_VMEM] * 6,
        out_specs=[IN_VMEM] * (2 + len(shapes)),
        out_shape=[
            jax.ShapeDtypeStruct((SIDE + 2, SIDE + 2, batch, C_MID), BF),
            jax.ShapeDtypeStruct((C_MID, SIDE * SIDE * batch), BF),
        ] + shapes,
        scratch_shapes=[pltpu.VMEM(part_shape(n, r) + (C_MID,), F32)],
        compiler_params=room(8),
        cost_estimate=cost(1, 1),
        name="taps_grad_first",
    )(me, y2, sums2, back, params, dpool, h1)


def taps_grad_more(me, pad, turned, n, r, first_tap, count):
    shapes = split_shapes(count, n, r, C_MID)
    return pl.pallas_call(
        functools.partial(taps_more_kernel, first_tap),
        in_specs=[SMEM, IN_VMEM, IN_VMEM],
        out_specs=[IN_VMEM] * len(shapes),
        out_shape=shapes,
        scratch_shapes=[pltpu.VMEM(part_shape(n, r) + (C_MID,), F32)],
        compiler_params=room(8),
        cost_estimate=cost(1, 1),
        name="taps_grad_more",
    )(me, pad, turned)


def input_grad_kernel(total, pad, y1, sums1, params, taps, dz1, sums):
    sums[...] = jnp.zeros_like(sums)
    mean, rstd, factor, offset = norm_rows(sums1[...], params[0:1], params[1:2], total)
    for k in range(SIDE):
        dh = None
        for a in range(3):
            for b in range(3):
                if 0 <= k + 1 - a < SIDE:
                    part = lax.dot_general(
                        flat(pad[k + 2 - a, 2 - b : 2 - b + SIDE]), taps[3 * a + b],
                        (((1,), (1,)), ((), ())), preferred_element_type=F32,
                    )
                    dh = part if dh is None else dh + part
        dz = dh * slope_of(*gate(y1[k], factor, offset))
        dz1[k] = dz
        add_sums(sums, dz * ((y1[k] - mean) * rstd), dz)


def input_grad(pad, y1, sums1, params, taps, total):
    return pl.pallas_call(
        functools.partial(input_grad_kernel, total),
        in_specs=[IN_VMEM] * 5,
        out_specs=[IN_VMEM] * 2,
        out_shape=[jax.ShapeDtypeStruct(y1.shape, F32), jax.ShapeDtypeStruct((2, C_MID), F32)],
        compiler_params=room(8),
        cost_estimate=cost(1, 1),
        name="input_grad",
    )(pad, y1, sums1, params, taps)


def one_first(x, dy, at, block):
    block[...] = lax.dot_general(
        flat(x[:, :, at * C_MID : (at + 1) * C_MID]), flat(dy[...]), (((0,), (0,)), ((), ())),
        preferred_element_type=F32,
    ).reshape(block.shape)


def first_grad_kernel(total, me, dz1, y1, sums1, back, params, x, dy, *refs):
    outs, block = refs[:-1], refs[-1]
    mean, rstd, factor, _ = norm_rows(sums1[...], params[0:1], params[1:2], total)
    d, e = back_rows(back, rstd, mean, factor, total)
    for k in range(SIDE):
        dy[k] = (dz1[k] * factor + (y1[k] * d + e)).astype(BF)
    emit_all(outs[-1].shape[0], lambda i: one_first(x, dy, i, block), block, me, 1, outs)


def first_more_kernel(bit, first, me, x, dy, *refs):
    outs, block = refs[:-1], refs[-1]
    make = lambda i: one_first(x, dy, first + i, block)
    emit_all(outs[-1].shape[0], make, block, me, bit, outs)


def first_grad_first(me, dz1, y1, sums1, back, params, x, total, n, r, count):
    shapes = split_shapes(count, n, r, C_MID)
    return pl.pallas_call(
        functools.partial(first_grad_kernel, total),
        in_specs=[SMEM] + [IN_VMEM] * 6,
        out_specs=[IN_VMEM] * (1 + len(shapes)),
        out_shape=[jax.ShapeDtypeStruct(y1.shape, BF)] + shapes,
        scratch_shapes=[pltpu.VMEM(part_shape(n, r) + (C_MID,), F32)],
        compiler_params=room(8),
        cost_estimate=cost(1, 1),
        name="first_grad_first",
    )(me, dz1, y1, sums1, back, params, x)


def first_grad_more(me, bit, x, dy, n, r, first_block, count):
    shapes = split_shapes(count, n, r, C_MID)
    return pl.pallas_call(
        functools.partial(first_more_kernel, bit, first_block),
        in_specs=[SMEM, IN_VMEM, IN_VMEM],
        out_specs=[IN_VMEM] * len(shapes),
        out_shape=shapes,
        scratch_shapes=[pltpu.VMEM(part_shape(n, r) + (C_MID,), F32)],
        compiler_params=room(8),
        cost_estimate=cost(1, 1),
        name="first_grad_more",
    )(me, x, dy)


def adamw(weight, grad, first, second, rate):
    first = 0.9 * first + 0.1 * grad
    second = 0.999 * second + 0.001 * grad * grad
    normal_step = first / (1.0 - 0.9**STEP) / (jnp.sqrt(second / (1.0 - 0.999**STEP)) + 1e-08)
    return (-rate * (normal_step + 0.01 * weight), first, second)


def outer_step(start, step_sum, momentum, groups):
    delta = -(step_sum / groups)
    momentum = 0.9 * momentum + delta
    return (start - 0.7 * (delta + 0.9 * momentum), momentum)


def rep_sum(x):
    for bit in bits_of("rep"):
        low = x.astype(BF)
        x = low.astype(F32) + swap(low, "rep", bit).astype(F32)
    return x


def finish_kernel(n_parts, at, before, *refs):
    parts, state, refs = refs[:n_parts], refs[n_parts : n_parts + 5], refs[n_parts + 5 + before :]
    outs, (low, *refs) = refs[:3], refs[3:]
    bufs, sems = refs[:3], refs[3:]
    given = scales_of(parts[1]) if n_parts == 2 else None

    def body(i):
        if n_parts == 2:
            keep, got = parts
            r = keep.shape[2]
            owned = keep[i, 0] + value_of(got[i * r : (i + 1) * r, :], given[i : i + 1])
        else:
            owned = parts[0][i]
        weight, mask, rank = (ref[at + i] for ref in state[:3])
        first, second = (ref[0, at + i] for ref in state[3:])
        bufs[2][i] = mask_of(mask, rank)
        old, new = masks(mask, rank)
        effective = weight * old
        kept = old * new
        dense = owned + 5e-05 * effective
        step, m, v = adamw(weight * kept, new * dense, first * kept, second * kept, 0.03)
        bufs[0][i] = m * new
        bufs[1][i] = v * new
        low[i] = (step * new).astype(BF)

    here = lambda ref: lambda i: ref.at[at + i]
    here_rep = lambda ref: lambda i: ref.at[0, at + i]
    wheres = (here_rep, here_rep, here)
    by_blocks(low.shape[0], [(f(ref), *two) for f, ref, *two in zip(wheres, outs, bufs, sems)], body)


def mask_of(old, rank):
    return jnp.where(rank < DROP_CUT, 0, jnp.where(rank >= GROW_CUT, 1, old))


def masks(old, rank):
    return old.astype(F32), mask_of(old, rank).astype(F32)


def finish(parts, state, before, at, count):
    shard, w = state[0].shape[1:]
    own = lambda t: pltpu.VMEM((count, shard, w), t)
    n_in = len(parts) + 5
    return pl.pallas_call(
        functools.partial(finish_kernel, len(parts), at, len(before)),
        in_specs=[IN_VMEM] * n_in + [ANY] * len(before),
        out_specs=[ANY, ANY, ANY, IN_VMEM],
        out_shape=[
            jax.ShapeDtypeStruct(state[3].shape, F32), jax.ShapeDtypeStruct(state[4].shape, F32),
            jax.ShapeDtypeStruct(state[1].shape, I32),
            jax.ShapeDtypeStruct((count, shard, w), BF),
        ],
        input_output_aliases={n_in + k: k for k in range(len(before))},
        scratch_shapes=[own(F32), own(F32), own(I32)] + [dma(count)] * 3,
        compiler_params=room(12),
        cost_estimate=cost(1, 1),
        name="finish",
    )(*parts, *state, *before)


def outer_kernel(groups, at, before, low, got, *refs):
    state, refs = refs[:4], refs[4 + before :]
    outs, bufs, sems = refs[:2], refs[2:4], refs[4:]

    def body(i):
        weight, mask, rank, momentum = (ref[at + i] for ref in state)
        old, new = masks(mask, rank)
        total = low[i].astype(F32) + got[i].astype(F32)
        value, mom = outer_step(weight * (old * new), total, momentum, groups)
        bufs[0][i] = value * new
        bufs[1][i] = mom * new

    here = lambda ref: lambda i: ref.at[at + i]
    by_blocks(low.shape[0], [(here(ref), *two) for ref, *two in zip(outs, bufs, sems)], body)


def outer(low, got, state, before, at, groups):
    return pl.pallas_call(
        functools.partial(outer_kernel, groups, at, len(before)),
        in_specs=[IN_VMEM] * 6 + [ANY] * len(before),
        out_specs=[ANY, ANY],
        out_shape=[jax.ShapeDtypeStruct(state[0].shape, F32)] * 2,
        input_output_aliases={6 + k: k for k in range(len(before))},
        scratch_shapes=[pltpu.VMEM(low.shape, F32)] * 2 + [dma(low.shape[0])] * 2,
        compiler_params=room(12),
        cost_estimate=cost(1, 1),
        name="outer",
    )(low, got, *state, *before)


def per_device(
    images, labels, conv_weight, conv_mask, conv_rank, head_weight, norm_params, head_bias,
    conv_first, conv_second, head_first, head_second, norm_first, norm_second, bias_first,
    bias_second, conv_outer, head_outer, norm_outer, bias_outer,
):
    devices = lax.axis_size("dp")
    groups = lax.axis_size("rep")
    width = C_MID
    blocks = C_IN // C_MID
    core = lax.axis_index("rep") % 2
    dp = lax.axis_index("dp")
    me = jnp.stack([dp, core]).astype(I32)
    bits = bits_of("dp")
    shard = conv_weight.shape[1]
    batch = images.shape[0]
    rows = batch * PIX
    total = float(rows * devices)
    group_images = batch * devices
    half = shard // 2

    def mine(x):
        return pick(x.reshape(-1, 2, half, width), 1, core)

    def active(sl):
        return jnp.where(mine(conv_mask[sl]) == 1, mine(conv_weight[sl]), 0.0).astype(BF)

    head_wide = jnp.pad(head_weight.astype(BF), ((0, 0), (0, WIDE - CLASSES)))
    head_low = mine(head_wide.reshape(shard, 2, width).transpose(1, 0, 2))
    taps_low = active(slice(blocks, None))
    get_first = Gather(active(slice(0, blocks))).start()
    get_first.join()
    get_taps = Gather(after(taps_low, get_first.own)).start()
    get_first.own = after(get_first.own, taps_low)
    get_first.turn_near()
    get_first.turn_side()
    get_first.turn_far()
    first_pieces, first_codes = get_first.finish()
    fine = first_codes is not None
    classes = labels.reshape(1, batch)
    x = images.transpose(1, 2, 0, 3).reshape(SIDE, SIDE * batch, C_IN)
    y_one, sums_one = first_forward(me, x, first_pieces, first_codes)
    head_got = gather_more(after(head_low, y_one)[None], [0], bits[0])
    sums_one = sums_one + swap(sums_one, "dp", bits[0])
    get_taps.join(sums_one, head_got[0])
    get_taps.turn_near()
    get_taps.turn_side()
    get_taps.turn_far(get_taps.side)
    for bit in bits[1:]:
        sums_one = sums_one + swap(sums_one, "dp", bit)
    taps_pieces, taps_codes = get_taps.finish(sums_one)
    buf, rel = after(head_got[0], get_taps.near), head_got[1]
    head_more = swap(buf, "dp", bits[-1])
    h_one, y_two, sums_two, taps = second_forward(
        me, y_one, sums_one, norm_params, taps_pieces, taps_codes, total
    )
    buf = jnp.concatenate([buf, after(head_more, sums_two)], axis=0)
    rel = rel + [code ^ bits[-1] for code in rel]
    for bit in reversed(bits[2:-1]):
        buf, rel = gather_more(buf, rel, bit)
    head_more = swap(buf, "dp", bits[1])
    for bit in bits[:-1]:
        sums_two = sums_two + swap(sums_two, "dp", bit)
    buf = jnp.concatenate([buf, after(head_more, sums_two)], axis=0)
    rel = rel + [code ^ bits[1] for code in rel]
    head_pieces, head_codes = [buf, swap(buf, "rep", 1)], [[(c, r) for r in rel] for c in range(2)]
    if not fine:
        head_pieces, head_codes = place(head_pieces, head_codes), None
    sums_two = sums_two + swap(sums_two, "dp", bits[-1])
    bias_wide = jnp.pad(head_bias, (0, WIDE - CLASSES)).reshape(1, WIDE)
    *outs, packed, dpool = head_step(
        me, y_two, sums_two, norm_params, bias_wide, classes, head_pieces, head_codes, total,
        group_images, devices, shard,
    )
    n, r = devices, shard
    sum_head = Sum(me, *split_of(me, outs, n, r, 1, 1), bits)
    packed = sum_all(packed, "dp")
    cut = 5
    dpool = after(dpool, sum_head.turn(packed))
    pad, turned, *outs = taps_grad_first(
        me, y_two, sums_two, packed, norm_params, dpool, h_one, total, n, r, (cut,), bits[:1]
    )
    sum_a = Sum(me, *split_of(me, outs, n, r, 1, 1), bits)
    pad = after(pad, outs[0])
    dz_one, back_one = input_grad(pad, y_one, sums_one, norm_params, taps, total)
    turned = after(turned, dz_one)
    outs = taps_grad_more(me, pad, turned, n, r, cut, 9 - cut)
    back_one = sum_all(back_one, "dp", sum_head.turn(outs[0]))
    send, keep = split_of(me, outs, n, r, 1, 1)
    sum_b = Sum(me, after(send, back_one), keep, bits)
    last = sum_a.turn(back_one)
    dy_one, *outs = first_grad_first(
        me, dz_one, y_one, sums_one, after(back_one, last), norm_params, x, total, n, r, 2
    )
    sum_c = Sum(me, *split_of(me, outs, n, r, 1, 1), bits)
    outs = first_grad_more(me, 1, x, after(dy_one, outs[0]), n, r, 2, 2)
    sum_d = Sum(me, *split_of(me, outs, n, r, 1, 1), bits)
    state = (conv_weight, conv_mask, conv_rank, conv_first, conv_second)
    rep_bits = bits_of("rep")
    results, new = (), ()

    def close(one, at, *deps):
        one.turns()
        keep = after(one.keep, *deps)
        parts = (keep, one.got) if fine else (keep[:, 0] + decode(one.got, keep.shape[0]),)
        *both, low = finish(parts, state, results, at, keep.shape[0])
        return both, low

    def to_groups(low):
        for b in rep_bits[:-1]:
            low = (low.astype(F32) + swap(low, "rep", b).astype(F32)).astype(BF)
        return low, swap(low, "rep", rep_bits[-1])

    last = sum_a.turn(*sum_head.turns(outs[0]))
    last = sum_b.turn(last)
    last = sum_c.turn(last)
    results, low_a = close(sum_a, blocks, last)
    last = sum_b.turn(low_a)
    last = sum_d.turn(last)
    last = sum_c.turn(last)
    low_a, got_a = to_groups(low_a)
    last = sum_d.turn(last)
    results, low_b = close(sum_b, blocks + cut, last, got_a)
    results, low_c = close(sum_c, 0, low_b)
    results, low_d = close(sum_d, 2, low_c)
    low_b, got_b = to_groups(low_b)
    low_c, got_c = to_groups(jnp.concatenate([low_c, low_d], axis=0))
    back_one, packed = after((back_one, packed), low_a)
    bias_grad = packed[2:].reshape(-1)[:CLASSES]
    loss_sum = packed[3, C_MID - 1 :]
    head_grad = after(sum_head.keep, low_a)[:, 0] + decode(sum_head.got, 2)
    head_grad = head_grad.transpose(1, 0, 2).reshape(shard, WIDE)[:, :CLASSES]
    for low, got, at in ((low_a, got_a, blocks), (low_b, got_b, blocks + cut), (low_c, got_c, 0)):
        new = outer(low, got, state[:3] + (conv_outer,), new, at, groups)
    (conv_m, conv_v, mask_int), (conv_new, conv_mom) = results, new
    norm_grad = jnp.concatenate([back_one, packed[:2]], axis=0)
    head_s, head_m, head_v = adamw(head_weight, head_grad, head_first[0], head_second[0], 0.03)
    head_new, head_mom = outer_step(head_weight, rep_sum(head_s), head_outer, groups)
    norm_s, norm_m, norm_v = adamw(norm_params, norm_grad, norm_first[0], norm_second[0], 0.3)
    bias_s, bias_m, bias_v = adamw(head_bias, bias_grad, bias_first[0], bias_second[0], 0.3)
    wide = jnp.pad(bias_s, (0, WIDE - CLASSES)).reshape(2, width)
    small = jnp.pad(norm_s, ((0, 2), (0, 0))) + jnp.pad(wide, ((4, 0), (0, 0)))
    small = sum_all(small, "rep")
    norm_new, norm_mom = outer_step(norm_params, small[:4], norm_outer, groups)
    bias_new, bias_mom = outer_step(head_bias, small[4:].reshape(-1)[:CLASSES], bias_outer, groups)
    return (
        conv_new, mask_int, conv_m, conv_v, conv_mom,
        head_new, head_m[None], head_v[None], head_mom,
        norm_new, norm_m[None], norm_v[None], norm_mom,
        bias_new, bias_m[None], bias_v[None], bias_mom, loss_sum,
    )
def solution(mesh):
    conv = P(None, "dp", None)
    conv_rep = P("rep", None, "dp", None)
    head = P("dp", None)
    head_rep = P("rep", "dp", None)
    in_specs = (
        P(("rep", "dp"), None, None, None), P(("rep", "dp")), conv, conv, conv, head, P(), P(),
        conv_rep, conv_rep, head_rep, head_rep, P("rep", None, None), P("rep", None, None),
        P("rep", None), P("rep", None), conv, head, P(), P(),
    )
    out_specs = (
        conv, conv, conv_rep, conv_rep, conv, head, head_rep, head_rep, head,
        P(), P("rep", None, None), P("rep", None, None), P(),
        P(), P("rep", None), P("rep", None), P(), P("rep"),
    )
    return jax.shard_map(
        per_device, mesh=mesh, in_specs=in_specs, out_specs=out_specs, check_vma=False
    )
```

```python
import functools

import jax
import jax.numpy as jnp
from jax import lax
from jax.experimental import pallas as pl
from jax.experimental.pallas import tpu as pltpu
from jax.sharding import PartitionSpec as P

C_IN = 2048
C_MID = 512
CLASSES = 1000
WIDE = 1024
SIDE = 7
STEP = 10
PIX = 49
DROP_CUT = 78643
GROW_CUT = 242484
BF = jnp.bfloat16
F32 = jnp.float32
I32 = jnp.int32
I16 = jnp.int16
EXTRA = 16
LEVELS = 32000.0
LOG2E = 1.4426950408889634


def swap(x, axis, bit):
    n = lax.axis_size(axis)
    return lax.ppermute(x, axis, [(i, i ^ bit) for i in range(n)])


def bits_of(axis):
    n = lax.axis_size(axis)
    return [1 << k for k in range(n.bit_length() - 1)]


def sum_all(x, axis, *deps):
    bits = bits_of(axis)
    bits = bits[1:] + bits[:1]
    for bit in bits:
        if deps and bit == bits[-1]:
            x = after(x, *deps)
        x = x + swap(x, axis, bit)
    return x


def room(mib):
    return pltpu.CompilerParams(vmem_limit_bytes=mib * 1024 * 1024)


def pick(x, axis, index):
    return lax.dynamic_index_in_dim(x, index, axis, keepdims=False)


def gather_more(buf, rel, bit, *deps):
    buf = after(buf, *deps) if deps else buf
    return jnp.concatenate([buf, swap(buf, "dp", bit)], axis=0), rel + [r ^ bit for r in rel]


class Gather:
    def __init__(self, own):
        self.own, self.rel = own[None], [0]
        self.got = None

    def start(self):
        for bit in reversed(bits_of("dp")[2:]):
            self.join()
            self.got = swap(self.own, "dp", bit)
            self.rel = self.rel + [r ^ bit for r in self.rel]
        return self

    def join(self, *deps):
        if self.got is not None:
            got = after(self.got, *deps) if deps else self.got
            self.own, self.got = jnp.concatenate([self.own, got], axis=0), None

    def turn_near(self, *deps):
        self.join()
        own = after(self.own, *deps) if deps else self.own
        self.near = swap(own, "dp", bits_of("dp")[1])

    def turn_side(self, *deps):
        own = after(self.own, *deps) if deps else self.own
        self.side = swap(own, "dp", bits_of("dp")[0])

    def turn_far(self, *deps):
        near = after(self.near, *deps) if deps else self.near
        self.far = swap(near, "dp", bits_of("dp")[0])

    def finish(self, *deps):
        bits = bits_of("dp")
        far = after(self.far, *deps) if deps else self.far
        pieces = [self.own, self.near, self.side, far]
        shifts = [0, bits[1], bits[0], bits[1] | bits[0]]
        codes = [[(0, r ^ s) for r in self.rel] for s in shifts]
        pieces += [swap(p, "rep", 1) for p in pieces]
        codes += [[(1, r) for _, r in c] for c in codes]
        if self.own.shape[2] % 16:
            return place(pieces, codes), None
        return pieces, codes


def place(pieces, codes):
    n = lax.axis_size("dp")
    flat = [c * n + r for code in codes for c, r in code]
    cores = len(flat) // n
    inverse = jnp.array([flat.index(k) for k in range(len(flat))], I32)
    me = (lax.axis_index("rep") % cores) * n + lax.axis_index("dp")
    where = inverse[jnp.arange(len(flat), dtype=I32) ^ me]
    full = jnp.take(jnp.concatenate(pieces, axis=0), where, axis=0)
    _, blocks, r, w = full.shape
    full = full.reshape(cores, n, blocks, r, w).transpose(2, 1, 0, 3, 4)
    return [full.reshape(1, blocks, n * cores * r, w)]


def fetch(src, dst, sem):
    copy = pltpu.make_async_copy(src, dst, sem)
    copy.start()
    return copy


def wait_all(copies):
    for copy in copies:
        copy.wait()


def entries(pieces):
    return sum(p.shape[0] for p in pieces)


def fetch_pieces(refs, codes, me, out, sems):
    copies = []
    for p, ref in enumerate(refs):
        r = ref.shape[2]
        for i in range(ref.shape[0]):
            if codes is None:
                row = 0
            else:
                c, s = codes[p][i]
                row = me[0] ^ s
                if any(c for code in codes for c, _ in code):
                    row = row * 2 + (me[1] ^ c)
                row = pl.multiple_of(row * r, 16)
            copies.append(fetch(ref.at[i], out.at[:, pl.ds(row, r), :], sems.at[len(copies)]))
    return copies


def by_blocks(count, outs, body):
    done = []
    for i in range(count):
        body(i)
        done += [fetch(buf.at[i], at(i), sems.at[i]) for at, buf, sems in outs]
    wait_all(done)


def dma(n):
    return pltpu.SemaphoreType.DMA((n,))


ANY = pl.BlockSpec(memory_space=pl.ANY)
IN_VMEM = pl.BlockSpec(memory_space=pltpu.VMEM)


SMEM = pl.BlockSpec(memory_space=pltpu.SMEM)

def cost(flops, byte_count):
    return pl.CostEstimate(flops=1, bytes_accessed=1, transcendentals=0)


def code_scale(k):
    return jnp.exp2(k * (1.0 / 16.0))


def code_step(top):
    return jnp.minimum(jnp.ceil(jnp.log2(jnp.maximum(top, 1e-30)) * 16.0), 2032.0)


def code_of(x, k):
    return jnp.floor(x * (LEVELS / code_scale(k)) + 0.5).astype(I32).astype(I16)


def value_of(q, k):
    return q.astype(I32).astype(F32) * (code_scale(k) * (1.0 / LEVELS))


def encode(x):
    k = code_step(jnp.max(jnp.abs(x), axis=1, keepdims=True))
    tail = jnp.pad(k[:, 0], ((0, EXTRA - x.shape[0]), (0, 0))).astype(I32).astype(I16)
    return jnp.concatenate([code_of(x, k).reshape(-1, x.shape[2]), tail], axis=0)


def decode(payload, blocks):
    q = payload[:-EXTRA].reshape(blocks, -1, payload.shape[1])
    return value_of(q, payload[-EXTRA:][:blocks, None, :].astype(F32))


def split_plain(full, bit, stride=1):
    b, n, r, w = full.shape
    view = full.reshape(b, n // (2 * stride), 2, stride, r, w)
    keep = pick(view, 2, bit).reshape(b, n // 2, r, w)
    return encode(pick(view, 2, 1 - bit).reshape(b, n // 2 * r, w)), keep


def side_of(me, bit):
    return (me[0] // bit) % 2


def put_split(block, bit, stride, send_ref, keep_ref, at):
    n, r, w = block.shape
    top = jnp.zeros((1, w), F32)
    base = [j // stride * 2 * stride + j % stride for j in range(n // 2)]
    for j in range(n // 2):
        keep_ref[at, j] = block[base[j] + stride * bit]
        top = jnp.maximum(
            top, jnp.max(jnp.abs(block[base[j] + stride * (1 - bit)]), axis=0, keepdims=True)
        )
    k = code_step(top)
    for j in range(n // 2):
        row = (at * (n // 2) + j) * r
        send_ref[row : row + r, :] = code_of(block[base[j] + stride * (1 - bit)], k)
    return k


def put_scales(send_ref, scales):
    w = send_ref.shape[1]
    row = lax.broadcasted_iota(I32, (EXTRA, w), 0)
    tail = jnp.zeros((EXTRA, w), F32)
    for i, k in enumerate(scales):
        tail = jnp.where(row == i, k, tail)
    send_ref[send_ref.shape[0] - EXTRA :, :] = tail.astype(I32).astype(I16)


def scales_of(got):
    return got[got.shape[0] - EXTRA :, :].astype(I32).astype(F32)


def part_shape(n, r):
    return (n, r) if r % 16 == 0 else (1, n * r)


def split_of(me, outs, n, r, bit, stride):
    if len(outs) == 2:
        return outs
    full = outs[0]
    return split_plain(full.reshape(full.shape[0], n, r, full.shape[-1]), side_of(me, bit), stride)


def split_shapes(blocks, n, r, w):
    if r % 16:
        return [jax.ShapeDtypeStruct((blocks, 1, n * r, w), F32)]
    return [
        jax.ShapeDtypeStruct((blocks * (n // 2) * r + EXTRA, w), I16),
        jax.ShapeDtypeStruct((blocks, n // 2, r, w), F32),
    ]


def add_split_kernel(bit, stride, me, keep_in, got, send, keep, total):
    n, r = keep_in.shape[1:3]
    given, scales = scales_of(got), []
    for i in range(keep_in.shape[0]):
        for j in range(n):
            row = (i * n + j) * r
            total[j] = keep_in[i, j] + value_of(got[row : row + r, :], given[i : i + 1])
        scales.append(put_split(total, side_of(me, bit), stride, send, keep, i))
    put_scales(send, scales)


def add_split(me, keep, got, bit, stride):
    b, n, r, w = keep.shape
    if r % 16:
        return split_plain(keep + decode(got, b).reshape(keep.shape), side_of(me, bit), stride)
    return pl.pallas_call(
        functools.partial(add_split_kernel, bit, stride),
        in_specs=[SMEM, IN_VMEM, IN_VMEM],
        out_specs=[IN_VMEM, IN_VMEM],
        out_shape=split_shapes(b, n, r, w),
        scratch_shapes=[pltpu.VMEM((n, r, w), F32)],
        compiler_params=room(8),
        cost_estimate=cost(1, 1),
        name="add_split",
    )(me, keep, got)


def after(x, *deps):
    return lax.optimization_barrier((x, deps))[0]


class Sum:
    def __init__(self, me, send, keep, bits):
        self.me = me
        self.send, self.keep, self.bits, self.done = send, keep, list(bits), []
        self.got = swap(send, "dp", self.bits[0])

    def turn(self, *deps):
        self.done.append(self.bits.pop(0))
        nxt = self.bits[0]
        stride = nxt
        for used in self.done:
            stride = stride // 2 if used < nxt else stride
        got = after(self.got, *deps) if deps else self.got
        self.send, self.keep = add_split(self.me, self.keep, got, nxt, stride)
        self.got = swap(self.send, "dp", nxt)
        return self.keep

    def turns(self, *deps):
        while len(self.bits) > 1:
            deps = (self.turn(*deps),)
        return deps


def norm_rows(sums, gain, shift, total):
    mean = sums[0:1] * (1.0 / total)
    var = sums[1:2] * (1.0 / total) - mean * mean
    rstd = lax.rsqrt(var + 1e-05)
    factor = gain * rstd
    return mean, rstd, factor, shift - mean * factor


def inverse(d):
    r = pl.reciprocal(d, approx=True)
    return r * (2.0 - d * r)


def gate(y, factor, offset):
    z = y * factor + offset
    power = jnp.minimum(y * (factor * -LOG2E) + offset * -LOG2E, 100.0)
    return z, inverse(1.0 + jnp.exp2(power))


def slope_of(z, sig):
    return sig * (1.0 + (z - z * sig))


def back_rows(back, rstd, mean, factor, total):
    d = -(factor * rstd) * (back[0:1] * (1.0 / total))
    return d, -factor * (back[1:2] * (1.0 / total)) - mean * d


def flat(x):
    return x.reshape(-1, x.shape[-1])


def add_sums(sums, one, two):
    sums[0:1] += jnp.sum(one, axis=0, keepdims=True)
    sums[1:2] += jnp.sum(two, axis=0, keepdims=True)


def first_kernel(codes, count, me, x, *refs):
    pieces, (y, sums, weights, p_sem) = refs[:count], refs[count:]
    copies = fetch_pieces(pieces, codes, me, weights, p_sem)
    sums[...] = jnp.zeros_like(sums)
    wait_all(copies)
    for k in range(SIDE):
        out = jnp.dot(x[k], weights[...].reshape(-1, C_MID), preferred_element_type=F32)
        y[k] = out
        add_sums(sums, out, out * out)


def first_forward(me, x, pieces, codes):
    rows = x.shape[1]
    return pl.pallas_call(
        functools.partial(first_kernel, codes, len(pieces)),
        in_specs=[SMEM, IN_VMEM] + [ANY] * len(pieces),
        out_specs=[IN_VMEM, IN_VMEM],
        out_shape=[
            jax.ShapeDtypeStruct((SIDE, rows, C_MID), F32), jax.ShapeDtypeStruct((2, C_MID), F32),
        ],
        scratch_shapes=[
            pltpu.VMEM((C_IN // C_MID, C_MID, C_MID), BF), dma(entries(pieces)),
        ],
        compiler_params=room(8),
        cost_estimate=cost(1, 1),
        name="first_forward",
    )(me, x, *pieces)


def clear_border(pad):
    zero = jnp.zeros(pad.shape[1:], pad.dtype)
    pad[0] = zero
    pad[SIDE + 1] = zero
    for k in range(1, SIDE + 1):
        pad[k, 0] = zero[0]
        pad[k, SIDE + 1] = zero[0]


def second_kernel(codes, count, total, me, y1, sums1, params, *refs):
    pieces, (h1, y2, sums2, taps, pad, p_sem) = refs[:count], refs[count:]
    batch = pad.shape[2]
    copies = fetch_pieces(pieces, codes, me, taps, p_sem)
    clear_border(pad)
    sums2[...] = jnp.zeros_like(sums2)
    _, _, factor, offset = norm_rows(sums1[...], params[0:1], params[1:2], total)

    def act(k):
        z, sig = gate(y1[k], factor, offset)
        h = (z * sig).astype(BF).reshape(SIDE, batch, C_MID)
        pad[k + 1, 1 : SIDE + 1] = h
        h1[k] = h

    act(0)
    act(1)
    wait_all(copies)
    for k in range(SIDE):
        out = None
        for a in range(3):
            if 0 <= k + a - 1 < SIDE:
                patch = jnp.concatenate([flat(pad[k + a, b : b + SIDE]) for b in range(3)], axis=1)
                part = jnp.dot(
                    patch, taps[3 * a : 3 * a + 3].reshape(3 * C_MID, C_MID),
                    preferred_element_type=F32,
                )
                out = part if out is None else out + part
        if k + 2 < SIDE:
            act(k + 2)
        y2[k] = out
        add_sums(sums2, out, out * out)


def second_forward(me, y1, sums1, params, pieces, codes, total):
    rows = y1.shape[1]
    batch = rows // SIDE
    return pl.pallas_call(
        functools.partial(second_kernel, codes, len(pieces), total),
        in_specs=[SMEM, IN_VMEM, IN_VMEM, IN_VMEM] + [ANY] * len(pieces),
        out_specs=[IN_VMEM] * 4,
        out_shape=[
            jax.ShapeDtypeStruct((SIDE, SIDE, batch, C_MID), BF),
            jax.ShapeDtypeStruct(y1.shape, F32),
            jax.ShapeDtypeStruct((2, C_MID), F32),
            jax.ShapeDtypeStruct((9, C_MID, C_MID), BF),
        ],
        scratch_shapes=[
            pltpu.VMEM((SIDE + 2, SIDE + 2, batch, C_MID), BF), dma(entries(pieces)),
        ],
        compiler_params=room(12),
        cost_estimate=cost(1, 1),
        name="second_forward",
    )(me, y1, sums1, params, *pieces)


def head_kernel(codes, count, outs_n, total, group_images, me, y2, sums2, params, bias, labels, *refs):
    pieces, refs = refs[:count], refs[count:]
    outs, (packed, dpool_out, head, block, p_sem) = refs[:outs_n], refs[outs_n:]
    batch = dpool_out.shape[0]
    copies = fetch_pieces(pieces, codes, me, head, p_sem)
    mean, rstd, factor, offset = norm_rows(sums2[...], params[2:3], params[3:4], total)
    sum_h = sum_a = sum_b = jnp.zeros((batch, C_MID), F32)
    fold = lambda v: jnp.sum(v.reshape(SIDE, batch, C_MID), axis=0)
    for k in range(SIDE):
        z, sig = gate(y2[k], factor, offset)
        slope = slope_of(z, sig)
        sum_h = sum_h + fold(z * sig)
        sum_a = sum_a + fold(slope)
        sum_b = sum_b + fold(slope * ((y2[k] - mean) * rstd))
    wait_all(copies)
    pooled = (sum_h * (1.0 / PIX)).astype(BF)
    logits = jnp.concatenate(
        [jnp.dot(pooled, head[k], preferred_element_type=F32) for k in range(2)], axis=1
    )
    logits = logits + bias[...]
    column = lax.broadcasted_iota(I32, (batch, WIDE), 1)
    logits = jnp.where(column < CLASSES, logits, -1e30)
    across = lax.broadcasted_iota(I32, (batch, batch), 0) == lax.broadcasted_iota(I32, (batch, batch), 1)
    label = jnp.sum(jnp.where(across, labels[...], 0), axis=1, keepdims=True)
    onehot = (label == column).astype(F32)
    top = jnp.max(logits, axis=1, keepdims=True)
    expo = jnp.exp(logits - top)
    expsum = jnp.sum(expo, axis=1, keepdims=True)
    lse = top + jnp.log(expsum)
    loss = jnp.sum(lse - jnp.sum(logits * onehot, axis=1, keepdims=True), axis=0, keepdims=True)
    dlogits = ((jnp.exp(logits - lse) - onehot) * (1.0 / group_images)).astype(BF)
    bias_sum = jnp.sum(dlogits.astype(F32), axis=0, keepdims=True)
    last = lax.broadcasted_iota(I32, (1, WIDE), 1) == WIDE - 1
    bias_sum = jnp.where(last, loss, bias_sum)
    dpool = jnp.zeros((batch, C_MID), F32)
    for k in range(2):
        part = dlogits[:, k * C_MID : (k + 1) * C_MID]
        dpool = dpool + lax.dot_general(
            part, head[k], (((1,), (1,)), ((), ())), preferred_element_type=F32
        )

    def make(k):
        block[...] = lax.dot_general(
            pooled, dlogits[:, k * C_MID : (k + 1) * C_MID], (((0,), (0,)), ((), ())),
            preferred_element_type=F32,
        ).reshape(block.shape)

    emit_all(2, make, block, me, 1, outs)
    dpool = dpool * (1.0 / PIX)
    dpool_out[...] = dpool
    packed[0:1] = jnp.sum(dpool * sum_b, axis=0, keepdims=True)
    packed[1:2] = jnp.sum(dpool * sum_a, axis=0, keepdims=True)
    packed[2:3] = bias_sum[:, :C_MID]
    packed[3:4] = bias_sum[:, C_MID:]


def head_step(me, y2, sums2, params, bias, labels, pieces, codes, total, group_images, n, r):
    rows = y2.shape[1]
    batch = rows // SIDE
    shapes = split_shapes(2, n, r, C_MID)
    return pl.pallas_call(
        functools.partial(head_kernel, codes, len(pieces), len(shapes), total, group_images),
        in_specs=[SMEM] + [IN_VMEM] * 5 + [ANY] * len(pieces),
        out_specs=[IN_VMEM] * (2 + len(shapes)),
        out_shape=shapes + [
            jax.ShapeDtypeStruct((4, C_MID), F32), jax.ShapeDtypeStruct((batch, C_MID), F32),
        ],
        scratch_shapes=[
            pltpu.VMEM((2, C_MID, C_MID), BF), pltpu.VMEM(part_shape(n, r) + (C_MID,), F32),
            dma(entries(pieces)),
        ],
        compiler_params=room(8),
        cost_estimate=cost(1, 1),
        name="head_step",
    )(me, y2, sums2, params, bias, labels, *pieces)


def emit_all(count, make, block, me, bit, outs):
    scales = []
    for i in range(count):
        make(i)
        if len(outs) == 1:
            outs[0][i] = block[...]
        else:
            scales.append(put_split(block, side_of(me, bit), bit, *outs, i))
    if scales:
        put_scales(outs[0], scales)


def one_tap(tap, pad, turned, block):
    a, b = tap // 3, tap % 3
    moved = pad[2 - a : 2 - a + SIDE, 2 - b : 2 - b + SIDE].reshape(-1, C_MID)
    block[...] = jnp.dot(turned[...], moved, preferred_element_type=F32).reshape(block.shape)


def taps_kernel(total, bits, me, y2, sums2, back, params, dpool, h1, pad, turned, *refs):
    outs, block = refs[:-1], refs[-1]
    batch = pad.shape[2]
    clear_border(pad)
    mean, rstd, factor, offset = norm_rows(sums2[...], params[2:3], params[3:4], total)
    d, e = back_rows(back, rstd, mean, factor, total)
    scaled = (dpool[...] * factor)[None]
    turned[...] = h1[...].reshape(-1, C_MID).T
    for k in range(SIDE):
        z, sig = gate(y2[k], factor, offset)
        dz = flat(slope_of(z, sig).reshape(SIDE, batch, C_MID) * scaled)
        dy = dz + (y2[k] * d + e)
        pad[k + 1, 1 : SIDE + 1] = dy.astype(BF).reshape(SIDE, batch, C_MID)
    each, first = len(outs) // len(bits), 0
    for k, bit in enumerate(bits):
        some = outs[k * each : (k + 1) * each]
        make = lambda i, first=first: one_tap(first + i, pad, turned, block)
        emit_all(some[-1].shape[0], make, block, me, bit, some)
        first += some[-1].shape[0]


def taps_more_kernel(first_tap, me, pad, turned, *refs):
    outs, block = refs[:-1], refs[-1]
    make = lambda i: one_tap(i + first_tap, pad, turned, block)
    emit_all(outs[-1].shape[0], make, block, me, 1, outs)


def taps_grad_first(me, y2, sums2, back, params, dpool, h1, total, n, r, counts, bits):
    batch = h1.shape[2]
    shapes = [v for count in counts for v in split_shapes(count, n, r, C_MID)]
    return pl.pallas_call(
        functools.partial(taps_kernel, total, bits),
        in_specs=[SMEM] + [IN_VMEM] * 6,
        out_specs=[IN_VMEM] * (2 + len(shapes)),
        out_shape=[
            jax.ShapeDtypeStruct((SIDE + 2, SIDE + 2, batch, C_MID), BF),
            jax.ShapeDtypeStruct((C_MID, SIDE * SIDE * batch), BF),
        ] + shapes,
        scratch_shapes=[pltpu.VMEM(part_shape(n, r) + (C_MID,), F32)],
        compiler_params=room(8),
        cost_estimate=cost(1, 1),
        name="taps_grad_first",
    )(me, y2, sums2, back, params, dpool, h1)


def taps_grad_more(me, pad, turned, n, r, first_tap, count):
    shapes = split_shapes(count, n, r, C_MID)
    return pl.pallas_call(
        functools.partial(taps_more_kernel, first_tap),
        in_specs=[SMEM, IN_VMEM, IN_VMEM],
        out_specs=[IN_VMEM] * len(shapes),
        out_shape=shapes,
        scratch_shapes=[pltpu.VMEM(part_shape(n, r) + (C_MID,), F32)],
        compiler_params=room(8),
        cost_estimate=cost(1, 1),
        name="taps_grad_more",
    )(me, pad, turned)


def input_grad_kernel(total, pad, y1, sums1, params, taps, dz1, sums):
    sums[...] = jnp.zeros_like(sums)
    mean, rstd, factor, offset = norm_rows(sums1[...], params[0:1], params[1:2], total)
    for k in range(SIDE):
        dh = None
        for a in range(3):
            for b in range(3):
                if 0 <= k + 1 - a < SIDE:
                    part = lax.dot_general(
                        flat(pad[k + 2 - a, 2 - b : 2 - b + SIDE]), taps[3 * a + b],
                        (((1,), (1,)), ((), ())), preferred_element_type=F32,
                    )
                    dh = part if dh is None else dh + part
        dz = dh * slope_of(*gate(y1[k], factor, offset))
        dz1[k] = dz
        add_sums(sums, dz * ((y1[k] - mean) * rstd), dz)


def input_grad(pad, y1, sums1, params, taps, total):
    return pl.pallas_call(
        functools.partial(input_grad_kernel, total),
        in_specs=[IN_VMEM] * 5,
        out_specs=[IN_VMEM] * 2,
        out_shape=[jax.ShapeDtypeStruct(y1.shape, F32), jax.ShapeDtypeStruct((2, C_MID), F32)],
        compiler_params=room(8),
        cost_estimate=cost(1, 1),
        name="input_grad",
    )(pad, y1, sums1, params, taps)


def one_first(x, dy, at, block):
    block[...] = lax.dot_general(
        flat(x[:, :, at * C_MID : (at + 1) * C_MID]), flat(dy[...]), (((0,), (0,)), ((), ())),
        preferred_element_type=F32,
    ).reshape(block.shape)


def first_grad_kernel(total, me, dz1, y1, sums1, back, params, x, dy, *refs):
    outs, block = refs[:-1], refs[-1]
    mean, rstd, factor, _ = norm_rows(sums1[...], params[0:1], params[1:2], total)
    d, e = back_rows(back, rstd, mean, factor, total)
    for k in range(SIDE):
        dy[k] = (dz1[k] * factor + (y1[k] * d + e)).astype(BF)
    emit_all(outs[-1].shape[0], lambda i: one_first(x, dy, i, block), block, me, 1, outs)


def first_more_kernel(bit, first, me, x, dy, *refs):
    outs, block = refs[:-1], refs[-1]
    make = lambda i: one_first(x, dy, first + i, block)
    emit_all(outs[-1].shape[0], make, block, me, bit, outs)


def first_grad_first(me, dz1, y1, sums1, back, params, x, total, n, r, count):
    shapes = split_shapes(count, n, r, C_MID)
    return pl.pallas_call(
        functools.partial(first_grad_kernel, total),
        in_specs=[SMEM] + [IN_VMEM] * 6,
        out_specs=[IN_VMEM] * (1 + len(shapes)),
        out_shape=[jax.ShapeDtypeStruct(y1.shape, BF)] + shapes,
        scratch_shapes=[pltpu.VMEM(part_shape(n, r) + (C_MID,), F32)],
        compiler_params=room(8),
        cost_estimate=cost(1, 1),
        name="first_grad_first",
    )(me, dz1, y1, sums1, back, params, x)


def first_grad_more(me, bit, x, dy, n, r, first_block, count):
    shapes = split_shapes(count, n, r, C_MID)
    return pl.pallas_call(
        functools.partial(first_more_kernel, bit, first_block),
        in_specs=[SMEM, IN_VMEM, IN_VMEM],
        out_specs=[IN_VMEM] * len(shapes),
        out_shape=shapes,
        scratch_shapes=[pltpu.VMEM(part_shape(n, r) + (C_MID,), F32)],
        compiler_params=room(8),
        cost_estimate=cost(1, 1),
        name="first_grad_more",
    )(me, x, dy)


def adamw(weight, grad, first, second, rate):
    first = 0.9 * first + 0.1 * grad
    second = 0.999 * second + 0.001 * grad * grad
    normal_step = first / (1.0 - 0.9**STEP) / (jnp.sqrt(second / (1.0 - 0.999**STEP)) + 1e-08)
    return (-rate * (normal_step + 0.01 * weight), first, second)


def outer_step(start, step_sum, momentum, groups):
    delta = -(step_sum / groups)
    momentum = 0.9 * momentum + delta
    return (start - 0.7 * (delta + 0.9 * momentum), momentum)


def rep_sum(x):
    for bit in bits_of("rep"):
        low = x.astype(BF)
        x = low.astype(F32) + swap(low, "rep", bit).astype(F32)
    return x


def finish_kernel(n_parts, at, before, *refs):
    parts, state, refs = refs[:n_parts], refs[n_parts : n_parts + 5], refs[n_parts + 5 + before :]
    outs, (low, *refs) = refs[:3], refs[3:]
    bufs, sems = refs[:3], refs[3:]
    given = scales_of(parts[1]) if n_parts == 2 else None

    def body(i):
        if n_parts == 2:
            keep, got = parts
            r = keep.shape[2]
            owned = keep[i, 0] + value_of(got[i * r : (i + 1) * r, :], given[i : i + 1])
        else:
            owned = parts[0][i]
        weight, mask, rank = (ref[at + i] for ref in state[:3])
        first, second = (ref[0, at + i] for ref in state[3:])
        bufs[2][i] = mask_of(mask, rank)
        old, new = masks(mask, rank)
        effective = weight * old
        kept = old * new
        dense = owned + 5e-05 * effective
        step, m, v = adamw(weight * kept, new * dense, first * kept, second * kept, 0.03)
        bufs[0][i] = m * new
        bufs[1][i] = v * new
        low[i] = (step * new).astype(BF)

    here = lambda ref: lambda i: ref.at[at + i]
    here_rep = lambda ref: lambda i: ref.at[0, at + i]
    wheres = (here_rep, here_rep, here)
    by_blocks(low.shape[0], [(f(ref), *two) for f, ref, *two in zip(wheres, outs, bufs, sems)], body)


def mask_of(old, rank):
    return jnp.where(rank < DROP_CUT, 0, jnp.where(rank >= GROW_CUT, 1, old))


def masks(old, rank):
    return old.astype(F32), mask_of(old, rank).astype(F32)


def finish(parts, state, before, at, count):
    shard, w = state[0].shape[1:]
    own = lambda t: pltpu.VMEM((count, shard, w), t)
    n_in = len(parts) + 5
    return pl.pallas_call(
        functools.partial(finish_kernel, len(parts), at, len(before)),
        in_specs=[IN_VMEM] * n_in + [ANY] * len(before),
        out_specs=[ANY, ANY, ANY, IN_VMEM],
        out_shape=[
            jax.ShapeDtypeStruct(state[3].shape, F32), jax.ShapeDtypeStruct(state[4].shape, F32),
            jax.ShapeDtypeStruct(state[1].shape, I32),
            jax.ShapeDtypeStruct((count, shard, w), BF),
        ],
        input_output_aliases={n_in + k: k for k in range(len(before))},
        scratch_shapes=[own(F32), own(F32), own(I32)] + [dma(count)] * 3,
        compiler_params=room(12),
        cost_estimate=cost(1, 1),
        name="finish",
    )(*parts, *state, *before)


def outer_kernel(groups, at, before, low, got, *refs):
    state, refs = refs[:4], refs[4 + before :]
    outs, bufs, sems = refs[:2], refs[2:4], refs[4:]

    def body(i):
        weight, mask, rank, momentum = (ref[at + i] for ref in state)
        old, new = masks(mask, rank)
        total = low[i].astype(F32) + got[i].astype(F32)
        value, mom = outer_step(weight * (old * new), total, momentum, groups)
        bufs[0][i] = value * new
        bufs[1][i] = mom * new

    here = lambda ref: lambda i: ref.at[at + i]
    by_blocks(low.shape[0], [(here(ref), *two) for ref, *two in zip(outs, bufs, sems)], body)


def outer(low, got, state, before, at, groups):
    return pl.pallas_call(
        functools.partial(outer_kernel, groups, at, len(before)),
        in_specs=[IN_VMEM] * 6 + [ANY] * len(before),
        out_specs=[ANY, ANY],
        out_shape=[jax.ShapeDtypeStruct(state[0].shape, F32)] * 2,
        input_output_aliases={6 + k: k for k in range(len(before))},
        scratch_shapes=[pltpu.VMEM(low.shape, F32)] * 2 + [dma(low.shape[0])] * 2,
        compiler_params=room(12),
        cost_estimate=cost(1, 1),
        name="outer",
    )(low, got, *state, *before)


def per_device(
    images, labels, conv_weight, conv_mask, conv_rank, head_weight, norm_params, head_bias,
    conv_first, conv_second, head_first, head_second, norm_first, norm_second, bias_first,
    bias_second, conv_outer, head_outer, norm_outer, bias_outer,
):
    devices = lax.axis_size("dp")
    groups = lax.axis_size("rep")
    width = C_MID
    blocks = C_IN // C_MID
    core = lax.axis_index("rep") % 2
    dp = lax.axis_index("dp")
    me = jnp.stack([dp, core]).astype(I32)
    bits = bits_of("dp")
    shard = conv_weight.shape[1]
    batch = images.shape[0]
    rows = batch * PIX
    total = float(rows * devices)
    group_images = batch * devices
    half = shard // 2

    def mine(x):
        return pick(x.reshape(-1, 2, half, width), 1, core)

    def active(sl):
        return jnp.where(mine(conv_mask[sl]) == 1, mine(conv_weight[sl]), 0.0).astype(BF)

    head_wide = jnp.pad(head_weight.astype(BF), ((0, 0), (0, WIDE - CLASSES)))
    head_low = mine(head_wide.reshape(shard, 2, width).transpose(1, 0, 2))
    taps_low = active(slice(blocks, None))
    get_first = Gather(active(slice(0, blocks))).start()
    get_first.join()
    get_taps = Gather(after(taps_low, get_first.own)).start()
    get_first.own = after(get_first.own, taps_low)
    get_first.turn_near()
    get_first.turn_side()
    get_first.turn_far()
    first_pieces, first_codes = get_first.finish()
    fine = first_codes is not None
    classes = labels.reshape(1, batch)
    x = images.transpose(1, 2, 0, 3).reshape(SIDE, SIDE * batch, C_IN)
    y_one, sums_one = first_forward(me, x, first_pieces, first_codes)
    head_got = gather_more(after(head_low, y_one)[None], [0], bits[0])
    sums_one = sums_one + swap(sums_one, "dp", bits[0])
    get_taps.join(sums_one, head_got[0])
    get_taps.turn_near()
    get_taps.turn_side()
    get_taps.turn_far(get_taps.side)
    for bit in bits[1:]:
        sums_one = sums_one + swap(sums_one, "dp", bit)
    taps_pieces, taps_codes = get_taps.finish(sums_one)
    buf, rel = after(head_got[0], get_taps.near), head_got[1]
    head_more = swap(buf, "dp", bits[-1])
    h_one, y_two, sums_two, taps = second_forward(
        me, y_one, sums_one, norm_params, taps_pieces, taps_codes, total
    )
    buf = jnp.concatenate([buf, after(head_more, sums_two)], axis=0)
    rel = rel + [code ^ bits[-1] for code in rel]
    for bit in reversed(bits[2:-1]):
        buf, rel = gather_more(buf, rel, bit)
    head_more = swap(buf, "dp", bits[1])
    for bit in bits[:-1]:
        sums_two = sums_two + swap(sums_two, "dp", bit)
    buf = jnp.concatenate([buf, after(head_more, sums_two)], axis=0)
    rel = rel + [code ^ bits[1] for code in rel]
    head_pieces, head_codes = [buf, swap(buf, "rep", 1)], [[(c, r) for r in rel] for c in range(2)]
    if not fine:
        head_pieces, head_codes = place(head_pieces, head_codes), None
    sums_two = sums_two + swap(sums_two, "dp", bits[-1])
    bias_wide = jnp.pad(head_bias, (0, WIDE - CLASSES)).reshape(1, WIDE)
    *outs, packed, dpool = head_step(
        me, y_two, sums_two, norm_params, bias_wide, classes, head_pieces, head_codes, total,
        group_images, devices, shard,
    )
    n, r = devices, shard
    sum_head = Sum(me, *split_of(me, outs, n, r, 1, 1), bits)
    packed = sum_all(packed, "dp")
    cut = 5
    dpool = after(dpool, sum_head.turn(packed))
    pad, turned, *outs = taps_grad_first(
        me, y_two, sums_two, packed, norm_params, dpool, h_one, total, n, r, (cut,), bits[:1]
    )
    sum_a = Sum(me, *split_of(me, outs, n, r, 1, 1), bits)
    pad = after(pad, outs[0])
    dz_one, back_one = input_grad(pad, y_one, sums_one, norm_params, taps, total)
    turned = after(turned, dz_one)
    outs = taps_grad_more(me, pad, turned, n, r, cut, 9 - cut)
    back_one = sum_all(back_one, "dp", sum_head.turn(outs[0]))
    send, keep = split_of(me, outs, n, r, 1, 1)
    sum_b = Sum(me, after(send, back_one), keep, bits)
    last = sum_a.turn(back_one)
    dy_one, *outs = first_grad_first(
        me, dz_one, y_one, sums_one, after(back_one, last), norm_params, x, total, n, r, 2
    )
    sum_c = Sum(me, *split_of(me, outs, n, r, 1, 1), bits)
    outs = first_grad_more(me, 1, x, after(dy_one, outs[0]), n, r, 2, 2)
    sum_d = Sum(me, *split_of(me, outs, n, r, 1, 1), bits)
    state = (conv_weight, conv_mask, conv_rank, conv_first, conv_second)
    rep_bits = bits_of("rep")
    results, new = (), ()

    def close(one, at, *deps):
        one.turns()
        keep = after(one.keep, *deps)
        parts = (keep, one.got) if fine else (keep[:, 0] + decode(one.got, keep.shape[0]),)
        *both, low = finish(parts, state, results, at, keep.shape[0])
        return both, low

    def to_groups(low):
        for b in rep_bits[:-1]:
            low = (low.astype(F32) + swap(low, "rep", b).astype(F32)).astype(BF)
        return low, swap(low, "rep", rep_bits[-1])

    last = sum_a.turn(*sum_head.turns(outs[0]))
    last = sum_b.turn(last)
    last = sum_c.turn(last)
    results, low_a = close(sum_a, blocks, last)
    last = sum_b.turn(low_a)
    last = sum_d.turn(last)
    last = sum_c.turn(last)
    low_a, got_a = to_groups(low_a)
    last = sum_d.turn(last, got_a)
    results, low_b = close(sum_b, blocks + cut, last)
    results, low_c = close(sum_c, 0, low_b)
    results, low_d = close(sum_d, 2, low_c)
    low_b, got_b = to_groups(low_b)
    low_c, got_c = to_groups(jnp.concatenate([low_c, low_d], axis=0))
    back_one, packed = after((back_one, packed), low_a)
    bias_grad = packed[2:].reshape(-1)[:CLASSES]
    loss_sum = packed[3, C_MID - 1 :]
    head_grad = after(sum_head.keep, low_a)[:, 0] + decode(sum_head.got, 2)
    head_grad = head_grad.transpose(1, 0, 2).reshape(shard, WIDE)[:, :CLASSES]
    for low, got, at in ((low_a, got_a, blocks), (low_b, got_b, blocks + cut), (low_c, got_c, 0)):
        new = outer(low, got, state[:3] + (conv_outer,), new, at, groups)
    (conv_m, conv_v, mask_int), (conv_new, conv_mom) = results, new
    norm_grad = jnp.concatenate([back_one, packed[:2]], axis=0)
    head_s, head_m, head_v = adamw(head_weight, head_grad, head_first[0], head_second[0], 0.03)
    head_new, head_mom = outer_step(head_weight, rep_sum(head_s), head_outer, groups)
    norm_s, norm_m, norm_v = adamw(norm_params, norm_grad, norm_first[0], norm_second[0], 0.3)
    bias_s, bias_m, bias_v = adamw(head_bias, bias_grad, bias_first[0], bias_second[0], 0.3)
    wide = jnp.pad(bias_s, (0, WIDE - CLASSES)).reshape(2, width)
    small = jnp.pad(norm_s, ((0, 2), (0, 0))) + jnp.pad(wide, ((4, 0), (0, 0)))
    small = sum_all(small, "rep")
    norm_new, norm_mom = outer_step(norm_params, small[:4], norm_outer, groups)
    bias_new, bias_mom = outer_step(head_bias, small[4:].reshape(-1)[:CLASSES], bias_outer, groups)
    return (
        conv_new, mask_int, conv_m, conv_v, conv_mom,
        head_new, head_m[None], head_v[None], head_mom,
        norm_new, norm_m[None], norm_v[None], norm_mom,
        bias_new, bias_m[None], bias_v[None], bias_mom, loss_sum,
    )
def solution(mesh):
    conv = P(None, "dp", None)
    conv_rep = P("rep", None, "dp", None)
    head = P("dp", None)
    head_rep = P("rep", "dp", None)
    in_specs = (
        P(("rep", "dp"), None, None, None), P(("rep", "dp")), conv, conv, conv, head, P(), P(),
        conv_rep, conv_rep, head_rep, head_rep, P("rep", None, None), P("rep", None, None),
        P("rep", None), P("rep", None), conv, head, P(), P(),
    )
    out_specs = (
        conv, conv, conv_rep, conv_rep, conv, head, head_rep, head_rep, head,
        P(), P("rep", None, None), P("rep", None, None), P(),
        P(), P("rep", None), P("rep", None), P(), P("rep"),
    )
    return jax.shard_map(
        per_device, mesh=mesh, in_specs=in_specs, out_specs=out_specs, check_vma=False
    )
```

```python
import functools

import jax
import jax.numpy as jnp
from jax import lax
from jax.experimental import pallas as pl
from jax.experimental.pallas import tpu as pltpu
from jax.sharding import PartitionSpec as P

C_IN = 2048
C_MID = 512
CLASSES = 1000
WIDE = 1024
SIDE = 7
STEP = 10
PIX = 49
DROP_CUT = 78643
GROW_CUT = 242484
BF = jnp.bfloat16
F32 = jnp.float32
I32 = jnp.int32
I16 = jnp.int16
EXTRA = 16
LEVELS = 32000.0
LOG2E = 1.4426950408889634


def swap(x, axis, bit):
    n = lax.axis_size(axis)
    return lax.ppermute(x, axis, [(i, i ^ bit) for i in range(n)])


def bits_of(axis):
    n = lax.axis_size(axis)
    return [1 << k for k in range(n.bit_length() - 1)]


def sum_all(x, axis, *deps):
    bits = bits_of(axis)
    bits = bits[1:] + bits[:1]
    for bit in bits:
        if deps and bit == bits[-1]:
            x = after(x, *deps)
        x = x + swap(x, axis, bit)
    return x


def room(mib):
    return pltpu.CompilerParams(vmem_limit_bytes=mib * 1024 * 1024)


def pick(x, axis, index):
    return lax.dynamic_index_in_dim(x, index, axis, keepdims=False)


def gather_more(buf, rel, bit, *deps):
    buf = after(buf, *deps) if deps else buf
    return jnp.concatenate([buf, swap(buf, "dp", bit)], axis=0), rel + [r ^ bit for r in rel]


class Gather:
    def __init__(self, own):
        self.own, self.rel = own[None], [0]
        self.got = None

    def start(self):
        for bit in reversed(bits_of("dp")[2:]):
            self.join()
            self.got = swap(self.own, "dp", bit)
            self.rel = self.rel + [r ^ bit for r in self.rel]
        return self

    def join(self, *deps):
        if self.got is not None:
            got = after(self.got, *deps) if deps else self.got
            self.own, self.got = jnp.concatenate([self.own, got], axis=0), None

    def turn_near(self, *deps):
        self.join()
        own = after(self.own, *deps) if deps else self.own
        self.near = swap(own, "dp", bits_of("dp")[1])

    def turn_side(self, *deps):
        own = after(self.own, *deps) if deps else self.own
        self.side = swap(own, "dp", bits_of("dp")[0])

    def turn_far(self, *deps):
        near = after(self.near, *deps) if deps else self.near
        self.far = swap(near, "dp", bits_of("dp")[0])

    def finish(self, *deps):
        bits = bits_of("dp")
        far = after(self.far, *deps) if deps else self.far
        pieces = [self.own, self.near, self.side, far]
        shifts = [0, bits[1], bits[0], bits[1] | bits[0]]
        codes = [[(0, r ^ s) for r in self.rel] for s in shifts]
        pieces += [swap(p, "rep", 1) for p in pieces]
        codes += [[(1, r) for _, r in c] for c in codes]
        if self.own.shape[2] % 16:
            return place(pieces, codes), None
        return pieces, codes


def place(pieces, codes):
    n = lax.axis_size("dp")
    flat = [c * n + r for code in codes for c, r in code]
    cores = len(flat) // n
    inverse = jnp.array([flat.index(k) for k in range(len(flat))], I32)
    me = (lax.axis_index("rep") % cores) * n + lax.axis_index("dp")
    where = inverse[jnp.arange(len(flat), dtype=I32) ^ me]
    full = jnp.take(jnp.concatenate(pieces, axis=0), where, axis=0)
    _, blocks, r, w = full.shape
    full = full.reshape(cores, n, blocks, r, w).transpose(2, 1, 0, 3, 4)
    return [full.reshape(1, blocks, n * cores * r, w)]


def fetch(src, dst, sem):
    copy = pltpu.make_async_copy(src, dst, sem)
    copy.start()
    return copy


def wait_all(copies):
    for copy in copies:
        copy.wait()


def entries(pieces):
    return sum(p.shape[0] for p in pieces)


def fetch_pieces(refs, codes, me, out, sems):
    copies = []
    for p, ref in enumerate(refs):
        r = ref.shape[2]
        for i in range(ref.shape[0]):
            if codes is None:
                row = 0
            else:
                c, s = codes[p][i]
                row = me[0] ^ s
                if any(c for code in codes for c, _ in code):
                    row = row * 2 + (me[1] ^ c)
                row = pl.multiple_of(row * r, 16)
            copies.append(fetch(ref.at[i], out.at[:, pl.ds(row, r), :], sems.at[len(copies)]))
    return copies


def by_blocks(count, outs, body):
    done = []
    for i in range(count):
        body(i)
        done += [fetch(buf.at[i], at(i), sems.at[i]) for at, buf, sems in outs]
    wait_all(done)


def dma(n):
    return pltpu.SemaphoreType.DMA((n,))


ANY = pl.BlockSpec(memory_space=pl.ANY)
IN_VMEM = pl.BlockSpec(memory_space=pltpu.VMEM)


SMEM = pl.BlockSpec(memory_space=pltpu.SMEM)

def cost(flops, byte_count):
    return pl.CostEstimate(flops=1, bytes_accessed=1, transcendentals=0)


def code_scale(k):
    return jnp.exp2(k * (1.0 / 16.0))


def code_step(top):
    return jnp.minimum(jnp.ceil(jnp.log2(jnp.maximum(top, 1e-30)) * 16.0), 2032.0)


def code_of(x, k):
    return jnp.floor(x * (LEVELS / code_scale(k)) + 0.5).astype(I32).astype(I16)


def value_of(q, k):
    return q.astype(I32).astype(F32) * (code_scale(k) * (1.0 / LEVELS))


def encode(x):
    k = code_step(jnp.max(jnp.abs(x), axis=1, keepdims=True))
    tail = jnp.pad(k[:, 0], ((0, EXTRA - x.shape[0]), (0, 0))).astype(I32).astype(I16)
    return jnp.concatenate([code_of(x, k).reshape(-1, x.shape[2]), tail], axis=0)


def decode(payload, blocks):
    q = payload[:-EXTRA].reshape(blocks, -1, payload.shape[1])
    return value_of(q, payload[-EXTRA:][:blocks, None, :].astype(F32))


def split_plain(full, bit, stride=1):
    b, n, r, w = full.shape
    view = full.reshape(b, n // (2 * stride), 2, stride, r, w)
    keep = pick(view, 2, bit).reshape(b, n // 2, r, w)
    return encode(pick(view, 2, 1 - bit).reshape(b, n // 2 * r, w)), keep


def side_of(me, bit):
    return (me[0] // bit) % 2


def put_split(block, bit, stride, send_ref, keep_ref, at):
    n, r, w = block.shape
    top = jnp.zeros((1, w), F32)
    base = [j // stride * 2 * stride + j % stride for j in range(n // 2)]
    for j in range(n // 2):
        keep_ref[at, j] = block[base[j] + stride * bit]
        top = jnp.maximum(
            top, jnp.max(jnp.abs(block[base[j] + stride * (1 - bit)]), axis=0, keepdims=True)
        )
    k = code_step(top)
    for j in range(n // 2):
        row = (at * (n // 2) + j) * r
        send_ref[row : row + r, :] = code_of(block[base[j] + stride * (1 - bit)], k)
    return k


def put_scales(send_ref, scales):
    w = send_ref.shape[1]
    row = lax.broadcasted_iota(I32, (EXTRA, w), 0)
    tail = jnp.zeros((EXTRA, w), F32)
    for i, k in enumerate(scales):
        tail = jnp.where(row == i, k, tail)
    send_ref[send_ref.shape[0] - EXTRA :, :] = tail.astype(I32).astype(I16)


def scales_of(got):
    return got[got.shape[0] - EXTRA :, :].astype(I32).astype(F32)


def part_shape(n, r):
    return (n, r) if r % 16 == 0 else (1, n * r)


def split_of(me, outs, n, r, bit, stride):
    if len(outs) == 2:
        return outs
    full = outs[0]
    return split_plain(full.reshape(full.shape[0], n, r, full.shape[-1]), side_of(me, bit), stride)


def split_shapes(blocks, n, r, w):
    if r % 16:
        return [jax.ShapeDtypeStruct((blocks, 1, n * r, w), F32)]
    return [
        jax.ShapeDtypeStruct((blocks * (n // 2) * r + EXTRA, w), I16),
        jax.ShapeDtypeStruct((blocks, n // 2, r, w), F32),
    ]


def add_split_kernel(bit, stride, me, keep_in, got, send, keep, total):
    n, r = keep_in.shape[1:3]
    given, scales = scales_of(got), []
    for i in range(keep_in.shape[0]):
        for j in range(n):
            row = (i * n + j) * r
            total[j] = keep_in[i, j] + value_of(got[row : row + r, :], given[i : i + 1])
        scales.append(put_split(total, side_of(me, bit), stride, send, keep, i))
    put_scales(send, scales)


def add_split(me, keep, got, bit, stride):
    b, n, r, w = keep.shape
    if r % 16:
        return split_plain(keep + decode(got, b).reshape(keep.shape), side_of(me, bit), stride)
    return pl.pallas_call(
        functools.partial(add_split_kernel, bit, stride),
        in_specs=[SMEM, IN_VMEM, IN_VMEM],
        out_specs=[IN_VMEM, IN_VMEM],
        out_shape=split_shapes(b, n, r, w),
        scratch_shapes=[pltpu.VMEM((n, r, w), F32)],
        compiler_params=room(8),
        cost_estimate=cost(1, 1),
        name="add_split",
    )(me, keep, got)


def after(x, *deps):
    return lax.optimization_barrier((x, deps))[0]


class Sum:
    def __init__(self, me, send, keep, bits):
        self.me = me
        self.send, self.keep, self.bits, self.done = send, keep, list(bits), []
        self.got = swap(send, "dp", self.bits[0])

    def turn(self, *deps):
        self.done.append(self.bits.pop(0))
        nxt = self.bits[0]
        stride = nxt
        for used in self.done:
            stride = stride // 2 if used < nxt else stride
        got = after(self.got, *deps) if deps else self.got
        self.send, self.keep = add_split(self.me, self.keep, got, nxt, stride)
        self.got = swap(self.send, "dp", nxt)
        return self.keep

    def turns(self, *deps):
        while len(self.bits) > 1:
            deps = (self.turn(*deps),)
        return deps


def norm_rows(sums, gain, shift, total):
    mean = sums[0:1] * (1.0 / total)
    var = sums[1:2] * (1.0 / total) - mean * mean
    rstd = lax.rsqrt(var + 1e-05)
    factor = gain * rstd
    return mean, rstd, factor, shift - mean * factor


def inverse(d):
    r = pl.reciprocal(d, approx=True)
    return r * (2.0 - d * r)


def gate(y, factor, offset):
    z = y * factor + offset
    power = jnp.minimum(y * (factor * -LOG2E) + offset * -LOG2E, 100.0)
    return z, inverse(1.0 + jnp.exp2(power))


def slope_of(z, sig):
    return sig * (1.0 + (z - z * sig))


def back_rows(back, rstd, mean, factor, total):
    d = -(factor * rstd) * (back[0:1] * (1.0 / total))
    return d, -factor * (back[1:2] * (1.0 / total)) - mean * d


def flat(x):
    return x.reshape(-1, x.shape[-1])


def add_sums(sums, one, two):
    sums[0:1] += jnp.sum(one, axis=0, keepdims=True)
    sums[1:2] += jnp.sum(two, axis=0, keepdims=True)


def first_kernel(codes, count, me, x, *refs):
    pieces, (y, sums, weights, p_sem) = refs[:count], refs[count:]
    copies = fetch_pieces(pieces, codes, me, weights, p_sem)
    sums[...] = jnp.zeros_like(sums)
    wait_all(copies)
    for k in range(SIDE):
        out = jnp.dot(x[k], weights[...].reshape(-1, C_MID), preferred_element_type=F32)
        y[k] = out
        add_sums(sums, out, out * out)


def first_forward(me, x, pieces, codes):
    rows = x.shape[1]
    return pl.pallas_call(
        functools.partial(first_kernel, codes, len(pieces)),
        in_specs=[SMEM, IN_VMEM] + [ANY] * len(pieces),
        out_specs=[IN_VMEM, IN_VMEM],
        out_shape=[
            jax.ShapeDtypeStruct((SIDE, rows, C_MID), F32), jax.ShapeDtypeStruct((2, C_MID), F32),
        ],
        scratch_shapes=[
            pltpu.VMEM((C_IN // C_MID, C_MID, C_MID), BF), dma(entries(pieces)),
        ],
        compiler_params=room(8),
        cost_estimate=cost(1, 1),
        name="first_forward",
    )(me, x, *pieces)


def clear_border(pad):
    zero = jnp.zeros(pad.shape[1:], pad.dtype)
    pad[0] = zero
    pad[SIDE + 1] = zero
    for k in range(1, SIDE + 1):
        pad[k, 0] = zero[0]
        pad[k, SIDE + 1] = zero[0]


def second_kernel(codes, count, total, me, y1, sums1, params, *refs):
    pieces, (h1, y2, sums2, taps, pad, p_sem) = refs[:count], refs[count:]
    batch = pad.shape[2]
    copies = fetch_pieces(pieces, codes, me, taps, p_sem)
    clear_border(pad)
    sums2[...] = jnp.zeros_like(sums2)
    _, _, factor, offset = norm_rows(sums1[...], params[0:1], params[1:2], total)

    def act(k):
        z, sig = gate(y1[k], factor, offset)
        h = (z * sig).astype(BF).reshape(SIDE, batch, C_MID)
        pad[k + 1, 1 : SIDE + 1] = h
        h1[k] = h

    act(0)
    act(1)
    wait_all(copies)
    for k in range(SIDE):
        out = None
        for a in range(3):
            if 0 <= k + a - 1 < SIDE:
                patch = jnp.concatenate([flat(pad[k + a, b : b + SIDE]) for b in range(3)], axis=1)
                part = jnp.dot(
                    patch, taps[3 * a : 3 * a + 3].reshape(3 * C_MID, C_MID),
                    preferred_element_type=F32,
                )
                out = part if out is None else out + part
        if k + 2 < SIDE:
            act(k + 2)
        y2[k] = out
        add_sums(sums2, out, out * out)


def second_forward(me, y1, sums1, params, pieces, codes, total):
    rows = y1.shape[1]
    batch = rows // SIDE
    return pl.pallas_call(
        functools.partial(second_kernel, codes, len(pieces), total),
        in_specs=[SMEM, IN_VMEM, IN_VMEM, IN_VMEM] + [ANY] * len(pieces),
        out_specs=[IN_VMEM] * 4,
        out_shape=[
            jax.ShapeDtypeStruct((SIDE, SIDE, batch, C_MID), BF),
            jax.ShapeDtypeStruct(y1.shape, F32),
            jax.ShapeDtypeStruct((2, C_MID), F32),
            jax.ShapeDtypeStruct((9, C_MID, C_MID), BF),
        ],
        scratch_shapes=[
            pltpu.VMEM((SIDE + 2, SIDE + 2, batch, C_MID), BF), dma(entries(pieces)),
        ],
        compiler_params=room(12),
        cost_estimate=cost(1, 1),
        name="second_forward",
    )(me, y1, sums1, params, *pieces)


def head_kernel(codes, count, outs_n, total, group_images, me, y2, sums2, params, bias, labels, *refs):
    pieces, refs = refs[:count], refs[count:]
    outs, (packed, dpool_out, slopes, head, block, p_sem) = refs[:outs_n], refs[outs_n:]
    batch = dpool_out.shape[0]
    copies = fetch_pieces(pieces, codes, me, head, p_sem)
    mean, rstd, factor, offset = norm_rows(sums2[...], params[2:3], params[3:4], total)
    sum_h = sum_a = sum_b = jnp.zeros((batch, C_MID), F32)
    fold = lambda v: jnp.sum(v.reshape(SIDE, batch, C_MID), axis=0)
    for k in range(SIDE):
        z, sig = gate(y2[k], factor, offset)
        slope = slope_of(z, sig)
        slopes[k] = slope
        sum_h = sum_h + fold(z * sig)
        sum_a = sum_a + fold(slope)
        sum_b = sum_b + fold(slope * ((y2[k] - mean) * rstd))
    wait_all(copies)
    pooled = (sum_h * (1.0 / PIX)).astype(BF)
    logits = jnp.concatenate(
        [jnp.dot(pooled, head[k], preferred_element_type=F32) for k in range(2)], axis=1
    )
    logits = logits + bias[...]
    column = lax.broadcasted_iota(I32, (batch, WIDE), 1)
    logits = jnp.where(column < CLASSES, logits, -1e30)
    across = lax.broadcasted_iota(I32, (batch, batch), 0) == lax.broadcasted_iota(I32, (batch, batch), 1)
    label = jnp.sum(jnp.where(across, labels[...], 0), axis=1, keepdims=True)
    onehot = (label == column).astype(F32)
    top = jnp.max(logits, axis=1, keepdims=True)
    expo = jnp.exp(logits - top)
    expsum = jnp.sum(expo, axis=1, keepdims=True)
    lse = top + jnp.log(expsum)
    loss = jnp.sum(lse - jnp.sum(logits * onehot, axis=1, keepdims=True), axis=0, keepdims=True)
    dlogits = ((jnp.exp(logits - lse) - onehot) * (1.0 / group_images)).astype(BF)
    bias_sum = jnp.sum(dlogits.astype(F32), axis=0, keepdims=True)
    last = lax.broadcasted_iota(I32, (1, WIDE), 1) == WIDE - 1
    bias_sum = jnp.where(last, loss, bias_sum)
    dpool = jnp.zeros((batch, C_MID), F32)
    for k in range(2):
        part = dlogits[:, k * C_MID : (k + 1) * C_MID]
        dpool = dpool + lax.dot_general(
            part, head[k], (((1,), (1,)), ((), ())), preferred_element_type=F32
        )

    def make(k):
        block[...] = lax.dot_general(
            pooled, dlogits[:, k * C_MID : (k + 1) * C_MID], (((0,), (0,)), ((), ())),
            preferred_element_type=F32,
        ).reshape(block.shape)

    emit_all(2, make, block, me, 1, outs)
    dpool = dpool * (1.0 / PIX)
    dpool_out[...] = dpool
    packed[0:1] = jnp.sum(dpool * sum_b, axis=0, keepdims=True)
    packed[1:2] = jnp.sum(dpool * sum_a, axis=0, keepdims=True)
    packed[2:3] = bias_sum[:, :C_MID]
    packed[3:4] = bias_sum[:, C_MID:]


def head_step(me, y2, sums2, params, bias, labels, pieces, codes, total, group_images, n, r):
    rows = y2.shape[1]
    batch = rows // SIDE
    shapes = split_shapes(2, n, r, C_MID)
    return pl.pallas_call(
        functools.partial(head_kernel, codes, len(pieces), len(shapes), total, group_images),
        in_specs=[SMEM] + [IN_VMEM] * 5 + [ANY] * len(pieces),
        out_specs=[IN_VMEM] * (3 + len(shapes)),
        out_shape=shapes + [
            jax.ShapeDtypeStruct((4, C_MID), F32), jax.ShapeDtypeStruct((batch, C_MID), F32),
            jax.ShapeDtypeStruct(y2.shape, F32),
        ],
        scratch_shapes=[
            pltpu.VMEM((2, C_MID, C_MID), BF), pltpu.VMEM(part_shape(n, r) + (C_MID,), F32),
            dma(entries(pieces)),
        ],
        compiler_params=room(8),
        cost_estimate=cost(1, 1),
        name="head_step",
    )(me, y2, sums2, params, bias, labels, *pieces)


def emit_all(count, make, block, me, bit, outs):
    scales = []
    for i in range(count):
        make(i)
        if len(outs) == 1:
            outs[0][i] = block[...]
        else:
            scales.append(put_split(block, side_of(me, bit), bit, *outs, i))
    if scales:
        put_scales(outs[0], scales)


def one_tap(tap, pad, turned, block):
    a, b = tap // 3, tap % 3
    moved = pad[2 - a : 2 - a + SIDE, 2 - b : 2 - b + SIDE].reshape(-1, C_MID)
    block[...] = jnp.dot(turned[...], moved, preferred_element_type=F32).reshape(block.shape)


def taps_kernel(total, bits, me, y2, slopes, sums2, back, params, dpool, h1, pad, turned, *refs):
    outs, block = refs[:-1], refs[-1]
    batch = pad.shape[2]
    clear_border(pad)
    mean, rstd, factor, _ = norm_rows(sums2[...], params[2:3], params[3:4], total)
    d, e = back_rows(back, rstd, mean, factor, total)
    scaled = (dpool[...] * factor)[None]
    turned[...] = h1[...].reshape(-1, C_MID).T
    for k in range(SIDE):
        dz = flat(slopes[k].reshape(SIDE, batch, C_MID) * scaled)
        dy = dz + (y2[k] * d + e)
        pad[k + 1, 1 : SIDE + 1] = dy.astype(BF).reshape(SIDE, batch, C_MID)
    each, first = len(outs) // len(bits), 0
    for k, bit in enumerate(bits):
        some = outs[k * each : (k + 1) * each]
        make = lambda i, first=first: one_tap(first + i, pad, turned, block)
        emit_all(some[-1].shape[0], make, block, me, bit, some)
        first += some[-1].shape[0]


def taps_more_kernel(first_tap, me, pad, turned, *refs):
    outs, block = refs[:-1], refs[-1]
    make = lambda i: one_tap(i + first_tap, pad, turned, block)
    emit_all(outs[-1].shape[0], make, block, me, 1, outs)


def taps_grad_first(me, y2, slopes, sums2, back, params, dpool, h1, total, n, r, counts, bits):
    batch = h1.shape[2]
    shapes = [v for count in counts for v in split_shapes(count, n, r, C_MID)]
    return pl.pallas_call(
        functools.partial(taps_kernel, total, bits),
        in_specs=[SMEM] + [IN_VMEM] * 7,
        out_specs=[IN_VMEM] * (2 + len(shapes)),
        out_shape=[
            jax.ShapeDtypeStruct((SIDE + 2, SIDE + 2, batch, C_MID), BF),
            jax.ShapeDtypeStruct((C_MID, SIDE * SIDE * batch), BF),
        ] + shapes,
        scratch_shapes=[pltpu.VMEM(part_shape(n, r) + (C_MID,), F32)],
        compiler_params=room(8),
        cost_estimate=cost(1, 1),
        name="taps_grad_first",
    )(me, y2, slopes, sums2, back, params, dpool, h1)


def taps_grad_more(me, pad, turned, n, r, first_tap, count):
    shapes = split_shapes(count, n, r, C_MID)
    return pl.pallas_call(
        functools.partial(taps_more_kernel, first_tap),
        in_specs=[SMEM, IN_VMEM, IN_VMEM],
        out_specs=[IN_VMEM] * len(shapes),
        out_shape=shapes,
        scratch_shapes=[pltpu.VMEM(part_shape(n, r) + (C_MID,), F32)],
        compiler_params=room(8),
        cost_estimate=cost(1, 1),
        name="taps_grad_more",
    )(me, pad, turned)


def input_grad_kernel(total, pad, y1, sums1, params, taps, dz1, sums):
    sums[...] = jnp.zeros_like(sums)
    mean, rstd, factor, offset = norm_rows(sums1[...], params[0:1], params[1:2], total)
    for k in range(SIDE):
        dh = None
        for a in range(3):
            for b in range(3):
                if 0 <= k + 1 - a < SIDE:
                    part = lax.dot_general(
                        flat(pad[k + 2 - a, 2 - b : 2 - b + SIDE]), taps[3 * a + b],
                        (((1,), (1,)), ((), ())), preferred_element_type=F32,
                    )
                    dh = part if dh is None else dh + part
        dz = dh * slope_of(*gate(y1[k], factor, offset))
        dz1[k] = dz
        add_sums(sums, dz * ((y1[k] - mean) * rstd), dz)


def input_grad(pad, y1, sums1, params, taps, total):
    return pl.pallas_call(
        functools.partial(input_grad_kernel, total),
        in_specs=[IN_VMEM] * 5,
        out_specs=[IN_VMEM] * 2,
        out_shape=[jax.ShapeDtypeStruct(y1.shape, F32), jax.ShapeDtypeStruct((2, C_MID), F32)],
        compiler_params=room(8),
        cost_estimate=cost(1, 1),
        name="input_grad",
    )(pad, y1, sums1, params, taps)


def one_first(x, dy, at, block):
    block[...] = lax.dot_general(
        flat(x[:, :, at * C_MID : (at + 1) * C_MID]), flat(dy[...]), (((0,), (0,)), ((), ())),
        preferred_element_type=F32,
    ).reshape(block.shape)


def first_grad_kernel(total, me, dz1, y1, sums1, back, params, x, dy, *refs):
    outs, block = refs[:-1], refs[-1]
    mean, rstd, factor, _ = norm_rows(sums1[...], params[0:1], params[1:2], total)
    d, e = back_rows(back, rstd, mean, factor, total)
    for k in range(SIDE):
        dy[k] = (dz1[k] * factor + (y1[k] * d + e)).astype(BF)
    emit_all(outs[-1].shape[0], lambda i: one_first(x, dy, i, block), block, me, 1, outs)


def first_more_kernel(bit, first, me, x, dy, *refs):
    outs, block = refs[:-1], refs[-1]
    make = lambda i: one_first(x, dy, first + i, block)
    emit_all(outs[-1].shape[0], make, block, me, bit, outs)


def first_grad_first(me, dz1, y1, sums1, back, params, x, total, n, r, count):
    shapes = split_shapes(count, n, r, C_MID)
    return pl.pallas_call(
        functools.partial(first_grad_kernel, total),
        in_specs=[SMEM] + [IN_VMEM] * 6,
        out_specs=[IN_VMEM] * (1 + len(shapes)),
        out_shape=[jax.ShapeDtypeStruct(y1.shape, BF)] + shapes,
        scratch_shapes=[pltpu.VMEM(part_shape(n, r) + (C_MID,), F32)],
        compiler_params=room(8),
        cost_estimate=cost(1, 1),
        name="first_grad_first",
    )(me, dz1, y1, sums1, back, params, x)


def first_grad_more(me, bit, x, dy, n, r, first_block, count):
    shapes = split_shapes(count, n, r, C_MID)
    return pl.pallas_call(
        functools.partial(first_more_kernel, bit, first_block),
        in_specs=[SMEM, IN_VMEM, IN_VMEM],
        out_specs=[IN_VMEM] * len(shapes),
        out_shape=shapes,
        scratch_shapes=[pltpu.VMEM(part_shape(n, r) + (C_MID,), F32)],
        compiler_params=room(8),
        cost_estimate=cost(1, 1),
        name="first_grad_more",
    )(me, x, dy)


def adamw(weight, grad, first, second, rate):
    first = 0.9 * first + 0.1 * grad
    second = 0.999 * second + 0.001 * grad * grad
    normal_step = first / (1.0 - 0.9**STEP) / (jnp.sqrt(second / (1.0 - 0.999**STEP)) + 1e-08)
    return (-rate * (normal_step + 0.01 * weight), first, second)


def outer_step(start, step_sum, momentum, groups):
    delta = -(step_sum / groups)
    momentum = 0.9 * momentum + delta
    return (start - 0.7 * (delta + 0.9 * momentum), momentum)


def rep_sum(x):
    for bit in bits_of("rep"):
        low = x.astype(BF)
        x = low.astype(F32) + swap(low, "rep", bit).astype(F32)
    return x


def finish_kernel(n_parts, at, before, *refs):
    parts, state, refs = refs[:n_parts], refs[n_parts : n_parts + 5], refs[n_parts + 5 + before :]
    outs, (low, *refs) = refs[:3], refs[3:]
    bufs, sems = refs[:3], refs[3:]
    given = scales_of(parts[1]) if n_parts == 2 else None

    def body(i):
        if n_parts == 2:
            keep, got = parts
            r = keep.shape[2]
            owned = keep[i, 0] + value_of(got[i * r : (i + 1) * r, :], given[i : i + 1])
        else:
            owned = parts[0][i]
        weight, mask, rank = (ref[at + i] for ref in state[:3])
        first, second = (ref[0, at + i] for ref in state[3:])
        bufs[2][i] = mask_of(mask, rank)
        old, new = masks(mask, rank)
        effective = weight * old
        kept = old * new
        dense = owned + 5e-05 * effective
        step, m, v = adamw(weight * kept, new * dense, first * kept, second * kept, 0.03)
        bufs[0][i] = m * new
        bufs[1][i] = v * new
        low[i] = (step * new).astype(BF)

    here = lambda ref: lambda i: ref.at[at + i]
    here_rep = lambda ref: lambda i: ref.at[0, at + i]
    wheres = (here_rep, here_rep, here)
    by_blocks(low.shape[0], [(f(ref), *two) for f, ref, *two in zip(wheres, outs, bufs, sems)], body)


def mask_of(old, rank):
    return jnp.where(rank < DROP_CUT, 0, jnp.where(rank >= GROW_CUT, 1, old))


def masks(old, rank):
    return old.astype(F32), mask_of(old, rank).astype(F32)


def finish(parts, state, before, at, count):
    shard, w = state[0].shape[1:]
    own = lambda t: pltpu.VMEM((count, shard, w), t)
    n_in = len(parts) + 5
    return pl.pallas_call(
        functools.partial(finish_kernel, len(parts), at, len(before)),
        in_specs=[IN_VMEM] * n_in + [ANY] * len(before),
        out_specs=[ANY, ANY, ANY, IN_VMEM],
        out_shape=[
            jax.ShapeDtypeStruct(state[3].shape, F32), jax.ShapeDtypeStruct(state[4].shape, F32),
            jax.ShapeDtypeStruct(state[1].shape, I32),
            jax.ShapeDtypeStruct((count, shard, w), BF),
        ],
        input_output_aliases={n_in + k: k for k in range(len(before))},
        scratch_shapes=[own(F32), own(F32), own(I32)] + [dma(count)] * 3,
        compiler_params=room(12),
        cost_estimate=cost(1, 1),
        name="finish",
    )(*parts, *state, *before)


def outer_kernel(groups, at, before, low, got, *refs):
    state, refs = refs[:4], refs[4 + before :]
    outs, bufs, sems = refs[:2], refs[2:4], refs[4:]

    def body(i):
        weight, mask, rank, momentum = (ref[at + i] for ref in state)
        old, new = masks(mask, rank)
        total = low[i].astype(F32) + got[i].astype(F32)
        value, mom = outer_step(weight * (old * new), total, momentum, groups)
        bufs[0][i] = value * new
        bufs[1][i] = mom * new

    here = lambda ref: lambda i: ref.at[at + i]
    by_blocks(low.shape[0], [(here(ref), *two) for ref, *two in zip(outs, bufs, sems)], body)


def outer(low, got, state, before, at, groups):
    return pl.pallas_call(
        functools.partial(outer_kernel, groups, at, len(before)),
        in_specs=[IN_VMEM] * 6 + [ANY] * len(before),
        out_specs=[ANY, ANY],
        out_shape=[jax.ShapeDtypeStruct(state[0].shape, F32)] * 2,
        input_output_aliases={6 + k: k for k in range(len(before))},
        scratch_shapes=[pltpu.VMEM(low.shape, F32)] * 2 + [dma(low.shape[0])] * 2,
        compiler_params=room(12),
        cost_estimate=cost(1, 1),
        name="outer",
    )(low, got, *state, *before)


def per_device(
    images, labels, conv_weight, conv_mask, conv_rank, head_weight, norm_params, head_bias,
    conv_first, conv_second, head_first, head_second, norm_first, norm_second, bias_first,
    bias_second, conv_outer, head_outer, norm_outer, bias_outer,
):
    devices = lax.axis_size("dp")
    groups = lax.axis_size("rep")
    width = C_MID
    blocks = C_IN // C_MID
    core = lax.axis_index("rep") % 2
    dp = lax.axis_index("dp")
    me = jnp.stack([dp, core]).astype(I32)
    bits = bits_of("dp")
    shard = conv_weight.shape[1]
    batch = images.shape[0]
    rows = batch * PIX
    total = float(rows * devices)
    group_images = batch * devices
    half = shard // 2

    def mine(x):
        return pick(x.reshape(-1, 2, half, width), 1, core)

    def active(sl):
        return jnp.where(mine(conv_mask[sl]) == 1, mine(conv_weight[sl]), 0.0).astype(BF)

    head_wide = jnp.pad(head_weight.astype(BF), ((0, 0), (0, WIDE - CLASSES)))
    head_low = mine(head_wide.reshape(shard, 2, width).transpose(1, 0, 2))
    taps_low = active(slice(blocks, None))
    get_first = Gather(active(slice(0, blocks))).start()
    get_first.join()
    get_taps = Gather(after(taps_low, get_first.own)).start()
    get_first.own = after(get_first.own, taps_low)
    get_first.turn_near()
    get_first.turn_side()
    get_first.turn_far()
    first_pieces, first_codes = get_first.finish()
    fine = first_codes is not None
    classes = labels.reshape(1, batch)
    x = images.transpose(1, 2, 0, 3).reshape(SIDE, SIDE * batch, C_IN)
    y_one, sums_one = first_forward(me, x, first_pieces, first_codes)
    head_got = gather_more(after(head_low, y_one)[None], [0], bits[0])
    sums_one = sums_one + swap(sums_one, "dp", bits[0])
    get_taps.join(sums_one, head_got[0])
    get_taps.turn_near()
    get_taps.turn_side()
    get_taps.turn_far(get_taps.side)
    for bit in bits[1:]:
        sums_one = sums_one + swap(sums_one, "dp", bit)
    taps_pieces, taps_codes = get_taps.finish(sums_one)
    buf, rel = after(head_got[0], get_taps.near), head_got[1]
    head_more = swap(buf, "dp", bits[-1])
    h_one, y_two, sums_two, taps = second_forward(
        me, y_one, sums_one, norm_params, taps_pieces, taps_codes, total
    )
    buf = jnp.concatenate([buf, after(head_more, sums_two)], axis=0)
    rel = rel + [code ^ bits[-1] for code in rel]
    for bit in reversed(bits[2:-1]):
        buf, rel = gather_more(buf, rel, bit)
    head_more = swap(buf, "dp", bits[1])
    for bit in bits[:-1]:
        sums_two = sums_two + swap(sums_two, "dp", bit)
    buf = jnp.concatenate([buf, after(head_more, sums_two)], axis=0)
    rel = rel + [code ^ bits[1] for code in rel]
    head_pieces, head_codes = [buf, swap(buf, "rep", 1)], [[(c, r) for r in rel] for c in range(2)]
    if not fine:
        head_pieces, head_codes = place(head_pieces, head_codes), None
    sums_two = sums_two + swap(sums_two, "dp", bits[-1])
    bias_wide = jnp.pad(head_bias, (0, WIDE - CLASSES)).reshape(1, WIDE)
    *outs, packed, dpool, slopes = head_step(
        me, y_two, sums_two, norm_params, bias_wide, classes, head_pieces, head_codes, total,
        group_images, devices, shard,
    )
    n, r = devices, shard
    sum_head = Sum(me, *split_of(me, outs, n, r, 1, 1), bits)
    packed = sum_all(packed, "dp")
    cut = 5
    dpool = after(dpool, sum_head.turn(packed))
    pad, turned, *outs = taps_grad_first(
        me, y_two, slopes, sums_two, packed, norm_params, dpool, h_one, total, n, r, (cut,), bits[:1]
    )
    sum_a = Sum(me, *split_of(me, outs, n, r, 1, 1), bits)
    pad = after(pad, outs[0])
    dz_one, back_one = input_grad(pad, y_one, sums_one, norm_params, taps, total)
    turned = after(turned, dz_one)
    outs = taps_grad_more(me, pad, turned, n, r, cut, 9 - cut)
    back_one = sum_all(back_one, "dp", sum_head.turn(outs[0]))
    send, keep = split_of(me, outs, n, r, 1, 1)
    sum_b = Sum(me, after(send, back_one), keep, bits)
    last = sum_a.turn(back_one)
    dy_one, *outs = first_grad_first(
        me, dz_one, y_one, sums_one, after(back_one, last), norm_params, x, total, n, r, 2
    )
    sum_c = Sum(me, *split_of(me, outs, n, r, 1, 1), bits)
    outs = first_grad_more(me, 1, x, after(dy_one, outs[0]), n, r, 2, 2)
    sum_d = Sum(me, *split_of(me, outs, n, r, 1, 1), bits)
    state = (conv_weight, conv_mask, conv_rank, conv_first, conv_second)
    rep_bits = bits_of("rep")
    results, new = (), ()

    def close(one, at, *deps):
        one.turns()
        keep = after(one.keep, *deps)
        parts = (keep, one.got) if fine else (keep[:, 0] + decode(one.got, keep.shape[0]),)
        *both, low = finish(parts, state, results, at, keep.shape[0])
        return both, low

    def to_groups(low):
        for b in rep_bits[:-1]:
            low = (low.astype(F32) + swap(low, "rep", b).astype(F32)).astype(BF)
        return low, swap(low, "rep", rep_bits[-1])

    last = sum_a.turn(*sum_head.turns(outs[0]))
    last = sum_b.turn(last)
    last = sum_c.turn(last)
    results, low_a = close(sum_a, blocks, last)
    last = sum_b.turn(low_a)
    last = sum_d.turn(last)
    last = sum_c.turn(last)
    low_a, got_a = to_groups(low_a)
    last = sum_d.turn(last, got_a)
    results, low_b = close(sum_b, blocks + cut, last)
    results, low_c = close(sum_c, 0, low_b)
    results, low_d = close(sum_d, 2, low_c)
    low_b, got_b = to_groups(low_b)
    low_c, got_c = to_groups(jnp.concatenate([low_c, low_d], axis=0))
    back_one, packed = after((back_one, packed), low_a)
    bias_grad = packed[2:].reshape(-1)[:CLASSES]
    loss_sum = packed[3, C_MID - 1 :]
    head_grad = after(sum_head.keep, low_a)[:, 0] + decode(sum_head.got, 2)
    head_grad = head_grad.transpose(1, 0, 2).reshape(shard, WIDE)[:, :CLASSES]
    for low, got, at in ((low_a, got_a, blocks), (low_b, got_b, blocks + cut), (low_c, got_c, 0)):
        new = outer(low, got, state[:3] + (conv_outer,), new, at, groups)
    (conv_m, conv_v, mask_int), (conv_new, conv_mom) = results, new
    norm_grad = jnp.concatenate([back_one, packed[:2]], axis=0)
    head_s, head_m, head_v = adamw(head_weight, head_grad, head_first[0], head_second[0], 0.03)
    head_new, head_mom = outer_step(head_weight, rep_sum(head_s), head_outer, groups)
    norm_s, norm_m, norm_v = adamw(norm_params, norm_grad, norm_first[0], norm_second[0], 0.3)
    bias_s, bias_m, bias_v = adamw(head_bias, bias_grad, bias_first[0], bias_second[0], 0.3)
    wide = jnp.pad(bias_s, (0, WIDE - CLASSES)).reshape(2, width)
    small = jnp.pad(norm_s, ((0, 2), (0, 0))) + jnp.pad(wide, ((4, 0), (0, 0)))
    small = sum_all(small, "rep")
    norm_new, norm_mom = outer_step(norm_params, small[:4], norm_outer, groups)
    bias_new, bias_mom = outer_step(head_bias, small[4:].reshape(-1)[:CLASSES], bias_outer, groups)
    return (
        conv_new, mask_int, conv_m, conv_v, conv_mom,
        head_new, head_m[None], head_v[None], head_mom,
        norm_new, norm_m[None], norm_v[None], norm_mom,
        bias_new, bias_m[None], bias_v[None], bias_mom, loss_sum,
    )
def solution(mesh):
    conv = P(None, "dp", None)
    conv_rep = P("rep", None, "dp", None)
    head = P("dp", None)
    head_rep = P("rep", "dp", None)
    in_specs = (
        P(("rep", "dp"), None, None, None), P(("rep", "dp")), conv, conv, conv, head, P(), P(),
        conv_rep, conv_rep, head_rep, head_rep, P("rep", None, None), P("rep", None, None),
        P("rep", None), P("rep", None), conv, head, P(), P(),
    )
    out_specs = (
        conv, conv, conv_rep, conv_rep, conv, head, head_rep, head_rep, head,
        P(), P("rep", None, None), P("rep", None, None), P(),
        P(), P("rep", None), P("rep", None), P(), P("rep"),
    )
    return jax.shard_map(
        per_device, mesh=mesh, in_specs=in_specs, out_specs=out_specs, check_vma=False
    )
```
